256 devices in a mesh: ctx: 16 (over x, y), head: 16 (over z, core).
Axes of the slice: x: 4, y: 4, z: 8, core: 2. Of those that a mesh axis runs over, the one named last changes fastest.
Arguments:
- lin_q: bfloat16 [4096, 64, 128], P('ctx', 'head'), may hold values from -6 to 6
- lin_k: bfloat16 [4096, 64, 128], P('ctx', 'head'), may hold values from -6 to 6
- lin_v: bfloat16 [4096, 64, 128], P('ctx', 'head'), may hold values from -6 to 6
- log_decay: float32 [64, 4096], P('head', 'ctx'), may hold values from -2.2 to 0
- lin_gain: float32 [64, 128], P('head'), may hold values from 0.1 to 1.9
- lin_grad: bfloat16 [4096, 64, 128], P('ctx', 'head'), may hold values from -6 to 6
- soft_q: bfloat16 [4096, 64, 128], P('ctx', 'head'), may hold values from -170 to 170
- soft_k: bfloat16 [4096, 8, 128], P('ctx'), may hold values from -6 to 6
- soft_v: bfloat16 [4096, 8, 128], P('ctx'), may hold values from -6 to 6
- soft_grad: bfloat16 [4096, 64, 128], P('ctx', 'head'), may hold values from -6 to 6
- span_reach: int32 [32], replicated, may hold values from 0 to 32, as said below
Outputs:
- lin_out: bfloat16 [4096, 64, 128], P('ctx', 'head')
- lin_dq: bfloat16 [4096, 64, 128], P('ctx', 'head')
- lin_dk: bfloat16 [4096, 64, 128], P('ctx', 'head')
- lin_dv: bfloat16 [4096, 64, 128], P('ctx', 'head')
- soft_out: bfloat16 [4096, 64, 128], P('ctx', 'head')
- soft_dq: bfloat16 [4096, 64, 128], P('ctx', 'head')
- soft_dk: bfloat16 [4096, 8, 128], P('ctx')
- soft_dv: bfloat16 [4096, 8, 128], P('ctx')
The draws below stay inside these ranges and needn't reach their ends.
Inputs may be any that keep to these rules, and one draw needn't show every extreme that they name: span_reach[i] is 0 for a text block; for an image block it is one more than the index of the last block of the image span that holds block i. Block 0 is text; the last block belongs to an image span.
All inputs are finite; a program needn't handle non-finite values.
Results may differ from the reference program's by a relative error of at most 0.017.
Values may be sent and summed in bfloat16 or wider, within the bound.
No kernel may reach another device: no remote copies, remote signals or barrier semaphores. Data moves between devices by JAX's collectives and lax.ppermute only.
A program may use at most 64 MiB of HBM per device.

```python
import math
import jax
import jax.numpy as jnp
from jax import lax

HEAD_TOTAL = 64
HD = 128
KVH = 8
LB = 256
BLK = 128
TOKEN_POSITIONS = 4096


def base_keys(key):
    return jax.random.truncated_normal(jax.random.fold_in(key, 11), -6.0, 6.0, (TOKEN_POSITIONS, KVH, HD), jnp.float32)


def draw_soft_k(key, part):
    shared_rows = base_keys(key)
    return shared_rows.astype(jnp.bfloat16)


def draw_soft_q(key, part):
    key = jax.random.fold_in(key, 17)
    own_rows = jax.random.truncated_normal(key, -6.0, 6.0, (TOKEN_POSITIONS, HEAD_TOTAL, HD), jnp.float32)
    return own_rows.astype(jnp.bfloat16)


def draw_log_decay(key, part):
    key = jax.random.fold_in(key, 5)
    random_subkeys = jax.random.split(key, 5)
    fast_share = 0.5
    fast_heads = jax.random.uniform(random_subkeys[0], (HEAD_TOTAL, 1)) < fast_share
    fast_rate = jnp.exp(jax.random.uniform(random_subkeys[1], (HEAD_TOTAL, 1), minval=math.log(1.0 / 50.0), maxval=math.log(1.0 / 30.0)))
    slow_rate = math.log(10.0) / (4.0 * TOKEN_POSITIONS)
    baseline_rate = jnp.where(fast_heads, fast_rate, slow_rate)
    jitter_amount = jnp.exp(jax.random.uniform(random_subkeys[2], (HEAD_TOTAL, TOKEN_POSITIONS), minval=math.log(0.5), maxval=math.log(2.0)))
    spike_location = jax.random.randint(random_subkeys[3], (HEAD_TOTAL, 3), 0, TOKEN_POSITIONS)
    spike_length = jax.random.uniform(random_subkeys[4], (HEAD_TOTAL, 3), minval=0.22, maxval=0.69)
    token_places = jnp.arange(TOKEN_POSITIONS, dtype=jnp.int32)
    spike_penalty = jnp.sum(jnp.where(token_places[None, None, :] == spike_location[:, :, None], spike_length[:, :, None], 0.0), axis=1)
    return -(baseline_rate * jitter_amount + spike_penalty)


def draw_span_reach(key, part):
    key = jax.random.fold_in(key, 7)
    start_key, kind_key = jax.random.split(key)
    block_count = TOKEN_POSITIONS // BLK
    ordering = jnp.arange(block_count, dtype=jnp.int32)
    span_start = (jax.random.randint(start_key, (block_count,), 0, 4) == 0) | (ordering == 0) | (ordering == block_count - 1)
    segments = jnp.cumsum(span_start.astype(jnp.int32)) - 1
    image_flag = jax.random.randint(kind_key, (block_count,), 0, 2)
    last_segment = segments[block_count - 1]
    is_image = ((jnp.take(image_flag, segments) == 1) | (segments == last_segment)) & (segments > 0)
    start_marks = jnp.where(span_start, ordering, block_count)
    shifted = jnp.concatenate([start_marks[1:], jnp.full((1,), block_count, jnp.int32)])
    span_end = lax.cummin(shifted, reverse=True)
    return jnp.where(is_image, span_end, 0).astype(jnp.int32)


def level_of(own_key, shape, cuts, low, largest):
    level, own = 1.0, jax.random.fold_in(own_key, 6)
    for dim, blocks in cuts:
        steps = jnp.exp(jax.random.uniform(jax.random.fold_in(own, dim), (blocks,), jnp.float32, low / len(cuts), largest / len(cuts)))
        level = level * jnp.repeat(steps, shape[dim] // blocks).reshape([-1 if axis == dim else 1 for axis in range(len(shape))])
    return level


def gaussian(own_key, dims, deviation, reach, pieces=(), kind=jnp.bfloat16):
    values = jax.random.normal(own_key, dims, jnp.float32) * deviation
    if len(pieces) > 0:
        values = level_of(own_key, dims, pieces, -0.22, 0.18) * values
    return jnp.clip(values, min=-reach, max=reach).astype(kind)


def setup_inputs(seed: int = 0) -> dict:
    streams_of = jax.random.split(jax.random.key(seed), 12)
    lin_q = gaussian(streams_of[0], (TOKEN_POSITIONS, HEAD_TOTAL, HD), 1.0, 6.0, ((0, 16), (1, 16)))
    lin_k = gaussian(streams_of[1], (TOKEN_POSITIONS, HEAD_TOTAL, HD), 1.0, 6.0, ((0, 16), (1, 16)))
    lin_v = gaussian(streams_of[2], (TOKEN_POSITIONS, HEAD_TOTAL, HD), 1.0, 6.0, ((0, 16), (1, 16)))
    log_decay = draw_log_decay(jax.random.fold_in(streams_of[11], 71), 0)
    lin_gain = jnp.clip(1.0 + 0.18 * jax.random.normal(streams_of[4], (HEAD_TOTAL, HD), jnp.float32), 0.1, 1.9)
    lin_grad = gaussian(streams_of[5], (TOKEN_POSITIONS, HEAD_TOTAL, HD), 1.0, 6.0, ((0, 16), (1, 16)))
    soft_q = draw_soft_q(jax.random.fold_in(streams_of[11], 71), 0)
    soft_k = draw_soft_k(jax.random.fold_in(streams_of[11], 71), 0)
    soft_v = gaussian(streams_of[8], (TOKEN_POSITIONS, KVH, HD), 1.0, 6.0, ((0, 16),))
    soft_grad = gaussian(streams_of[9], (TOKEN_POSITIONS, HEAD_TOTAL, HD), 1.0, 6.0, ((0, 16), (1, 16)))
    span_reach = draw_span_reach(jax.random.fold_in(streams_of[11], 71), 0)
    return {"lin_q": lin_q, "lin_k": lin_k, "lin_v": lin_v, "log_decay": log_decay, "lin_gain": lin_gain, "lin_grad": lin_grad, "soft_q": soft_q, "soft_k": soft_k, "soft_v": soft_v, "soft_grad": soft_grad, "span_reach": span_reach}


PRECISE = lax.Precision.HIGHEST
EPSILON = 1e-05
FAR_BELOW = -1e+30

def rounded(array):
    narrow = lax.optimization_barrier(array.astype(jnp.bfloat16))
    return narrow.astype(jnp.float32)

def decay_table(running):
    span_len = running.shape[-1]
    ordering = jnp.arange(span_len, dtype=jnp.int32)
    causal_pairs = ordering[:, None] >= ordering[None, :]
    return jnp.exp(jnp.where(causal_pairs, running[..., :, None] - running[..., None, :], FAR_BELOW))

def light_reference(lin_q, lin_k, lin_v, log_decay, lin_gain, lin_grad):
    block_count = TOKEN_POSITIONS // LB
    scaling = 1.0 / HD

    def blocked(array):
        return array.reshape(block_count, LB, HEAD_TOTAL, HD)
    queries, keyset, valueset = (blocked(lin_q), blocked(lin_k), blocked(lin_v))
    running_all = jnp.cumsum(log_decay.reshape(HEAD_TOTAL, block_count, LB).transpose(1, 0, 2), axis=2)
    block_totals = running_all[:, :, -1]
    zero_state = jnp.zeros((HEAD_TOTAL, HD, HD), jnp.float32)

    def forward_step(carried_state, inputs):
        query_part, key_part, value_part, running, block_total = inputs
        decays = decay_table(running)
        head_fade = jnp.exp(running).T[:, :, None]
        tail_fade = jnp.exp(block_total[:, None] - running).T[:, :, None]
        scores = jnp.einsum('thd,shd->hts', query_part.astype(jnp.float32), key_part.astype(jnp.float32), precision=PRECISE)
        weights = rounded(scores * decays * scaling)
        within = jnp.einsum('hts,shd->thd', weights, value_part.astype(jnp.float32), precision=PRECISE)
        from_state = jnp.einsum('thd,hde->the', query_part.astype(jnp.float32), carried_state, precision=PRECISE)
        own_term = jnp.einsum('shd,she->hde', key_part.astype(jnp.float32) * tail_fade, value_part.astype(jnp.float32), precision=PRECISE)
        next_state = jnp.exp(block_total)[:, None, None] * carried_state + own_term
        return (next_state, (within + scaling * head_fade * from_state, carried_state))
    _, (attended, entering) = lax.scan(forward_step, zero_state, (queries, keyset, valueset, running_all, block_totals))
    flattened = attended.reshape(TOKEN_POSITIONS, HEAD_TOTAL, HD)
    upstream = lin_grad.astype(jnp.float32) * lin_gain
    squares = lax.optimization_barrier(jnp.sum(flattened * flattened, axis=(1, 2)))
    cross_sum = lax.optimization_barrier(jnp.sum(upstream * flattened, axis=(1, 2)))
    inverse = lax.rsqrt(squares / (HEAD_TOTAL * HD) + EPSILON)[:, None, None]
    lin_out = (flattened * inverse * lin_gain).astype(jnp.bfloat16)
    att_grad = (inverse * upstream - flattened * inverse ** 3 * (cross_sum / (HEAD_TOTAL * HD))[:, None, None]).astype(jnp.bfloat16)

    def backward_step(later_state, inputs):
        query_part, key_part, value_part, grad_part, running, block_total, carried_state = inputs
        decays = decay_table(running)
        head_fade = jnp.exp(running).T[:, :, None]
        tail_fade = jnp.exp(block_total[:, None] - running).T[:, :, None]
        query_wide = query_part.astype(jnp.float32)
        key_wide = key_part.astype(jnp.float32)
        value_wide = value_part.astype(jnp.float32)
        grad_wide = grad_part.astype(jnp.float32)
        scores = jnp.einsum('thd,shd->hts', query_wide, key_wide, precision=PRECISE)
        weights = rounded(scores * decays * scaling)
        grad_probs = jnp.einsum('the,she->hts', grad_wide, value_wide, precision=PRECISE)
        grad_weights = rounded(grad_probs * decays * scaling)
        query_grad = jnp.einsum('hts,shd->thd', grad_weights, key_wide, precision=PRECISE) + scaling * head_fade * jnp.einsum('the,hde->thd', grad_wide, carried_state, precision=PRECISE)
        key_grad = jnp.einsum('hts,thd->shd', grad_weights, query_wide, precision=PRECISE) + scaling * tail_fade * jnp.einsum('she,hde->shd', value_wide, later_state, precision=PRECISE)
        value_grad = jnp.einsum('hts,the->she', weights, grad_wide, precision=PRECISE) + scaling * tail_fade * jnp.einsum('shd,hde->she', key_wide, later_state, precision=PRECISE)
        back_term = jnp.einsum('thd,the->hde', query_wide * head_fade, grad_wide, precision=PRECISE)
        earlier_state = back_term + jnp.exp(block_total)[:, None, None] * later_state
        return (earlier_state, (query_grad.astype(jnp.bfloat16), key_grad.astype(jnp.bfloat16), value_grad.astype(jnp.bfloat16)))
    _, (query_grads, key_grads, value_grads) = lax.scan(backward_step, zero_state, (queries, keyset, valueset, blocked(att_grad), running_all, block_totals, entering), reverse=True)
    shape_full = (TOKEN_POSITIONS, HEAD_TOTAL, HD)
    return (lin_out, query_grads.reshape(shape_full), key_grads.reshape(shape_full), value_grads.reshape(shape_full))

def soft_reference(soft_q, soft_k, soft_v, soft_grad, span_reach):
    scaling = 1.0 / math.sqrt(HD)
    group_size = HEAD_TOTAL // KVH
    token_places = jnp.arange(TOKEN_POSITIONS, dtype=jnp.int32)
    query_reach = span_reach[token_places // BLK]
    visible = (token_places[None, :] <= token_places[:, None]) | (token_places[None, :] // BLK < query_reach[:, None])

    def one_query(key_rows, value_rows, query_rows, grad_rows):
        scores = jnp.dot(query_rows, key_rows.T, preferred_element_type=jnp.float32) * scaling
        row_max = lax.optimization_barrier(jnp.max(jnp.where(visible, scores, FAR_BELOW), axis=1))
        unscaled = jnp.where(visible, jnp.exp(scores - row_max[:, None]), 0.0)
        row_mass = lax.optimization_barrier(jnp.sum(unscaled, axis=1))
        weighted = jnp.dot(unscaled.astype(jnp.bfloat16), value_rows, preferred_element_type=jnp.float32)
        output = (weighted / row_mass[:, None]).astype(jnp.bfloat16)
        log_mass = row_max + jnp.log(row_mass)
        output_wide = lax.optimization_barrier(output).astype(jnp.float32)
        row_dot = lax.optimization_barrier(jnp.sum(grad_rows.astype(jnp.float32) * output_wide, axis=1))
        exact_probs = jnp.where(visible, jnp.exp(scores - log_mass[:, None]), 0.0)
        grad_probs = jnp.dot(grad_rows, value_rows.T, preferred_element_type=jnp.float32)
        score_grads = (exact_probs * (grad_probs - row_dot[:, None]) * scaling).astype(jnp.bfloat16)
        query_grad = jnp.dot(score_grads, key_rows, preferred_element_type=jnp.float32).astype(jnp.bfloat16)
        key_term = jnp.dot(score_grads.T, query_rows, preferred_element_type=jnp.float32)
        value_term = jnp.dot(exact_probs.astype(jnp.bfloat16).T, grad_rows, preferred_element_type=jnp.float32)
        return (output, query_grad, key_term, value_term)

    def one_group(inputs):
        key_rows, value_rows, query_group, grad_group = inputs

        def step(sums, pair):
            output, query_grad, key_term, value_term = one_query(key_rows, value_rows, pair[0], pair[1])
            return ((sums[0] + key_term, sums[1] + value_term), (output, query_grad))
        zero_rows = jnp.zeros((TOKEN_POSITIONS, HD), jnp.float32)
        (key_sum, value_sum), (outputs, query_grads) = lax.scan(step, (zero_rows, zero_rows), (query_group, grad_group))
        return (outputs, query_grads, key_sum.astype(jnp.bfloat16), value_sum.astype(jnp.bfloat16))
    query_groups = jnp.swapaxes(soft_q, 0, 1).reshape(KVH, group_size, TOKEN_POSITIONS, HD)
    grad_groups = jnp.swapaxes(soft_grad, 0, 1).reshape(KVH, group_size, TOKEN_POSITIONS, HD)
    outputs, query_grads, key_grads, value_grads = lax.map(one_group, (jnp.swapaxes(soft_k, 0, 1), jnp.swapaxes(soft_v, 0, 1), query_groups, grad_groups))
    soft_out = jnp.swapaxes(outputs.reshape(HEAD_TOTAL, TOKEN_POSITIONS, HD), 0, 1)
    soft_dq = jnp.swapaxes(query_grads.reshape(HEAD_TOTAL, TOKEN_POSITIONS, HD), 0, 1)
    return (soft_out, soft_dq, jnp.swapaxes(key_grads, 0, 1), jnp.swapaxes(value_grads, 0, 1))

def reference(lin_q, lin_k, lin_v, log_decay, lin_gain, lin_grad, soft_q, soft_k, soft_v, soft_grad, span_reach):
    lin_out, lin_dq, lin_dk, lin_dv = light_reference(lin_q, lin_k, lin_v, log_decay, lin_gain, lin_grad)
    soft_out, soft_dq, soft_dk, soft_dv = soft_reference(soft_q, soft_k, soft_v, soft_grad, span_reach)
    return (lin_out, lin_dq, lin_dk, lin_dv, soft_out, soft_dq, soft_dk, soft_dv)
```

```python
import functools
import math

import jax
import jax.numpy as jnp
from jax import lax
from jax.experimental import pallas as pl
from jax.experimental.pallas import tpu as pltpu
from jax.sharding import PartitionSpec as P

HEAD_TOTAL = 64
HD = 128
KVH = 8
LB = 256
BLK = 128
CTX = 16
HEADS = 16
OWN = 4
ROWS = LB * OWN
HALF = LB // 2
SLICE = OWN * HD // CTX
EPSILON = 1e-05
FAR_BELOW = -1e30
SCALE_LIN = 1.0 / HD
SCALE_SOFT = 1.0 / math.sqrt(HD)
LOG2E = 1.4426950408889634
KEYS = 256
GROUPS = 2 * CTX * HALF // KEYS
PIECES = KEYS // HALF

f32 = jnp.float32
bf16 = jnp.bfloat16
PRECISE = lax.Precision.HIGHEST


def dot(a, b, dims, precision=None):
    return lax.dot_general(a, b, (dims, ((), ())), precision=precision, preferred_element_type=f32)


NN = ((1,), (0,))
NT = ((1,), (1,))
TN = ((0,), (0,))


def split_heads(source, scratch):
    scratch[...] = source[...].astype(f32)
    return [scratch[pl.ds(h, LB, stride=OWN), :] for h in range(OWN)]


def join_heads(parts, scratch, target):
    for h in range(OWN):
        scratch[pl.ds(h, LB, stride=OWN), :] = parts[h]
    target[...] = scratch[...].astype(bf16)


def run_sums(log_decay):
    row = lax.broadcasted_iota(jnp.int32, (LB, LB), 0)
    col = lax.broadcasted_iota(jnp.int32, (LB, LB), 1)
    upto = (row <= col).astype(f32)
    as_rows = dot(log_decay, upto, NN, PRECISE)
    as_cols = dot((row >= col).astype(f32), log_decay, NT, PRECISE)
    return as_rows, as_cols, row, col


def local_kernel(q_ref, k_ref, v_ref, decay_ref, kv_ref, pay_ref, within_ref, heads_ref, scratch):
    queries = [x.astype(bf16) for x in split_heads(q_ref, scratch)]
    keys_wide = split_heads(k_ref, scratch)
    values = [x.astype(bf16) for x in split_heads(v_ref, scratch)]
    as_rows, as_cols, row, col = run_sums(decay_ref[...])
    for j in range(CTX):
        pay_ref[j, 0:LB, :] = kv_ref[...]
    for h in range(OWN):
        run_row, run_col = as_rows[h : h + 1, :], as_cols[:, h : h + 1]
        total = run_row[:, LB - 1 : LB]
        keys = keys_wide[h].astype(bf16)
        heads_ref[0, h] = queries[h]
        heads_ref[1, h] = keys
        heads_ref[2, h] = values[h]
        tailed = (keys_wide[h] * jnp.exp(total - run_col)).astype(bf16)
        own = dot(tailed, values[h], TN).astype(bf16)
        high = total.astype(bf16)
        low = (total - high.astype(f32)).astype(bf16)
        marks = jnp.concatenate(
            [
                jnp.broadcast_to(high.astype(f32), (8, HD)),
                jnp.broadcast_to(low.astype(f32), (8, HD)),
            ],
            axis=0,
        ).astype(bf16)
        for i in range(OWN):
            pay_ref[h * OWN + i, LB : LB + SLICE, :] = own[i * SLICE : (i + 1) * SLICE]
            pay_ref[h * OWN + i, LB + SLICE :, :] = marks
        decays = jnp.exp(jnp.where(row >= col, run_col - run_row, FAR_BELOW))
        weights = (dot(queries[h], keys, NT) * decays * SCALE_LIN).astype(bf16)
        within_ref[h] = dot(weights, values[h], NN)


def prefix_kernel(got_ref, out_ref):
    state = jnp.zeros((SLICE, HD), f32)
    for j in range(CTX):
        out_ref[j] = state.astype(bf16)
        marks = got_ref[j, LB + SLICE :, :].astype(f32)
        fade = jnp.exp(marks[0:1, :] + marks[8:9, :])
        state = fade * state + got_ref[j, LB : LB + SLICE, :].astype(f32)


def attend_kernel(within_ref, heads_ref, state_ref, decay_ref, grad_ref, gain_ref, att_ref, up_ref, sums_ref, scratch):
    _, as_cols, _, _ = run_sums(decay_ref[...])
    grads = split_heads(grad_ref, scratch)
    squares = jnp.zeros((LB, HD), f32)
    crossed = jnp.zeros((LB, HD), f32)
    for h in range(OWN):
        state = state_ref[h * HD : (h + 1) * HD, :]
        fade = SCALE_LIN * jnp.exp(as_cols[:, h : h + 1])
        attended = within_ref[h] + fade * dot(heads_ref[0, h], state, NN)
        upstream = grads[h] * gain_ref[h : h + 1, :]
        att_ref[h] = attended
        up_ref[h] = upstream
        squares = squares + attended * attended
        crossed = crossed + upstream * attended
    ones = jnp.ones((8, HD), f32)
    square_row = dot(ones, squares, NT, PRECISE)
    cross_row = dot(ones, crossed, NT, PRECISE)
    first = lax.broadcasted_iota(jnp.int32, (8, LB), 0) < 4
    both = jnp.where(first, square_row, cross_row)
    for j in range(HEADS):
        sums_ref[j] = both


def grad_kernel(att_ref, up_ref, got_ref, heads_ref, decay_ref, gain_ref, out_ref, ag_ref, back_ref, scratch):
    _, as_cols, row, col = run_sums(decay_ref[...])
    total = got_ref[0]
    for j in range(1, HEADS):
        total = total + got_ref[j]
    cols = dot((row == col).astype(f32), total, NT, PRECISE)
    inverse = lax.rsqrt(cols[:, 0:1] / (HEAD_TOTAL * HD) + EPSILON)
    pull = inverse * inverse * inverse * (cols[:, 4:5] / (HEAD_TOTAL * HD))
    outs = []
    for h in range(OWN):
        attended = att_ref[h]
        outs.append(attended * inverse * gain_ref[h : h + 1, :])
        att_grad = (inverse * up_ref[h] - attended * pull).astype(bf16)
        ag_ref[h] = att_grad
        faded = (heads_ref[0, h].astype(f32) * jnp.exp(as_cols[:, h : h + 1])).astype(bf16)
        back = dot(faded, att_grad, TN).astype(bf16)
        back_ref[h * HD : (h + 1) * HD, :] = back
    join_heads(outs, scratch, out_ref)


def inner_kernel(heads_ref, ag_ref, state_ref, decay_ref, dq_ref, dk_ref, dv_ref, scratch):
    as_rows, as_cols, row, col = run_sums(decay_ref[...])
    query_grads = []
    for h in range(OWN):
        run_row, run_col = as_rows[h : h + 1, :], as_cols[:, h : h + 1]
        query, key, value, grad = heads_ref[0, h], heads_ref[1, h], heads_ref[2, h], ag_ref[h]
        decays = SCALE_LIN * jnp.exp(jnp.where(row >= col, run_col - run_row, FAR_BELOW))
        turned = SCALE_LIN * jnp.exp(jnp.where(col >= row, run_row - run_col, FAR_BELOW))
        grad_weights = (dot(grad, value, NT) * decays).astype(bf16)
        grad_turned = (dot(value, grad, NT) * turned).astype(bf16)
        weights_turned = (dot(key, query, NT) * turned).astype(bf16)
        state = state_ref[h * HD : (h + 1) * HD, :]
        fade = SCALE_LIN * jnp.exp(run_col)
        query_grads.append(dot(grad_weights, key, NN) + fade * dot(grad, state, NT))
        dk_ref[h] = dot(grad_turned, query, NN)
        dv_ref[h] = dot(weights_turned, grad, NN)
    join_heads(query_grads, scratch, dq_ref)


def finish_kernel(dk_ref, dv_ref, heads_ref, later_ref, decay_ref, dk_out, dv_out, scratch):
    as_rows, as_cols, _, _ = run_sums(decay_ref[...])
    key_grads, value_grads = [], []
    for h in range(OWN):
        later = later_ref[h * HD : (h + 1) * HD, :]
        tail = SCALE_LIN * jnp.exp(as_rows[h : h + 1, LB - 1 : LB] - as_cols[:, h : h + 1])
        key_grads.append(dk_ref[h] + tail * dot(heads_ref[2, h], later, NT))
        value_grads.append(dv_ref[h] + tail * dot(heads_ref[1, h], later, NN))
    join_heads(key_grads, scratch, dk_out)
    join_heads(value_grads, scratch, dv_out)


def soft_kernel(
    info_ref, q_ref, do_ref, mine_ref, other_ref, out_ref, dq_ref, dmine_ref, dother_ref, s_ref, p_ref
):
    base, side, reach0, reach1 = info_ref[0], info_ref[1], info_ref[2], info_ref[3]
    lowest = jnp.minimum(jnp.maximum(base + 1, reach0), jnp.maximum(base + 1 + BLK, reach1))
    highest = jnp.maximum(jnp.maximum(base + BLK, reach0), jnp.maximum(base + 2 * BLK, reach1))
    place = lax.broadcasted_iota(jnp.int32, (1, ROWS), 1) // OWN
    limit = jnp.maximum(base + place + 1, jnp.where(place < BLK, reach0, reach1))
    per_source = GROUPS // 2
    span = PIECES * LB
    used = (highest + span - 1) // span

    def keys_of(ref, g, part):
        block = ref[pl.ds(g * PIECES, PIECES), part * HALF : (part + 1) * HALF, :]
        return block.reshape(KEYS, HD)

    def both(step, carry):
        def body(g, carry):
            carry = step(mine_ref, dmine_ref, g, g, side, carry)
            return step(other_ref, dother_ref, g, per_source + g, 1 - side, carry)

        return lax.fori_loop(0, used, body, carry)

    queries = q_ref[...]

    def find_max(ref, _, g, at, half, top):
        scores = dot(keys_of(ref, g, 0), queries, NT)
        first = g * span + half * HALF

        def masked():
            index = lax.broadcasted_iota(jnp.int32, (KEYS, 1), 0)
            where = first + (index // HALF) * LB + index % HALF
            return jnp.where(where < limit, scores, FAR_BELOW)

        scores = lax.cond((g + 1) * span <= lowest, lambda: scores, masked)
        s_ref[at] = scores
        return jnp.maximum(top, jnp.max(scores.reshape(KEYS // 8, 8, ROWS), axis=0))

    top = both(find_max, jnp.full((8, ROWS), FAR_BELOW, f32))
    top = jnp.max(top, axis=0, keepdims=True)
    factor = SCALE_SOFT * LOG2E
    shift = top * factor

    def weigh(ref, _, g, at, half, carry):
        mass, out = carry
        probs = jnp.exp2(s_ref[at] * factor - shift)
        mass = mass + jnp.sum(probs.reshape(KEYS // 8, 8, ROWS), axis=0)
        probs = probs.astype(bf16)
        p_ref[at] = probs
        return mass, out + dot(keys_of(ref, g, 1), probs, TN)

    mass, out = both(weigh, (jnp.zeros((8, ROWS), f32), jnp.zeros((HD, ROWS), f32)))
    inverse = 1.0 / jnp.sum(mass, axis=0, keepdims=True)
    out = (out * inverse).astype(bf16)
    out_ref[...] = out.T
    grads = do_ref[...].astype(f32).T
    adjust = inverse * SCALE_SOFT
    row_dot = jnp.sum(grads * out.astype(f32), axis=0, keepdims=True) * adjust
    grads = (grads * adjust).astype(bf16)
    grad_rows = grads.T

    def pull(ref, target, g, at, half, dq):
        probs = p_ref[at]
        moved = dot(keys_of(ref, g, 1), grads, NN)
        pulls = (probs.astype(f32) * (moved - row_dot)).astype(bf16)
        dk = dot(pulls, queries, NN)
        dv = dot(probs, grad_rows, NN) * (1.0 / SCALE_SOFT)
        target[pl.ds(g * PIECES, PIECES), 0:HALF, :] = dk.astype(bf16).reshape(PIECES, HALF, HD)
        target[pl.ds(g * PIECES, PIECES), HALF:LB, :] = dv.astype(bf16).reshape(PIECES, HALF, HD)
        return dq + dot(keys_of(ref, g, 0), pulls, TN)

    dq = both(pull, jnp.zeros((HD, ROWS), f32))
    dq_ref[...] = dq.astype(bf16).T

    def clear(g, carry):
        zero = jnp.zeros((PIECES, LB, HD), bf16)
        dmine_ref[pl.ds(g * PIECES, PIECES)] = zero
        dother_ref[pl.ds(g * PIECES, PIECES)] = zero
        return carry

    lax.fori_loop(used, per_source, clear, 0)


def merge_kernel(mine_ref, got_ref, back_ref, pay_ref):
    for j in range(CTX):
        pay_ref[j, 0:LB, :] = (mine_ref[j].astype(f32) + got_ref[j].astype(f32)).astype(bf16)
        pay_ref[j, LB:, :] = back_ref[j]


def suffix_kernel(got_ref, fades_ref, block_ref, out_ref):
    block = got_ref[0, 0:LB, :].astype(f32)
    for j in range(1, CTX):
        block = block + got_ref[j, 0:LB, :].astype(f32)
    block_ref[...] = block.astype(bf16)
    state = jnp.zeros((SLICE, HD), f32)
    for j in reversed(range(CTX)):
        out_ref[j] = state.astype(bf16)
        marks = fades_ref[j].astype(f32)
        fade = jnp.exp(marks[0:1, :] + marks[8:9, :])
        state = fade * state + got_ref[j, LB:, :].astype(f32)


def spread_kernel(mine_ref, other_ref, info_ref, dk_ref, dv_ref, scratch):
    side = info_ref[1]
    for part, target in ((0, dk_ref), (1, dv_ref)):
        for z in range(KVH):
            rows = slice(part * HALF, (part + 1) * HALF)
            scratch[pl.ds(side * (HALF * KVH) + z, HALF, stride=KVH), :] = mine_ref[z, rows, :].astype(f32)
            scratch[pl.ds((1 - side) * (HALF * KVH) + z, HALF, stride=KVH), :] = other_ref[z, rows, :].astype(f32)
        target[...] = scratch[...].astype(bf16)


def call(kernel, outs, scratch=(), smem=(), count=0, flops=0, limit=32):
    spaces = [pl.BlockSpec(memory_space=pltpu.SMEM if n in smem else pltpu.VMEM) for n in range(count)]
    return pl.pallas_call(
        kernel,
        out_shape=[jax.ShapeDtypeStruct(shape, kind) for shape, kind in outs],
        in_specs=spaces,
        out_specs=[pl.BlockSpec(memory_space=pltpu.VMEM) for _ in outs],
        scratch_shapes=[pltpu.VMEM(shape, kind) for shape, kind in scratch],
        compiler_params=pltpu.CompilerParams(vmem_limit_bytes=limit * 1024 * 1024),
        cost_estimate=pl.CostEstimate(flops=flops, bytes_accessed=1 << 20, transcendentals=0),
    )


WIDE = ((ROWS, HD), f32)
FLAT = ((ROWS, HD), bf16)
BY_HEAD = ((OWN, LB, HD), f32)
OTHER_CORE = [(i, i ^ 1) for i in range(HEADS)]
SAME_CORE = [[2 * z + c for z in range(KVH)] for c in range(2)]


def per_device(lin_q, lin_k, lin_v, log_decay, lin_gain, lin_grad, soft_q, soft_k, soft_v, soft_grad, span_reach):
    here, head = lax.axis_index("ctx"), lax.axis_index("head")
    kv, side = head // 2, head % 2
    flat = lambda x: x.reshape(ROWS, HD)
    lin_q, lin_k, lin_v, lin_grad, soft_q, soft_grad = map(
        flat, (lin_q, lin_k, lin_v, lin_grad, soft_q, soft_grad)
    )
    reaches = lax.dynamic_slice(span_reach, (2 * here,), (2,)) * BLK
    info = jnp.concatenate([jnp.stack([here * LB, side]).astype(jnp.int32), reaches])
    kv_half = jnp.concatenate(
        [
            lax.dynamic_slice(x, (side * HALF, kv, 0), (HALF, 1, HD)).reshape(HALF, HD)
            for x in (soft_k, soft_v)
        ]
    )
    decay = jnp.concatenate([log_decay, jnp.zeros((8 - OWN, LB), f32)])

    pay, within, heads = call(
        local_kernel,
        [((CTX, LB + SLICE + 16, HD), bf16), BY_HEAD, ((3, OWN, LB, HD), bf16)],
        [WIDE],
        count=5,
        flops=10**9,
    )(lin_q, lin_k, lin_v, decay, kv_half)
    got = lax.all_to_all(pay, "ctx", 0, 0)
    mine = got[:, :LB]
    fades = got[:, LB + SLICE :]
    other = lax.ppermute(mine, "head", OTHER_CORE)
    (prefixes,) = call(prefix_kernel, [((CTX, SLICE, HD), bf16)], count=1, flops=10**8)(got)
    state = lax.all_to_all(prefixes, "ctx", 0, 0).reshape(OWN * HD, HD)

    soft_out, soft_dq, dmine, dother = call(
        soft_kernel,
        [FLAT, FLAT, ((CTX, LB, HD), bf16), ((CTX, LB, HD), bf16)],
        [((GROUPS, KEYS, ROWS), f32), ((GROUPS, KEYS, ROWS), bf16)],
        smem=(0,),
        count=5,
        flops=10**10,
        limit=56,
    )(info, soft_q, soft_grad, mine, other)
    dgot = lax.ppermute(dother, "head", OTHER_CORE)

    attended, upstream, sums = call(
        attend_kernel,
        [BY_HEAD, BY_HEAD, ((HEADS, 8, LB), f32)],
        [WIDE],
        count=6,
        flops=10**9,
    )(within, heads, state, decay, lin_grad, lin_gain)
    sums = lax.all_to_all(sums, "head", 0, 0)
    lin_out, att_grad, back = call(
        grad_kernel,
        [FLAT, ((OWN, LB, HD), bf16), ((OWN * HD, HD), bf16)],
        [WIDE],
        count=6,
        flops=10**9,
    )(attended, upstream, sums, heads, decay, lin_gain)
    (pay_back,) = call(merge_kernel, [((CTX, LB + SLICE, HD), bf16)], count=3, flops=10**8)(
        dmine, dgot, back.reshape(CTX, SLICE, HD)
    )
    got_back = lax.all_to_all(pay_back, "ctx", 0, 0)
    lin_dq, dk_own, dv_own = call(
        inner_kernel, [FLAT, BY_HEAD, BY_HEAD], [WIDE], count=4, flops=10**9
    )(heads, att_grad, state, decay)
    block, suffixes = call(
        suffix_kernel, [((LB, HD), bf16), ((CTX, SLICE, HD), bf16)], count=2, flops=10**8
    )(got_back, fades)
    later = lax.all_to_all(suffixes, "ctx", 0, 0).reshape(OWN * HD, HD)
    spread = lax.all_to_all(
        jnp.broadcast_to(block[None], (KVH, LB, HD)), "head", 0, 0, axis_index_groups=SAME_CORE
    )
    spread_other = lax.ppermute(spread, "head", OTHER_CORE)
    lin_dk, lin_dv = call(finish_kernel, [FLAT, FLAT], [WIDE], count=5, flops=10**9)(
        dk_own, dv_own, heads, later, decay
    )
    soft_dk, soft_dv = call(
        spread_kernel,
        [((LB * KVH, HD), bf16), ((LB * KVH, HD), bf16)],
        [((LB * KVH, HD), f32)],
        smem=(2,),
        count=3,
        flops=10**8,
    )(spread, spread_other, info)
    deep = lambda x: x.reshape(LB, OWN, HD)
    return (
        deep(lin_out),
        deep(lin_dq),
        deep(lin_dk),
        deep(lin_dv),
        deep(soft_out),
        deep(soft_dq),
        soft_dk.reshape(LB, KVH, HD),
        soft_dv.reshape(LB, KVH, HD),
    )


def solution(mesh):
    long, short = P("ctx", "head", None), P("ctx", None, None)
    return jax.shard_map(
        per_device,
        mesh=mesh,
        in_specs=(long, long, long, P("head", "ctx"), P("head", None), long, long, short, short, long, P()),
        out_specs=(long, long, long, long, long, long, short, short),
        check_vma=False,
    )
```

```python
import functools
import math

import jax
import jax.numpy as jnp
from jax import lax
from jax.experimental import pallas as pl
from jax.experimental.pallas import tpu as pltpu
from jax.sharding import PartitionSpec as P

HEAD_TOTAL = 64
HD = 128
KVH = 8
LB = 256
BLK = 128
CTX = 16
HEADS = 16
OWN = 4
ROWS = LB * OWN
HALF = LB // 2
SLICE = OWN * HD // CTX
EPSILON = 1e-05
FAR_BELOW = -1e30
SCALE_LIN = 1.0 / HD
SCALE_SOFT = 1.0 / math.sqrt(HD)
LOG2E = 1.4426950408889634
KEYS = 512
PIECES = KEYS // HALF
PER_SOURCE = CTX // PIECES
GROUPS = 2 * PER_SOURCE
SPAN = PIECES * LB

f32 = jnp.float32
bf16 = jnp.bfloat16
PRECISE = lax.Precision.HIGHEST


def dot(a, b, dims, precision=None):
    return lax.dot_general(a, b, (dims, ((), ())), precision=precision, preferred_element_type=f32)


NN = ((1,), (0,))
NT = ((1,), (1,))
TN = ((0,), (0,))


def split_heads(source, scratch):
    scratch[...] = source[...].astype(f32)
    return [scratch[pl.ds(h, LB, stride=OWN), :] for h in range(OWN)]


def join_heads(parts, scratch, target):
    for h in range(OWN):
        scratch[pl.ds(h, LB, stride=OWN), :] = parts[h]
    target[...] = scratch[...].astype(bf16)


def run_sums(log_decay):
    row = lax.broadcasted_iota(jnp.int32, (LB, LB), 0)
    col = lax.broadcasted_iota(jnp.int32, (LB, LB), 1)
    upto = (row <= col).astype(f32)
    as_rows = dot(log_decay, upto, NN, PRECISE)
    as_cols = dot((row >= col).astype(f32), log_decay, NT, PRECISE)
    return as_rows, as_cols, row, col


def local_kernel(
    q_hbm, k_hbm, v_hbm, decay_hbm, sk_hbm, sv_hbm, pay_hbm, within_hbm, heads_hbm,
    scratch, raw, halves, decay_ref, kv_ref, own_ref, within_ref, heads_ref, sems, out_sems,
):
    side = lax.axis_index("head") % 2
    kv = lax.axis_index("head") // 2
    half = pl.ds(pl.multiple_of(side * (HALF * KVH), HALF * KVH), HALF * KVH)
    copies = [
        pltpu.make_async_copy(sk_hbm.at[half], halves.at[0], sems.at[0]),
        pltpu.make_async_copy(sv_hbm.at[half], halves.at[1], sems.at[1]),
        pltpu.make_async_copy(k_hbm, raw.at[1], sems.at[2]),
        pltpu.make_async_copy(v_hbm, raw.at[2], sems.at[3]),
        pltpu.make_async_copy(q_hbm, raw.at[0], sems.at[4]),
        pltpu.make_async_copy(decay_hbm, decay_ref, sems.at[5]),
    ]
    for copy in copies:
        copy.start()
    for n in range(2):
        copies[n].wait()
        scratch[...] = halves[n].astype(f32)
        kv_ref[n * HALF : (n + 1) * HALF, :] = scratch[pl.ds(kv, HALF, stride=KVH), :].astype(bf16)
    sent = [
        pltpu.make_async_copy(kv_ref, pay_hbm.at[j, pl.ds(0, LB)], out_sems.at[j]) for j in range(CTX)
    ]
    for copy in sent:
        copy.start()
    copies[5].wait()
    as_rows, as_cols, row, col = run_sums(decay_ref[...])
    copies[2].wait()
    keys_wide = split_heads(raw.at[1], scratch)
    copies[3].wait()
    values = [x.astype(bf16) for x in split_heads(raw.at[2], scratch)]
    for h in range(OWN):
        run_col = as_cols[:, h : h + 1]
        total = as_rows[h : h + 1, LB - 1 : LB]
        heads_ref[1, h] = keys_wide[h].astype(bf16)
        heads_ref[2, h] = values[h]
        tailed = (keys_wide[h] * jnp.exp(total - run_col)).astype(bf16)
        own = dot(tailed, values[h], TN).astype(bf16)
        high = total.astype(bf16).astype(f32)
        marks = jnp.concatenate(
            [jnp.broadcast_to(high, (8, HD)), jnp.broadcast_to(total - high, (8, HD))], axis=0
        ).astype(bf16)
        for i in range(OWN):
            j = h * OWN + i
            own_ref[j, 0:SLICE, :] = own[i * SLICE : (i + 1) * SLICE]
            own_ref[j, SLICE:, :] = marks
    states = pltpu.make_async_copy(own_ref, pay_hbm.at[:, pl.ds(LB, SLICE + 16)], out_sems.at[CTX])
    states.start()
    copies[4].wait()
    queries = [x.astype(bf16) for x in split_heads(raw.at[0], scratch)]
    for h in range(OWN):
        heads_ref[0, h] = queries[h]
    kept = pltpu.make_async_copy(heads_ref, heads_hbm, out_sems.at[CTX + 1])
    kept.start()
    for h in range(OWN):
        decays = jnp.exp(jnp.where(row >= col, as_cols[:, h : h + 1] - as_rows[h : h + 1, :], FAR_BELOW))
        weights = (dot(queries[h], heads_ref[1, h], NT) * decays * SCALE_LIN).astype(bf16)
        within_ref[h] = dot(weights, values[h], NN)
    inner = pltpu.make_async_copy(within_ref, within_hbm, out_sems.at[CTX + 2])
    inner.start()
    for copy in sent + [states, kept, inner]:
        copy.wait()


def prefix_kernel(got_ref, out_ref):
    state = jnp.zeros((SLICE, HD), f32)
    for j in range(CTX):
        out_ref[j] = state.astype(bf16)
        marks = got_ref[j, LB + SLICE :, :].astype(f32)
        fade = jnp.exp(marks[0:1, :] + marks[8:9, :])
        state = fade * state + got_ref[j, LB : LB + SLICE, :].astype(f32)


def attend_kernel(within_ref, heads_ref, state_ref, decay_ref, grad_ref, gain_ref, att_ref, up_ref, sums_ref, scratch):
    _, as_cols, _, _ = run_sums(decay_ref[...])
    grads = split_heads(grad_ref, scratch)
    squares = jnp.zeros((LB, HD), f32)
    crossed = jnp.zeros((LB, HD), f32)
    for h in range(OWN):
        state = state_ref[h * HD : (h + 1) * HD, :]
        fade = SCALE_LIN * jnp.exp(as_cols[:, h : h + 1])
        attended = within_ref[h] + fade * dot(heads_ref[0, h], state, NN)
        upstream = grads[h] * gain_ref[h : h + 1, :]
        att_ref[h] = attended
        up_ref[h] = upstream
        squares = squares + attended * attended
        crossed = crossed + upstream * attended
    ones = jnp.ones((8, HD), f32)
    square_row = dot(ones, squares, NT, PRECISE)
    cross_row = dot(ones, crossed, NT, PRECISE)
    both = [x[0:1, n * HALF : (n + 1) * HALF] for x in (square_row, cross_row) for n in range(2)]
    for j in range(HEADS):
        for n in range(4):
            sums_ref[j, n : n + 1, :] = both[n]


def grad_kernel(att_ref, up_ref, got_ref, heads_ref, decay_ref, gain_ref, out_ref, ag_ref, back_ref, scratch):
    _, as_cols, row, col = run_sums(decay_ref[...])
    total = got_ref[0]
    for j in range(1, HEADS):
        total = total + got_ref[j]
    wide = jnp.concatenate(
        [jnp.concatenate([total[n : n + 1], total[n + 1 : n + 2]], axis=1) for n in (0, 2)]
        + [jnp.zeros((6, LB), f32)],
        axis=0,
    )
    cols = dot((row == col).astype(f32), wide, NT, PRECISE)
    inverse = lax.rsqrt(cols[:, 0:1] / (HEAD_TOTAL * HD) + EPSILON)
    pull = inverse * inverse * inverse * (cols[:, 1:2] / (HEAD_TOTAL * HD))
    outs = []
    for h in range(OWN):
        attended = att_ref[h]
        outs.append(attended * inverse * gain_ref[h : h + 1, :])
        att_grad = (inverse * up_ref[h] - attended * pull).astype(bf16)
        ag_ref[h] = att_grad
        faded = (heads_ref[0, h].astype(f32) * jnp.exp(as_cols[:, h : h + 1])).astype(bf16)
        back = dot(faded, att_grad, TN).astype(bf16)
        back_ref[h * HD : (h + 1) * HD, :] = back
    join_heads(outs, scratch, out_ref)


def inner_kernel(
    heads_ref, ag_ref, state_ref, later_ref, decay_ref, dq_ref, dk_ref, dv_ref, scratch
):
    as_rows, as_cols, row, col = run_sums(decay_ref[...])
    query_grads, key_grads, value_grads = [], [], []
    for h in range(OWN):
        run_row, run_col = as_rows[h : h + 1, :], as_cols[:, h : h + 1]
        query, key, value, grad = heads_ref[0, h], heads_ref[1, h], heads_ref[2, h], ag_ref[h]
        decays = SCALE_LIN * jnp.exp(jnp.where(row >= col, run_col - run_row, FAR_BELOW))
        turned = SCALE_LIN * jnp.exp(jnp.where(col >= row, run_row - run_col, FAR_BELOW))
        grad_weights = (dot(grad, value, NT) * decays).astype(bf16)
        grad_turned = (dot(value, grad, NT) * turned).astype(bf16)
        weights_turned = (dot(key, query, NT) * turned).astype(bf16)
        state = state_ref[h * HD : (h + 1) * HD, :]
        later = later_ref[h * HD : (h + 1) * HD, :]
        fade = SCALE_LIN * jnp.exp(run_col)
        tail = SCALE_LIN * jnp.exp(run_row[:, LB - 1 : LB] - run_col)
        query_grads.append(dot(grad_weights, key, NN) + fade * dot(grad, state, NT))
        key_grads.append(dot(grad_turned, query, NN) + tail * dot(value, later, NT))
        value_grads.append(dot(weights_turned, grad, NN) + tail * dot(key, later, NN))
    join_heads(query_grads, scratch, dq_ref)
    join_heads(key_grads, scratch, dk_ref)
    join_heads(value_grads, scratch, dv_ref)


def soft_limits(reach_ref):
    here = lax.axis_index("ctx")
    base = here * LB
    reach0, reach1 = reach_ref[2 * here] * BLK, reach_ref[2 * here + 1] * BLK
    place = lax.broadcasted_iota(jnp.int32, (1, ROWS), 1) // OWN
    limit = jnp.maximum(base + place + 1, jnp.where(place < BLK, reach0, reach1))
    lowest = jnp.minimum(jnp.maximum(base + 1, reach0), jnp.maximum(base + 1 + BLK, reach1))
    highest = jnp.maximum(jnp.maximum(base + BLK, reach0), jnp.maximum(base + 2 * BLK, reach1))
    return limit, lowest // SPAN, (highest + SPAN - 1) // SPAN


def keys_of(ref, g, part):
    return ref[pl.ds(g * PIECES, PIECES), part * HALF : (part + 1) * HALF, :].reshape(KEYS, HD)


def soft_kernel(
    reach_ref, q_ref, do_ref, mine_ref, other_ref, out_ref, dq_ref, dmine_ref, dother_ref,
    s_ref, p_ref, top_ref, mass_ref, sum_ref, turned_ref, rows_ref,
):
    side = lax.axis_index("head") % 2
    limit, full, used = soft_limits(reach_ref)
    top_ref[...] = jnp.full((8, ROWS), FAR_BELOW, f32)
    mass_ref[...] = jnp.zeros((8, ROWS), f32)
    sum_ref[...] = jnp.zeros((HD, ROWS), f32)

    def find_max(low, high, masked):
        @pl.loop(low, high)
        def _(g):
            for at, ref, half in ((g, mine_ref, side), (PER_SOURCE + g, other_ref, 1 - side)):
                scores = dot(keys_of(ref, g, 0), q_ref[...], NT)
                if masked:
                    index = lax.broadcasted_iota(jnp.int32, (KEYS, 1), 0)
                    where = g * SPAN + half * HALF + (index // HALF) * LB + index % HALF
                    scores = jnp.where(where < limit, scores, FAR_BELOW)
                s_ref[at] = scores
                top_ref[...] = jnp.maximum(
                    top_ref[...], jnp.max(scores.reshape(KEYS // 8, 8, ROWS), axis=0)
                )

    find_max(0, full, False)
    find_max(full, used, True)
    factor = SCALE_SOFT * LOG2E
    shift = jnp.max(top_ref[...], axis=0, keepdims=True) * factor

    @pl.loop(0, used)
    def _(g):
        for at, ref in ((g, mine_ref), (PER_SOURCE + g, other_ref)):
            probs = jnp.exp2(s_ref[at] * factor - shift)
            mass_ref[...] = mass_ref[...] + jnp.sum(probs.reshape(KEYS // 8, 8, ROWS), axis=0)
            probs = probs.astype(bf16)
            p_ref[at] = probs
            sum_ref[...] = sum_ref[...] + dot(keys_of(ref, g, 1), probs, TN)

    inverse = 1.0 / jnp.sum(mass_ref[...], axis=0, keepdims=True)
    out = (sum_ref[...] * inverse).astype(bf16)
    out_ref[...] = out.T
    grads = do_ref[...].astype(f32).T
    adjust = inverse * SCALE_SOFT
    row_dot = jnp.sum(grads * out.astype(f32), axis=0, keepdims=True) * adjust
    turned = (grads * adjust).astype(bf16)
    turned_ref[...] = turned
    rows_ref[...] = turned.T
    sum_ref[...] = jnp.zeros((HD, ROWS), f32)

    @pl.loop(0, used)
    def _(g):
        for at, ref, target in ((g, mine_ref, dmine_ref), (PER_SOURCE + g, other_ref, dother_ref)):
            probs = p_ref[at]
            moved = dot(keys_of(ref, g, 1), turned_ref[...], NN)
            pulls = (probs.astype(f32) * (moved - row_dot)).astype(bf16)
            dk = dot(pulls, q_ref[...], NN)
            dv = dot(probs, rows_ref[...], NN) * (1.0 / SCALE_SOFT)
            target[pl.ds(g * PIECES, PIECES), 0:HALF, :] = dk.astype(bf16).reshape(PIECES, HALF, HD)
            target[pl.ds(g * PIECES, PIECES), HALF:LB, :] = dv.astype(bf16).reshape(PIECES, HALF, HD)
            sum_ref[...] = sum_ref[...] + dot(keys_of(ref, g, 0), pulls, TN)

    dq_ref[...] = sum_ref[...].astype(bf16).T

    @pl.loop(used, PER_SOURCE)
    def _(g):
        zero = jnp.zeros((PIECES, LB, HD), bf16)
        dmine_ref[pl.ds(g * PIECES, PIECES)] = zero
        dother_ref[pl.ds(g * PIECES, PIECES)] = zero


def merge_kernel(mine_ref, got_ref, back_ref, pay_ref):
    for j in range(CTX):
        pay_ref[j, 0:LB, :] = (mine_ref[j].astype(f32) + got_ref[j].astype(f32)).astype(bf16)
        pay_ref[j, LB:, :] = back_ref[j]


def reduce_kernel(got_ref, block_ref, later_ref):
    block = got_ref[0, 0:LB, :].astype(f32)
    for j in range(1, CTX):
        block = block + got_ref[j, 0:LB, :].astype(f32)
    block = block.astype(bf16)
    for z in range(KVH):
        block_ref[z] = block
    for j in range(CTX):
        later_ref[j * SLICE : (j + 1) * SLICE, :] = got_ref[j, LB:, :]


def suffix_kernel(got_ref, first_ref, out_ref):
    state = jnp.zeros((SLICE, HD), f32)
    for j in reversed(range(CTX)):
        out_ref[j] = state.astype(bf16)
        marks = first_ref[j, LB + SLICE :, :].astype(f32)
        fade = jnp.exp(marks[0:1, :] + marks[8:9, :])
        state = fade * state + got_ref[j].astype(f32)


def spread_kernel(mine_ref, other_ref, dk_ref, dv_ref, scratch):
    side = lax.axis_index("head") % 2
    for part, target in ((0, dk_ref), (1, dv_ref)):
        for z in range(KVH):
            rows = slice(part * HALF, (part + 1) * HALF)
            scratch[pl.ds(side * (HALF * KVH) + z, HALF, stride=KVH), :] = mine_ref[z, rows, :].astype(f32)
            scratch[pl.ds((1 - side) * (HALF * KVH) + z, HALF, stride=KVH), :] = other_ref[z, rows, :].astype(f32)
        target[...] = scratch[...].astype(bf16)


def call(kernel, outs, scratch=(), smem=(), hbm=(), hbm_out=(), count=0, flops=0, limit=8):
    spaces = [
        pl.BlockSpec(memory_space=pltpu.SMEM if n in smem else pl.ANY if n in hbm else pltpu.VMEM)
        for n in range(count)
    ]
    return pl.pallas_call(
        kernel,
        out_shape=[jax.ShapeDtypeStruct(shape, kind) for shape, kind in outs],
        in_specs=spaces,
        out_specs=[
            pl.BlockSpec(memory_space=pl.ANY if n in hbm_out else pltpu.VMEM) for n in range(len(outs))
        ],
        scratch_shapes=[x if not isinstance(x, tuple) else pltpu.VMEM(*x) for x in scratch],
        compiler_params=pltpu.CompilerParams(vmem_limit_bytes=limit * 1024 * 1024),
        cost_estimate=pl.CostEstimate(flops=flops, bytes_accessed=1 << 20, transcendentals=0),
    )


def after(value, *earlier):
    return lax.optimization_barrier((value,) + earlier)[0]


WIDE = ((ROWS, HD), f32)
FLAT = ((ROWS, HD), bf16)
BY_HEAD = ((OWN, LB, HD), f32)
PROBS = ((GROUPS, KEYS, ROWS), bf16)
KEY_PARTS = ((CTX, LB, HD), bf16)
OTHER_CORE = [(i, i ^ 1) for i in range(HEADS)]
SAME_CORE = [[2 * z + c for z in range(KVH)] for c in range(2)]


def per_device(lin_q, lin_k, lin_v, decay, lin_gain, lin_grad, soft_q, soft_k, soft_v, soft_grad, reach):
    flat = lambda x: x.reshape(-1, HD)
    lin_q, lin_k, lin_v, lin_grad, soft_q, soft_grad, soft_k, soft_v = map(
        flat, (lin_q, lin_k, lin_v, lin_grad, soft_q, soft_grad, soft_k, soft_v)
    )
    pay, within, heads = call(
        local_kernel,
        [((CTX, LB + SLICE + 16, HD), bf16), BY_HEAD, ((3, OWN, LB, HD), bf16)],
        [
            WIDE,
            ((3, ROWS, HD), bf16),
            ((2, HALF * KVH, HD), bf16),
            ((OWN, LB), f32),
            ((LB, HD), bf16),
            ((CTX, SLICE + 16, HD), bf16),
            BY_HEAD,
            ((3, OWN, LB, HD), bf16),
            pltpu.SemaphoreType.DMA((6,)),
            pltpu.SemaphoreType.DMA((CTX + 3,)),
        ],
        hbm=(0, 1, 2, 3, 4, 5),
        hbm_out=(0, 1, 2),
        count=6,
        flops=10**9,
        limit=60,
    )(lin_q, lin_k, lin_v, decay, soft_k, soft_v)
    mine = lax.all_to_all(pay, "ctx", 0, 0)
    other = lax.ppermute(mine, "head", OTHER_CORE)
    (prefixes,) = call(prefix_kernel, [((CTX, SLICE, HD), bf16)], count=1, flops=10**8)(mine)
    state = lax.all_to_all(prefixes, "ctx", 0, 0).reshape(OWN * HD, HD)
    attended, upstream, sums = call(
        attend_kernel,
        [BY_HEAD, BY_HEAD, ((HEADS, 4, HALF), f32)],
        [WIDE],
        count=6,
        flops=10**9,
    )(within, heads, state, decay, lin_grad, lin_gain)
    total = lax.all_to_all(sums, "head", 0, 0)
    lin_out, att_grad, back = call(
        grad_kernel,
        [FLAT, ((OWN, LB, HD), bf16), ((OWN * HD, HD), bf16)],
        [WIDE],
        count=6,
        flops=10**9,
    )(attended, upstream, total, heads, decay, lin_gain)
    backs = lax.all_to_all(back.reshape(CTX, SLICE, HD), "ctx", 0, 0)
    (suffixes,) = call(suffix_kernel, [((CTX, SLICE, HD), bf16)], count=2, flops=10**8)(backs, mine)
    soft_out, soft_dq, dmine, dother = call(
        soft_kernel,
        [FLAT, FLAT, KEY_PARTS, KEY_PARTS],
        [
            ((GROUPS, KEYS, ROWS), f32),
            PROBS,
            ((8, ROWS), f32),
            ((8, ROWS), f32),
            ((HD, ROWS), f32),
            ((HD, ROWS), bf16),
            FLAT,
        ],
        smem=(0,),
        count=5,
        flops=10**10,
        limit=36,
    )(reach, after(soft_q, suffixes), soft_grad, mine, other)
    dgot = lax.ppermute(dother, "head", OTHER_CORE)
    (pay_back,) = call(merge_kernel, [((CTX, LB + SLICE, HD), bf16)], count=3, flops=10**8)(
        dmine, dgot, suffixes
    )
    got_back = lax.all_to_all(pay_back, "ctx", 0, 0)
    blocks, later = call(
        reduce_kernel, [((KVH, LB, HD), bf16), ((OWN * HD, HD), bf16)], count=1, flops=10**8
    )(got_back)
    spread = lax.all_to_all(blocks, "head", 0, 0, axis_index_groups=SAME_CORE)
    lin_dq, lin_dk, lin_dv = call(inner_kernel, [FLAT, FLAT, FLAT], [WIDE], count=5, flops=4 * 10**9)(
        heads, att_grad, state, later, decay
    )
    spread = after(spread, lin_dk)
    spread_other = lax.ppermute(spread, "head", OTHER_CORE)
    soft_dk, soft_dv = call(
        spread_kernel,
        [((LB * KVH, HD), bf16), ((LB * KVH, HD), bf16)],
        [((LB * KVH, HD), f32)],
        count=2,
        flops=10**8,
    )(spread, spread_other)
    deep = lambda x: x.reshape(LB, OWN, HD)
    return (
        deep(lin_out),
        deep(lin_dq),
        deep(lin_dk),
        deep(lin_dv),
        deep(soft_out),
        deep(soft_dq),
        soft_dk.reshape(LB, KVH, HD),
        soft_dv.reshape(LB, KVH, HD),
    )


def solution(mesh):
    long, short = P("ctx", "head", None), P("ctx", None, None)
    return jax.shard_map(
        per_device,
        mesh=mesh,
        in_specs=(long, long, long, P("head", "ctx"), P("head", None), long, long, short, short, long, P()),
        out_specs=(long, long, long, long, long, long, short, short),
        check_vma=False,
    )
```

```python
import functools
import math

import jax
import jax.numpy as jnp
from jax import lax
from jax.experimental import pallas as pl
from jax.experimental.pallas import tpu as pltpu
from jax.sharding import PartitionSpec as P

HEAD_TOTAL = 64
HD = 128
KVH = 8
LB = 256
BLK = 128
CTX = 16
HEADS = 16
OWN = 4
ROWS = LB * OWN
HALF = LB // 2
SLICE = OWN * HD // CTX
EPSILON = 1e-05
FAR_BELOW = -1e30
SCALE_LIN = 1.0 / HD
SCALE_SOFT = 1.0 / math.sqrt(HD)
LOG2E = 1.4426950408889634
KEYS = 512
PIECES = KEYS // HALF
PER_SOURCE = CTX // PIECES
GROUPS = 2 * PER_SOURCE
SPAN = PIECES * LB

f32 = jnp.float32
bf16 = jnp.bfloat16
PRECISE = lax.Precision.HIGHEST


def dot(a, b, dims, precision=None):
    return lax.dot_general(a, b, (dims, ((), ())), precision=precision, preferred_element_type=f32)


NN = ((1,), (0,))
NT = ((1,), (1,))
TN = ((0,), (0,))


def split_heads(source, scratch):
    scratch[...] = source[...].astype(f32)
    return [scratch[pl.ds(h, LB, stride=OWN), :] for h in range(OWN)]


def join_heads(parts, scratch, target):
    for h in range(OWN):
        scratch[pl.ds(h, LB, stride=OWN), :] = parts[h]
    target[...] = scratch[...].astype(bf16)


def run_sums(log_decay):
    row = lax.broadcasted_iota(jnp.int32, (LB, LB), 0)
    col = lax.broadcasted_iota(jnp.int32, (LB, LB), 1)
    upto = (row <= col).astype(f32)
    as_rows = dot(log_decay, upto, NN, PRECISE)
    as_cols = dot((row >= col).astype(f32), log_decay, NT, PRECISE)
    return as_rows, as_cols, row, col


def local_kernel(
    q_hbm, k_hbm, v_hbm, decay_hbm, sk_hbm, sv_hbm, sq_hbm, sg_hbm, pay_hbm, within_hbm, heads_hbm, trade_hbm,
    scratch, raw, halves, decay_ref, kv_ref, own_ref, within_ref, heads_ref, trade_ref, sems, out_sems,
):
    side = lax.axis_index("head") % 2
    kv = lax.axis_index("head") // 2
    half = pl.ds(pl.multiple_of(side * (HALF * KVH), HALF * KVH), HALF * KVH)
    copies = [
        pltpu.make_async_copy(sk_hbm.at[half], halves.at[0], sems.at[0]),
        pltpu.make_async_copy(sv_hbm.at[half], halves.at[1], sems.at[1]),
        pltpu.make_async_copy(k_hbm, raw.at[1], sems.at[2]),
        pltpu.make_async_copy(v_hbm, raw.at[2], sems.at[3]),
        pltpu.make_async_copy(q_hbm, raw.at[0], sems.at[4]),
        pltpu.make_async_copy(decay_hbm, decay_ref, sems.at[5]),
    ] + [
        pltpu.make_async_copy(
            x.at[pl.ds(ROWS // 2, ROWS // 2)], trade_ref.at[pl.ds(n * (ROWS // 2), ROWS // 2)], sems.at[6 + n]
        )
        for n, x in enumerate((sq_hbm, sg_hbm))
    ]
    for copy in copies:
        copy.start()
    for n in range(2):
        copies[n].wait()
        scratch[...] = halves[n].astype(f32)
        kv_ref[n * HALF : (n + 1) * HALF, :] = scratch[pl.ds(kv, HALF, stride=KVH), :].astype(bf16)
    sent = [
        pltpu.make_async_copy(kv_ref, pay_hbm.at[j, pl.ds(0, LB)], out_sems.at[j]) for j in range(CTX)
    ]
    for copy in sent:
        copy.start()
    for copy in copies[6:]:
        copy.wait()
    traded = pltpu.make_async_copy(trade_ref, trade_hbm, out_sems.at[CTX + 3])
    traded.start()
    copies[5].wait()
    as_rows, as_cols, row, col = run_sums(decay_ref[...])
    copies[2].wait()
    keys_wide = split_heads(raw.at[1], scratch)
    copies[3].wait()
    values = [x.astype(bf16) for x in split_heads(raw.at[2], scratch)]
    for h in range(OWN):
        run_col = as_cols[:, h : h + 1]
        total = as_rows[h : h + 1, LB - 1 : LB]
        heads_ref[1, h] = keys_wide[h].astype(bf16)
        heads_ref[2, h] = values[h]
        tailed = (keys_wide[h] * jnp.exp(total - run_col)).astype(bf16)
        own = dot(tailed, values[h], TN).astype(bf16)
        high = total.astype(bf16).astype(f32)
        marks = jnp.concatenate(
            [jnp.broadcast_to(high, (8, HD)), jnp.broadcast_to(total - high, (8, HD))], axis=0
        ).astype(bf16)
        for i in range(OWN):
            j = h * OWN + i
            own_ref[j, 0:SLICE, :] = own[i * SLICE : (i + 1) * SLICE]
            own_ref[j, SLICE:, :] = marks
    states = pltpu.make_async_copy(own_ref, pay_hbm.at[:, pl.ds(LB, SLICE + 16)], out_sems.at[CTX])
    states.start()
    copies[4].wait()
    queries = [x.astype(bf16) for x in split_heads(raw.at[0], scratch)]
    for h in range(OWN):
        heads_ref[0, h] = queries[h]
    kept = pltpu.make_async_copy(heads_ref, heads_hbm, out_sems.at[CTX + 1])
    kept.start()
    for h in range(OWN):
        decays = jnp.exp(jnp.where(row >= col, as_cols[:, h : h + 1] - as_rows[h : h + 1, :], FAR_BELOW))
        weights = (dot(queries[h], heads_ref[1, h], NT) * decays * SCALE_LIN).astype(bf16)
        within_ref[h] = dot(weights, values[h], NN)
    inner = pltpu.make_async_copy(within_ref, within_hbm, out_sems.at[CTX + 2])
    inner.start()
    for copy in sent + [traded, states, kept, inner]:
        copy.wait()


def prefix_kernel(got_ref, out_ref):
    state = jnp.zeros((SLICE, HD), f32)
    for j in range(CTX):
        out_ref[j] = state.astype(bf16)
        marks = got_ref[j, LB + SLICE :, :].astype(f32)
        fade = jnp.exp(marks[0:1, :] + marks[8:9, :])
        state = fade * state + got_ref[j, LB : LB + SLICE, :].astype(f32)


def attend_kernel(within_ref, heads_ref, state_ref, decay_ref, grad_ref, gain_ref, att_ref, up_ref, sums_ref, scratch):
    _, as_cols, _, _ = run_sums(decay_ref[...])
    grads = split_heads(grad_ref, scratch)
    squares = jnp.zeros((LB, HD), f32)
    crossed = jnp.zeros((LB, HD), f32)
    for h in range(OWN):
        state = state_ref[h * HD : (h + 1) * HD, :]
        fade = SCALE_LIN * jnp.exp(as_cols[:, h : h + 1])
        attended = within_ref[h] + fade * dot(heads_ref[0, h], state, NN)
        upstream = grads[h] * gain_ref[h : h + 1, :]
        att_ref[h] = attended
        up_ref[h] = upstream
        squares = squares + attended * attended
        crossed = crossed + upstream * attended
    ones = jnp.ones((8, HD), f32)
    square_row = dot(ones, squares, NT, PRECISE)
    cross_row = dot(ones, crossed, NT, PRECISE)
    both = [x[0:1, n * HALF : (n + 1) * HALF] for x in (square_row, cross_row) for n in range(2)]
    for j in range(HEADS):
        for n in range(4):
            sums_ref[j, n : n + 1, :] = both[n]


def grad_kernel(att_ref, up_ref, got_ref, heads_ref, decay_ref, gain_ref, out_ref, ag_ref, back_ref, scratch):
    _, as_cols, row, col = run_sums(decay_ref[...])
    total = got_ref[0]
    for j in range(1, HEADS):
        total = total + got_ref[j]
    wide = jnp.concatenate(
        [jnp.concatenate([total[n : n + 1], total[n + 1 : n + 2]], axis=1) for n in (0, 2)]
        + [jnp.zeros((6, LB), f32)],
        axis=0,
    )
    cols = dot((row == col).astype(f32), wide, NT, PRECISE)
    inverse = lax.rsqrt(cols[:, 0:1] / (HEAD_TOTAL * HD) + EPSILON)
    pull = inverse * inverse * inverse * (cols[:, 1:2] / (HEAD_TOTAL * HD))
    outs = []
    for h in range(OWN):
        attended = att_ref[h]
        outs.append(attended * inverse * gain_ref[h : h + 1, :])
        att_grad = (inverse * up_ref[h] - attended * pull).astype(bf16)
        ag_ref[h] = att_grad
        faded = (heads_ref[0, h].astype(f32) * jnp.exp(as_cols[:, h : h + 1])).astype(bf16)
        back = dot(faded, att_grad, TN).astype(bf16)
        back_ref[h * HD : (h + 1) * HD, :] = back
    join_heads(outs, scratch, out_ref)


def inner_kernel(
    heads_ref, ag_ref, state_ref, later_ref, decay_ref, out_ref, sdq_ref, traded_ref,
    dq_ref, dk_ref, dv_ref, soft_out_ref, soft_dq_ref, scratch,
):
    for n, (own, target) in enumerate(((out_ref, soft_out_ref), (sdq_ref, soft_dq_ref))):
        target[0 : ROWS // 2] = own[...]
        target[ROWS // 2 :] = traded_ref[n * (ROWS // 2) : (n + 1) * (ROWS // 2)]
    as_rows, as_cols, row, col = run_sums(decay_ref[...])
    query_grads, key_grads, value_grads = [], [], []
    for h in range(OWN):
        run_row, run_col = as_rows[h : h + 1, :], as_cols[:, h : h + 1]
        query, key, value, grad = heads_ref[0, h], heads_ref[1, h], heads_ref[2, h], ag_ref[h]
        decays = SCALE_LIN * jnp.exp(jnp.where(row >= col, run_col - run_row, FAR_BELOW))
        turned = SCALE_LIN * jnp.exp(jnp.where(col >= row, run_row - run_col, FAR_BELOW))
        grad_weights = (dot(grad, value, NT) * decays).astype(bf16)
        grad_turned = (dot(value, grad, NT) * turned).astype(bf16)
        weights_turned = (dot(key, query, NT) * turned).astype(bf16)
        state = state_ref[h * HD : (h + 1) * HD, :]
        later = later_ref[h * HD : (h + 1) * HD, :]
        fade = SCALE_LIN * jnp.exp(run_col)
        tail = SCALE_LIN * jnp.exp(run_row[:, LB - 1 : LB] - run_col)
        query_grads.append(dot(grad_weights, key, NN) + fade * dot(grad, state, NT))
        key_grads.append(dot(grad_turned, query, NN) + tail * dot(value, later, NT))
        value_grads.append(dot(weights_turned, grad, NN) + tail * dot(key, later, NN))
    join_heads(query_grads, scratch, dq_ref)
    join_heads(key_grads, scratch, dk_ref)
    join_heads(value_grads, scratch, dv_ref)


def keys_of(ref, g, part):
    return ref[pl.ds(g * PIECES, PIECES), part * HALF : (part + 1) * HALF, :].reshape(KEYS, HD)


def soft_kernel(
    reach_ref, q_ref, do_ref, trade_ref, mine_ref, other_ref, out_ref, dq_ref, back_ref, dmine_ref, dother_ref,
    rows_ref, s_ref, p_ref, top_ref, mass_ref, sum_ref, turned_ref, grad_ref, row_ref,
):
    here = lax.axis_index("ctx")
    side = lax.axis_index("head") % 2
    blocks = (2 * here, 2 * CTX - 1 - 2 * here)
    bases = [block * BLK for block in blocks]
    reaches = [reach_ref[block] * BLK for block in blocks]
    lowest = [jnp.maximum(base + 1, reach) // SPAN for base, reach in zip(bases, reaches)]
    used = [(jnp.maximum(base + BLK, reach) + SPAN - 1) // SPAN for base, reach in zip(bases, reaches)]
    common, most = jnp.minimum(used[0], used[1]), jnp.maximum(used[0], used[1])
    larger = (used[1] > used[0]).astype(jnp.int32)
    whole = pl.ds(0, ROWS)
    part = pl.ds(pl.multiple_of(larger * (ROWS // 2), ROWS // 2), ROWS // 2)
    full_both = jnp.minimum(jnp.minimum(lowest[0], lowest[1]), common)
    full_part = jnp.clip(jnp.where(larger == 1, lowest[1], lowest[0]), common, most)

    rows_ref[0 : ROWS // 2] = q_ref[0 : ROWS // 2]
    rows_ref[ROWS // 2 :] = trade_ref[0 : ROWS // 2]
    lane = lax.broadcasted_iota(jnp.int32, (8, ROWS), 1)
    second = lane >= ROWS // 2
    place = jnp.where(second, lane - ROWS // 2, lane) // OWN
    row_ref[...] = jnp.maximum(
        jnp.where(second, bases[1], bases[0]) + place + 1, jnp.where(second, reaches[1], reaches[0])
    ).astype(f32)
    top_ref[...] = jnp.full((8, ROWS), FAR_BELOW, f32)
    mass_ref[...] = jnp.zeros((8, ROWS), f32)
    sum_ref[...] = jnp.zeros((HD, ROWS), f32)

    def over_keys(step):
        def run(low, high, cols, width, masked):
            @pl.loop(low, high)
            def _(g):
                step(g, g, mine_ref, dmine_ref, side, cols, width, masked)
                step(g, PER_SOURCE + g, other_ref, dother_ref, 1 - side, cols, width, masked)

        return run

    def find_max(g, at, ref, _, half, cols, width, masked):
        scores = dot(keys_of(ref, g, 0), rows_ref[cols, :], NT)
        if masked:
            index = lax.broadcasted_iota(jnp.int32, (KEYS, 1), 0)
            where = g * SPAN + half * HALF + (index // HALF) * LB + index % HALF
            scores = jnp.where(where.astype(f32) < row_ref[0:1, cols], scores, FAR_BELOW)
        s_ref[at, :, cols] = scores
        top_ref[:, cols] = jnp.maximum(top_ref[:, cols], jnp.max(scores.reshape(KEYS // 8, 8, width), axis=0))

    run = over_keys(find_max)
    run(0, full_both, whole, ROWS, False)
    run(full_both, common, whole, ROWS, True)
    run(common, full_part, part, ROWS // 2, False)
    run(full_part, most, part, ROWS // 2, True)
    factor = SCALE_SOFT * LOG2E
    row_ref[...] = jnp.broadcast_to(jnp.max(top_ref[...], axis=0, keepdims=True) * factor, (8, ROWS))

    def weigh(g, at, ref, _, half, cols, width, masked):
        probs = jnp.exp2(s_ref[at, :, cols] * factor - row_ref[0:1, cols])
        mass_ref[:, cols] = mass_ref[:, cols] + jnp.sum(probs.reshape(KEYS // 8, 8, width), axis=0)
        probs = probs.astype(bf16)
        p_ref[at, :, cols] = probs
        sum_ref[:, cols] = sum_ref[:, cols] + dot(keys_of(ref, g, 1), probs, TN)

    run = over_keys(weigh)
    run(0, common, whole, ROWS, False)
    run(common, most, part, ROWS // 2, False)

    inverse = 1.0 / jnp.sum(mass_ref[...], axis=0, keepdims=True)
    out = (sum_ref[...] * inverse).astype(bf16)
    out_rows = out.T
    out_ref[...] = out_rows[0 : ROWS // 2]
    back_ref[0 : ROWS // 2] = out_rows[ROWS // 2 :]
    grads = jnp.concatenate(
        [do_ref[0 : ROWS // 2].astype(f32).T, trade_ref[ROWS // 2 :].astype(f32).T], axis=1
    )
    adjust = inverse * SCALE_SOFT
    row_ref[...] = jnp.broadcast_to(
        jnp.sum(grads * out.astype(f32), axis=0, keepdims=True) * adjust, (8, ROWS)
    )
    turned = (grads * adjust).astype(bf16)
    turned_ref[...] = turned
    grad_ref[...] = turned.T
    sum_ref[...] = jnp.zeros((HD, ROWS), f32)

    def pull(g, at, ref, target, half, cols, width, masked):
        probs = p_ref[at, :, cols]
        moved = dot(keys_of(ref, g, 1), turned_ref[:, cols], NN)
        pulls = (probs.astype(f32) * (moved - row_ref[0:1, cols])).astype(bf16)
        dk = dot(pulls, rows_ref[cols, :], NN)
        dv = dot(probs, grad_ref[cols, :], NN) * (1.0 / SCALE_SOFT)
        target[pl.ds(g * PIECES, PIECES), 0:HALF, :] = dk.astype(bf16).reshape(PIECES, HALF, HD)
        target[pl.ds(g * PIECES, PIECES), HALF:LB, :] = dv.astype(bf16).reshape(PIECES, HALF, HD)
        sum_ref[:, cols] = sum_ref[:, cols] + dot(keys_of(ref, g, 0), pulls, TN)

    run = over_keys(pull)
    run(0, common, whole, ROWS, False)
    run(common, most, part, ROWS // 2, False)
    dq_rows = sum_ref[...].astype(bf16).T
    dq_ref[...] = dq_rows[0 : ROWS // 2]
    back_ref[ROWS // 2 :] = dq_rows[ROWS // 2 :]

    @pl.loop(most, PER_SOURCE)
    def _(g):
        zero = jnp.zeros((PIECES, LB, HD), bf16)
        dmine_ref[pl.ds(g * PIECES, PIECES)] = zero
        dother_ref[pl.ds(g * PIECES, PIECES)] = zero


def merge_kernel(mine_ref, got_ref, back_ref, pay_ref):
    for j in range(CTX):
        pay_ref[j, 0:LB, :] = (mine_ref[j].astype(f32) + got_ref[j].astype(f32)).astype(bf16)
        pay_ref[j, LB:, :] = back_ref[j]


def reduce_kernel(got_ref, block_ref, later_ref):
    block = got_ref[0, 0:LB, :].astype(f32)
    for j in range(1, CTX):
        block = block + got_ref[j, 0:LB, :].astype(f32)
    block = block.astype(bf16)
    for z in range(KVH):
        block_ref[z] = block
    for j in range(CTX):
        later_ref[j * SLICE : (j + 1) * SLICE, :] = got_ref[j, LB:, :]


def suffix_kernel(got_ref, first_ref, out_ref):
    state = jnp.zeros((SLICE, HD), f32)
    for j in reversed(range(CTX)):
        out_ref[j] = state.astype(bf16)
        marks = first_ref[j, LB + SLICE :, :].astype(f32)
        fade = jnp.exp(marks[0:1, :] + marks[8:9, :])
        state = fade * state + got_ref[j].astype(f32)


def spread_kernel(mine_ref, other_ref, dk_ref, dv_ref, scratch):
    side = lax.axis_index("head") % 2
    for part, target in ((0, dk_ref), (1, dv_ref)):
        for z in range(KVH):
            rows = slice(part * HALF, (part + 1) * HALF)
            scratch[pl.ds(side * (HALF * KVH) + z, HALF, stride=KVH), :] = mine_ref[z, rows, :].astype(f32)
            scratch[pl.ds((1 - side) * (HALF * KVH) + z, HALF, stride=KVH), :] = other_ref[z, rows, :].astype(f32)
        target[...] = scratch[...].astype(bf16)


def call(kernel, outs, scratch=(), smem=(), hbm=(), hbm_out=(), count=0, flops=0, limit=8):
    spaces = [
        pl.BlockSpec(memory_space=pltpu.SMEM if n in smem else pl.ANY if n in hbm else pltpu.VMEM)
        for n in range(count)
    ]
    return pl.pallas_call(
        kernel,
        out_shape=[jax.ShapeDtypeStruct(shape, kind) for shape, kind in outs],
        in_specs=spaces,
        out_specs=[
            pl.BlockSpec(memory_space=pl.ANY if n in hbm_out else pltpu.VMEM) for n in range(len(outs))
        ],
        scratch_shapes=[x if not isinstance(x, tuple) else pltpu.VMEM(*x) for x in scratch],
        compiler_params=pltpu.CompilerParams(vmem_limit_bytes=limit * 1024 * 1024),
        cost_estimate=pl.CostEstimate(flops=flops, bytes_accessed=1 << 20, transcendentals=0),
    )


def after(value, *earlier):
    return lax.optimization_barrier((value,) + earlier)[0]


WIDE = ((ROWS, HD), f32)
FLAT = ((ROWS, HD), bf16)
BY_HEAD = ((OWN, LB, HD), f32)
HALF_FLAT = ((ROWS // 2, HD), bf16)
KEY_PARTS = ((CTX, LB, HD), bf16)
MIRROR = [(i, CTX - 1 - i) for i in range(CTX)]
OTHER_CORE = [(i, i ^ 1) for i in range(HEADS)]
SAME_CORE = [[2 * z + c for z in range(KVH)] for c in range(2)]


def per_device(lin_q, lin_k, lin_v, decay, lin_gain, lin_grad, soft_q, soft_k, soft_v, soft_grad, reach):
    flat = lambda x: x.reshape(-1, HD)
    lin_q, lin_k, lin_v, lin_grad, soft_q, soft_grad, soft_k, soft_v = map(
        flat, (lin_q, lin_k, lin_v, lin_grad, soft_q, soft_grad, soft_k, soft_v)
    )
    pay, within, heads, trade = call(
        local_kernel,
        [((CTX, LB + SLICE + 16, HD), bf16), BY_HEAD, ((3, OWN, LB, HD), bf16), FLAT],
        [
            WIDE,
            ((3, ROWS, HD), bf16),
            ((2, HALF * KVH, HD), bf16),
            ((OWN, LB), f32),
            ((LB, HD), bf16),
            ((CTX, SLICE + 16, HD), bf16),
            BY_HEAD,
            ((3, OWN, LB, HD), bf16),
            FLAT,
            pltpu.SemaphoreType.DMA((8,)),
            pltpu.SemaphoreType.DMA((CTX + 4,)),
        ],
        hbm=(0, 1, 2, 3, 4, 5, 6, 7),
        hbm_out=(0, 1, 2, 3),
        count=8,
        flops=10**9,
        limit=60,
    )(lin_q, lin_k, lin_v, decay, soft_k, soft_v, soft_q, soft_grad)
    trade = lax.ppermute(trade, "ctx", MIRROR)
    mine = lax.all_to_all(pay, "ctx", 0, 0)
    (prefixes,) = call(prefix_kernel, [((CTX, SLICE, HD), bf16)], count=1, flops=10**8)(mine)
    state = lax.all_to_all(prefixes, "ctx", 0, 0).reshape(OWN * HD, HD)
    attended, upstream, sums = call(
        attend_kernel,
        [BY_HEAD, BY_HEAD, ((HEADS, 4, HALF), f32)],
        [WIDE],
        count=6,
        flops=10**9,
    )(within, heads, state, decay, lin_grad, lin_gain)
    total = lax.all_to_all(after(sums, trade), "head", 0, 0)
    lin_out, att_grad, back = call(
        grad_kernel,
        [FLAT, ((OWN, LB, HD), bf16), ((OWN * HD, HD), bf16)],
        [WIDE],
        count=6,
        flops=10**10,
    )(attended, upstream, total, heads, decay, lin_gain)
    other = lax.ppermute(after(mine, back), "head", OTHER_CORE)
    backs = lax.all_to_all(back.reshape(CTX, SLICE, HD), "ctx", 0, 0)
    (suffixes,) = call(suffix_kernel, [((CTX, SLICE, HD), bf16)], count=2, flops=10**8)(backs, mine)
    own_out, own_dq, traded, dmine, dother = call(
        soft_kernel,
        [HALF_FLAT, HALF_FLAT, FLAT, KEY_PARTS, KEY_PARTS],
        [
            FLAT,
            ((GROUPS, KEYS, ROWS), f32),
            ((GROUPS, KEYS, ROWS), bf16),
            ((8, ROWS), f32),
            ((8, ROWS), f32),
            ((HD, ROWS), f32),
            ((HD, ROWS), bf16),
            FLAT,
            ((8, ROWS), f32),
        ],
        smem=(0,),
        count=6,
        flops=10**10,
        limit=36,
    )(reach, after(soft_q, suffixes), soft_grad, trade, mine, other)
    dgot = lax.ppermute(dother, "head", OTHER_CORE)
    (pay_back,) = call(merge_kernel, [((CTX, LB + SLICE, HD), bf16)], count=3, flops=10**8)(
        dmine, dgot, suffixes
    )
    traded = lax.ppermute(traded, "ctx", MIRROR)
    got_back = lax.all_to_all(pay_back, "ctx", 0, 0)
    blocks, later = call(
        reduce_kernel, [((KVH, LB, HD), bf16), ((OWN * HD, HD), bf16)], count=1, flops=10**8
    )(got_back)
    spread = lax.all_to_all(blocks, "head", 0, 0, axis_index_groups=SAME_CORE)
    lin_dq, lin_dk, lin_dv, soft_out, soft_dq = call(
        inner_kernel, [FLAT] * 5, [WIDE], count=8, flops=4 * 10**9
    )(heads, att_grad, state, later, decay, own_out, own_dq, traded)
    spread = after(spread, lin_dk)
    spread_other = lax.ppermute(spread, "head", OTHER_CORE)
    soft_dk, soft_dv = call(
        spread_kernel,
        [((LB * KVH, HD), bf16), ((LB * KVH, HD), bf16)],
        [((LB * KVH, HD), f32)],
        count=2,
        flops=10**8,
    )(spread, spread_other)
    deep = lambda x: x.reshape(LB, OWN, HD)
    return (
        deep(lin_out),
        deep(lin_dq),
        deep(lin_dk),
        deep(lin_dv),
        deep(soft_out),
        deep(soft_dq),
        soft_dk.reshape(LB, KVH, HD),
        soft_dv.reshape(LB, KVH, HD),
    )


def solution(mesh):
    long, short = P("ctx", "head", None), P("ctx", None, None)
    return jax.shard_map(
        per_device,
        mesh=mesh,
        in_specs=(long, long, long, P("head", "ctx"), P("head", None), long, long, short, short, long, P()),
        out_specs=(long, long, long, long, long, long, short, short),
        check_vma=False,
    )
```

```python
import functools
import math

import jax
import jax.numpy as jnp
from jax import lax
from jax.experimental import pallas as pl
from jax.experimental.pallas import tpu as pltpu
from jax.sharding import PartitionSpec as P

HEAD_TOTAL = 64
HD = 128
KVH = 8
LB = 256
BLK = 128
CTX = 16
HEADS = 16
OWN = 4
ROWS = LB * OWN
HALF = LB // 2
SLICE = OWN * HD // CTX
EPSILON = 1e-05
FAR_BELOW = -1e30
SCALE_LIN = 1.0 / HD
SCALE_SOFT = 1.0 / math.sqrt(HD)
LOG2E = 1.4426950408889634
KEYS = 512
PIECES = KEYS // HALF
PER_SOURCE = CTX // PIECES
GROUPS = 2 * PER_SOURCE
SPAN = PIECES * LB

f32 = jnp.float32
bf16 = jnp.bfloat16
PRECISE = lax.Precision.HIGHEST


def dot(a, b, dims, precision=None):
    return lax.dot_general(a, b, (dims, ((), ())), precision=precision, preferred_element_type=f32)


NN = ((1,), (0,))
NT = ((1,), (1,))
TN = ((0,), (0,))


def split_heads(source, scratch):
    scratch[...] = source[...].astype(f32)
    return [scratch[pl.ds(h, LB, stride=OWN), :] for h in range(OWN)]


def join_heads(parts, scratch, target):
    for h in range(OWN):
        scratch[pl.ds(h, LB, stride=OWN), :] = parts[h]
    target[...] = scratch[...].astype(bf16)


def run_sums(log_decay):
    row = lax.broadcasted_iota(jnp.int32, (LB, LB), 0)
    col = lax.broadcasted_iota(jnp.int32, (LB, LB), 1)
    upto = (row <= col).astype(f32)
    as_rows = dot(log_decay, upto, NN, PRECISE)
    as_cols = dot((row >= col).astype(f32), log_decay, NT, PRECISE)
    return as_rows, as_cols, row, col


def local_kernel(
    q_hbm, k_hbm, v_hbm, decay_hbm, sk_hbm, sv_hbm, sq_hbm, sg_hbm, pay_hbm, within_hbm, heads_hbm, trade_hbm,
    scratch, raw, halves, decay_ref, kv_ref, own_ref, within_ref, heads_ref, trade_ref, sems, out_sems,
):
    side = lax.axis_index("head") % 2
    kv = lax.axis_index("head") // 2
    half = pl.ds(pl.multiple_of(side * (HALF * KVH), HALF * KVH), HALF * KVH)
    copies = [
        pltpu.make_async_copy(sk_hbm.at[half], halves.at[0], sems.at[0]),
        pltpu.make_async_copy(sv_hbm.at[half], halves.at[1], sems.at[1]),
        pltpu.make_async_copy(k_hbm, raw.at[1], sems.at[2]),
        pltpu.make_async_copy(v_hbm, raw.at[2], sems.at[3]),
        pltpu.make_async_copy(q_hbm, raw.at[0], sems.at[4]),
        pltpu.make_async_copy(decay_hbm, decay_ref, sems.at[5]),
    ] + [
        pltpu.make_async_copy(
            x.at[pl.ds(ROWS // 2, ROWS // 2)], trade_ref.at[pl.ds(n * (ROWS // 2), ROWS // 2)], sems.at[6 + n]
        )
        for n, x in enumerate((sq_hbm, sg_hbm))
    ]
    for copy in copies:
        copy.start()
    for n in range(2):
        copies[n].wait()
        scratch[...] = halves[n].astype(f32)
        kv_ref[n * HALF : (n + 1) * HALF, :] = scratch[pl.ds(kv, HALF, stride=KVH), :].astype(bf16)
    sent = [
        pltpu.make_async_copy(kv_ref, pay_hbm.at[j, pl.ds(0, LB)], out_sems.at[j]) for j in range(CTX)
    ]
    for copy in sent:
        copy.start()
    for copy in copies[6:]:
        copy.wait()
    traded = pltpu.make_async_copy(trade_ref, trade_hbm, out_sems.at[CTX + 3])
    traded.start()
    copies[5].wait()
    as_rows, as_cols, row, col = run_sums(decay_ref[...])
    copies[2].wait()
    keys_wide = split_heads(raw.at[1], scratch)
    copies[3].wait()
    values = [x.astype(bf16) for x in split_heads(raw.at[2], scratch)]
    for h in range(OWN):
        run_col = as_cols[:, h : h + 1]
        total = as_rows[h : h + 1, LB - 1 : LB]
        heads_ref[1, h] = keys_wide[h].astype(bf16)
        heads_ref[2, h] = values[h]
        tailed = (keys_wide[h] * jnp.exp(total - run_col)).astype(bf16)
        own = dot(tailed, values[h], TN).astype(bf16)
        high = total.astype(bf16).astype(f32)
        marks = jnp.concatenate(
            [jnp.broadcast_to(high, (8, HD)), jnp.broadcast_to(total - high, (8, HD))], axis=0
        ).astype(bf16)
        for i in range(OWN):
            j = h * OWN + i
            own_ref[j, 0:SLICE, :] = own[i * SLICE : (i + 1) * SLICE]
            own_ref[j, SLICE:, :] = marks
    states = pltpu.make_async_copy(own_ref, pay_hbm.at[:, pl.ds(LB, SLICE + 16)], out_sems.at[CTX])
    states.start()
    copies[4].wait()
    queries = [x.astype(bf16) for x in split_heads(raw.at[0], scratch)]
    for h in range(OWN):
        heads_ref[0, h] = queries[h]
    kept = pltpu.make_async_copy(heads_ref, heads_hbm, out_sems.at[CTX + 1])
    kept.start()
    for h in range(OWN):
        decays = jnp.exp(jnp.where(row >= col, as_cols[:, h : h + 1] - as_rows[h : h + 1, :], FAR_BELOW))
        weights = (dot(queries[h], heads_ref[1, h], NT) * decays * SCALE_LIN).astype(bf16)
        within_ref[h] = dot(weights, values[h], NN)
    inner = pltpu.make_async_copy(within_ref, within_hbm, out_sems.at[CTX + 2])
    inner.start()
    for copy in sent + [traded, states, kept, inner]:
        copy.wait()


def prefix_kernel(got_ref, out_ref):
    state = jnp.zeros((SLICE, HD), f32)
    for j in range(CTX):
        out_ref[j] = state.astype(bf16)
        marks = got_ref[j, LB + SLICE :, :].astype(f32)
        fade = jnp.exp(marks[0:1, :] + marks[8:9, :])
        state = fade * state + got_ref[j, LB : LB + SLICE, :].astype(f32)


def attend_kernel(within_ref, heads_ref, state_ref, decay_ref, grad_ref, gain_ref, att_ref, up_ref, sums_ref, scratch):
    _, as_cols, _, _ = run_sums(decay_ref[...])
    grads = split_heads(grad_ref, scratch)
    squares = jnp.zeros((LB, HD), f32)
    crossed = jnp.zeros((LB, HD), f32)
    for h in range(OWN):
        state = state_ref[h * HD : (h + 1) * HD, :]
        fade = SCALE_LIN * jnp.exp(as_cols[:, h : h + 1])
        attended = within_ref[h] + fade * dot(heads_ref[0, h], state, NN)
        upstream = grads[h] * gain_ref[h : h + 1, :]
        att_ref[h] = attended
        up_ref[h] = upstream
        squares = squares + attended * attended
        crossed = crossed + upstream * attended
    ones = jnp.ones((8, HD), f32)
    square_row = dot(ones, squares, NT, PRECISE)
    cross_row = dot(ones, crossed, NT, PRECISE)
    both = [x[0:1, n * HALF : (n + 1) * HALF] for x in (square_row, cross_row) for n in range(2)]
    for j in range(HEADS):
        for n in range(4):
            sums_ref[j, n : n + 1, :] = both[n]


def grad_kernel(att_ref, up_ref, got_ref, heads_ref, decay_ref, gain_ref, out_ref, ag_ref, back_ref, scratch):
    _, as_cols, row, col = run_sums(decay_ref[...])
    total = got_ref[0]
    for j in range(1, HEADS):
        total = total + got_ref[j]
    wide = jnp.concatenate(
        [jnp.concatenate([total[n : n + 1], total[n + 1 : n + 2]], axis=1) for n in (0, 2)]
        + [jnp.zeros((6, LB), f32)],
        axis=0,
    )
    cols = dot((row == col).astype(f32), wide, NT, PRECISE)
    inverse = lax.rsqrt(cols[:, 0:1] / (HEAD_TOTAL * HD) + EPSILON)
    pull = inverse * inverse * inverse * (cols[:, 1:2] / (HEAD_TOTAL * HD))
    outs = []
    for h in range(OWN):
        attended = att_ref[h]
        outs.append(attended * inverse * gain_ref[h : h + 1, :])
        att_grad = (inverse * up_ref[h] - attended * pull).astype(bf16)
        ag_ref[h] = att_grad
        faded = (heads_ref[0, h].astype(f32) * jnp.exp(as_cols[:, h : h + 1])).astype(bf16)
        back = dot(faded, att_grad, TN).astype(bf16)
        back_ref[h * HD : (h + 1) * HD, :] = back
    join_heads(outs, scratch, out_ref)


def inner_kernel(
    heads_ref, ag_ref, state_ref, later_ref, decay_ref, out_ref, sdq_ref, traded_ref,
    dq_ref, dk_ref, dv_ref, soft_out_ref, soft_dq_ref, scratch,
):
    for n, (own, target) in enumerate(((out_ref, soft_out_ref), (sdq_ref, soft_dq_ref))):
        target[0 : ROWS // 2] = own[...]
        target[ROWS // 2 :] = traded_ref[n * (ROWS // 2) : (n + 1) * (ROWS // 2)]
    as_rows, as_cols, row, col = run_sums(decay_ref[...])
    query_grads, key_grads, value_grads = [], [], []
    for h in range(OWN):
        run_row, run_col = as_rows[h : h + 1, :], as_cols[:, h : h + 1]
        query, key, value, grad = heads_ref[0, h], heads_ref[1, h], heads_ref[2, h], ag_ref[h]
        decays = SCALE_LIN * jnp.exp(jnp.where(row >= col, run_col - run_row, FAR_BELOW))
        turned = SCALE_LIN * jnp.exp(jnp.where(col >= row, run_row - run_col, FAR_BELOW))
        grad_weights = (dot(grad, value, NT) * decays).astype(bf16)
        grad_turned = (dot(value, grad, NT) * turned).astype(bf16)
        weights_turned = (dot(key, query, NT) * turned).astype(bf16)
        state = state_ref[h * HD : (h + 1) * HD, :]
        later = later_ref[h * HD : (h + 1) * HD, :]
        fade = SCALE_LIN * jnp.exp(run_col)
        tail = SCALE_LIN * jnp.exp(run_row[:, LB - 1 : LB] - run_col)
        query_grads.append(dot(grad_weights, key, NN) + fade * dot(grad, state, NT))
        key_grads.append(dot(grad_turned, query, NN) + tail * dot(value, later, NT))
        value_grads.append(dot(weights_turned, grad, NN) + tail * dot(key, later, NN))
    join_heads(query_grads, scratch, dq_ref)
    join_heads(key_grads, scratch, dk_ref)
    join_heads(value_grads, scratch, dv_ref)


def keys_of(ref, g, part):
    return ref[pl.ds(g * PIECES, PIECES), part * HALF : (part + 1) * HALF, :].reshape(KEYS, HD)


def soft_kernel(
    reach_ref, q_ref, do_ref, trade_ref, mine_ref, other_ref, out_ref, dq_ref, back_ref, dmine_ref, dother_ref,
    rows_ref, s_ref, p_ref, top_ref, mass_ref, sum_ref, turned_ref, grad_ref, row_ref,
):
    here = lax.axis_index("ctx")
    side = lax.axis_index("head") % 2
    blocks = (2 * here, 2 * CTX - 1 - 2 * here)
    bases = [block * BLK for block in blocks]
    reaches = [reach_ref[block] * BLK for block in blocks]
    lowest = [jnp.maximum(base + 1, reach) // SPAN for base, reach in zip(bases, reaches)]
    used = [(jnp.maximum(base + BLK, reach) + SPAN - 1) // SPAN for base, reach in zip(bases, reaches)]
    common, most = jnp.minimum(used[0], used[1]), jnp.maximum(used[0], used[1])
    larger = (used[1] > used[0]).astype(jnp.int32)
    whole = pl.ds(0, ROWS)
    part = pl.ds(pl.multiple_of(larger * (ROWS // 2), ROWS // 2), ROWS // 2)
    full_both = jnp.minimum(jnp.minimum(lowest[0], lowest[1]), common)
    full_part = jnp.clip(jnp.where(larger == 1, lowest[1], lowest[0]), common, most)

    rows_ref[0 : ROWS // 2] = q_ref[0 : ROWS // 2]
    rows_ref[ROWS // 2 :] = trade_ref[0 : ROWS // 2]
    lane = lax.broadcasted_iota(jnp.int32, (8, ROWS), 1)
    second = lane >= ROWS // 2
    place = jnp.where(second, lane - ROWS // 2, lane) // OWN
    row_ref[...] = jnp.maximum(
        jnp.where(second, bases[1], bases[0]) + place + 1, jnp.where(second, reaches[1], reaches[0])
    ).astype(f32)
    top_ref[...] = jnp.full((8, ROWS), FAR_BELOW, f32)
    mass_ref[...] = jnp.zeros((8, ROWS), f32)
    sum_ref[...] = jnp.zeros((HD, ROWS), f32)

    def over_keys(step):
        def run(low, high, cols, width, masked):
            @pl.loop(low, high)
            def _(g):
                step(g, g, mine_ref, dmine_ref, side, cols, width, masked)
                step(g, PER_SOURCE + g, other_ref, dother_ref, 1 - side, cols, width, masked)

        return run

    def find_max(g, at, ref, _, half, cols, width, masked):
        scores = dot(keys_of(ref, g, 0), rows_ref[cols, :], NT)
        if masked:
            index = lax.broadcasted_iota(jnp.int32, (KEYS, 1), 0)
            where = g * SPAN + half * HALF + (index // HALF) * LB + index % HALF
            scores = jnp.where(where.astype(f32) < row_ref[0:1, cols], scores, FAR_BELOW)
        s_ref[at, :, cols] = scores
        top_ref[:, cols] = jnp.maximum(top_ref[:, cols], jnp.max(scores.reshape(KEYS // 8, 8, width), axis=0))

    run = over_keys(find_max)
    run(0, full_both, whole, ROWS, False)
    run(full_both, common, whole, ROWS, True)
    run(common, full_part, part, ROWS // 2, False)
    run(full_part, most, part, ROWS // 2, True)
    factor = SCALE_SOFT * LOG2E
    row_ref[...] = jnp.broadcast_to(jnp.max(top_ref[...], axis=0, keepdims=True) * factor, (8, ROWS))

    def weigh(g, at, ref, _, half, cols, width, masked):
        probs = jnp.exp2(s_ref[at, :, cols] * factor - row_ref[0:1, cols])
        mass_ref[:, cols] = mass_ref[:, cols] + jnp.sum(probs.reshape(KEYS // 8, 8, width), axis=0)
        probs = probs.astype(bf16)
        p_ref[at, :, cols] = probs
        sum_ref[:, cols] = sum_ref[:, cols] + dot(keys_of(ref, g, 1), probs, TN)

    run = over_keys(weigh)
    run(0, common, whole, ROWS, False)
    run(common, most, part, ROWS // 2, False)

    inverse = 1.0 / jnp.sum(mass_ref[...], axis=0, keepdims=True)
    out = (sum_ref[...] * inverse).astype(bf16)
    out_rows = out.T
    out_ref[...] = out_rows[0 : ROWS // 2]
    back_ref[0 : ROWS // 2] = out_rows[ROWS // 2 :]
    grads = jnp.concatenate(
        [do_ref[0 : ROWS // 2].astype(f32).T, trade_ref[ROWS // 2 :].astype(f32).T], axis=1
    )
    adjust = inverse * SCALE_SOFT
    row_ref[...] = jnp.broadcast_to(
        jnp.sum(grads * out.astype(f32), axis=0, keepdims=True) * adjust, (8, ROWS)
    )
    turned = (grads * adjust).astype(bf16)
    turned_ref[...] = turned
    grad_ref[...] = turned.T
    sum_ref[...] = jnp.zeros((HD, ROWS), f32)

    def pull(g, at, ref, target, half, cols, width, masked):
        probs = p_ref[at, :, cols]
        moved = dot(keys_of(ref, g, 1), turned_ref[:, cols], NN)
        pulls = (probs.astype(f32) * (moved - row_ref[0:1, cols])).astype(bf16)
        dk = dot(pulls, rows_ref[cols, :], NN)
        dv = dot(probs, grad_ref[cols, :], NN) * (1.0 / SCALE_SOFT)
        target[pl.ds(g * PIECES, PIECES), 0:HALF, :] = dk.astype(bf16).reshape(PIECES, HALF, HD)
        target[pl.ds(g * PIECES, PIECES), HALF:LB, :] = dv.astype(bf16).reshape(PIECES, HALF, HD)
        sum_ref[:, cols] = sum_ref[:, cols] + dot(keys_of(ref, g, 0), pulls, TN)

    run = over_keys(pull)
    run(0, common, whole, ROWS, False)
    run(common, most, part, ROWS // 2, False)
    dq_rows = sum_ref[...].astype(bf16).T
    dq_ref[...] = dq_rows[0 : ROWS // 2]
    back_ref[ROWS // 2 :] = dq_rows[ROWS // 2 :]

    @pl.loop(most, PER_SOURCE)
    def _(g):
        zero = jnp.zeros((PIECES, LB, HD), bf16)
        dmine_ref[pl.ds(g * PIECES, PIECES)] = zero
        dother_ref[pl.ds(g * PIECES, PIECES)] = zero


def merge_kernel(mine_ref, got_ref, back_ref, pay_ref):
    for j in range(CTX):
        pay_ref[j, 0:LB, :] = (mine_ref[j].astype(f32) + got_ref[j].astype(f32)).astype(bf16)
        pay_ref[j, LB:, :] = back_ref[j]


def reduce_kernel(got_ref, block_ref, later_ref):
    block = got_ref[0, 0:LB, :].astype(f32)
    for j in range(1, CTX):
        block = block + got_ref[j, 0:LB, :].astype(f32)
    block = block.astype(bf16)
    for z in range(KVH):
        block_ref[z] = block
    for j in range(CTX):
        later_ref[j * SLICE : (j + 1) * SLICE, :] = got_ref[j, LB:, :]


def suffix_kernel(got_ref, first_ref, out_ref):
    state = jnp.zeros((SLICE, HD), f32)
    for j in reversed(range(CTX)):
        out_ref[j] = state.astype(bf16)
        marks = first_ref[j, LB + SLICE :, :].astype(f32)
        fade = jnp.exp(marks[0:1, :] + marks[8:9, :])
        state = fade * state + got_ref[j].astype(f32)


def spread_kernel(mine_ref, other_ref, dk_ref, dv_ref, scratch):
    side = lax.axis_index("head") % 2
    for part, target in ((0, dk_ref), (1, dv_ref)):
        for z in range(KVH):
            rows = slice(part * HALF, (part + 1) * HALF)
            scratch[pl.ds(side * (HALF * KVH) + z, HALF, stride=KVH), :] = mine_ref[z, rows, :].astype(f32)
            scratch[pl.ds((1 - side) * (HALF * KVH) + z, HALF, stride=KVH), :] = other_ref[z, rows, :].astype(f32)
        target[...] = scratch[...].astype(bf16)


def call(kernel, outs, scratch=(), smem=(), hbm=(), hbm_out=(), count=0, flops=0, limit=8):
    spaces = [
        pl.BlockSpec(memory_space=pltpu.SMEM if n in smem else pl.ANY if n in hbm else pltpu.VMEM)
        for n in range(count)
    ]
    return pl.pallas_call(
        kernel,
        out_shape=[jax.ShapeDtypeStruct(shape, kind) for shape, kind in outs],
        in_specs=spaces,
        out_specs=[
            pl.BlockSpec(memory_space=pl.ANY if n in hbm_out else pltpu.VMEM) for n in range(len(outs))
        ],
        scratch_shapes=[x if not isinstance(x, tuple) else pltpu.VMEM(*x) for x in scratch],
        compiler_params=pltpu.CompilerParams(vmem_limit_bytes=limit * 1024 * 1024),
        cost_estimate=pl.CostEstimate(flops=flops, bytes_accessed=1 << 20, transcendentals=0),
    )


def after(value, *earlier):
    return lax.optimization_barrier((value,) + earlier)[0]


WIDE = ((ROWS, HD), f32)
FLAT = ((ROWS, HD), bf16)
BY_HEAD = ((OWN, LB, HD), f32)
HALF_FLAT = ((ROWS // 2, HD), bf16)
KEY_PARTS = ((CTX, LB, HD), bf16)
MIRROR = [(i, CTX - 1 - i) for i in range(CTX)]
OTHER_CORE = [(i, i ^ 1) for i in range(HEADS)]
SAME_CORE = [[2 * z + c for z in range(KVH)] for c in range(2)]


def per_device(lin_q, lin_k, lin_v, decay, lin_gain, lin_grad, soft_q, soft_k, soft_v, soft_grad, reach):
    flat = lambda x: x.reshape(-1, HD)
    lin_q, lin_k, lin_v, lin_grad, soft_q, soft_grad, soft_k, soft_v = map(
        flat, (lin_q, lin_k, lin_v, lin_grad, soft_q, soft_grad, soft_k, soft_v)
    )
    pay, within, heads, trade = call(
        local_kernel,
        [((CTX, LB + SLICE + 16, HD), bf16), BY_HEAD, ((3, OWN, LB, HD), bf16), FLAT],
        [
            WIDE,
            ((3, ROWS, HD), bf16),
            ((2, HALF * KVH, HD), bf16),
            ((OWN, LB), f32),
            ((LB, HD), bf16),
            ((CTX, SLICE + 16, HD), bf16),
            BY_HEAD,
            ((3, OWN, LB, HD), bf16),
            FLAT,
            pltpu.SemaphoreType.DMA((8,)),
            pltpu.SemaphoreType.DMA((CTX + 4,)),
        ],
        hbm=(0, 1, 2, 3, 4, 5, 6, 7),
        hbm_out=(0, 1, 2, 3),
        count=8,
        flops=10**9,
        limit=60,
    )(lin_q, lin_k, lin_v, decay, soft_k, soft_v, soft_q, soft_grad)
    trade = lax.ppermute(trade, "ctx", MIRROR)
    mine = lax.all_to_all(pay, "ctx", 0, 0)
    (prefixes,) = call(prefix_kernel, [((CTX, SLICE, HD), bf16)], count=1, flops=10**8)(mine)
    state = lax.all_to_all(prefixes, "ctx", 0, 0).reshape(OWN * HD, HD)
    attended, upstream, sums = call(
        attend_kernel,
        [BY_HEAD, BY_HEAD, ((HEADS, 4, HALF), f32)],
        [WIDE],
        count=6,
        flops=10**9,
    )(within, heads, state, decay, lin_grad, lin_gain)
    other = lax.ppermute(after(mine, sums, trade), "head", OTHER_CORE)
    total = lax.all_to_all(after(sums, trade), "head", 0, 0)
    lin_out, att_grad, back = call(
        grad_kernel,
        [FLAT, ((OWN, LB, HD), bf16), ((OWN * HD, HD), bf16)],
        [WIDE],
        count=6,
        flops=10**10,
    )(attended, upstream, total, heads, decay, lin_gain)
    backs = lax.all_to_all(back.reshape(CTX, SLICE, HD), "ctx", 0, 0)
    own_out, own_dq, traded, dmine, dother = call(
        soft_kernel,
        [HALF_FLAT, HALF_FLAT, FLAT, KEY_PARTS, KEY_PARTS],
        [
            FLAT,
            ((GROUPS, KEYS, ROWS), f32),
            ((GROUPS, KEYS, ROWS), bf16),
            ((8, ROWS), f32),
            ((8, ROWS), f32),
            ((HD, ROWS), f32),
            ((HD, ROWS), bf16),
            FLAT,
            ((8, ROWS), f32),
        ],
        smem=(0,),
        count=6,
        flops=10**10,
        limit=36,
    )(reach, after(soft_q, back), soft_grad, trade, mine, other)
    (suffixes,) = call(suffix_kernel, [((CTX, SLICE, HD), bf16)], count=2, flops=10**8)(after(backs, own_out), mine)
    dgot = lax.ppermute(dother, "head", OTHER_CORE)
    (pay_back,) = call(merge_kernel, [((CTX, LB + SLICE, HD), bf16)], count=3, flops=10**8)(
        dmine, dgot, suffixes
    )
    traded = lax.ppermute(traded, "ctx", MIRROR)
    got_back = lax.all_to_all(pay_back, "ctx", 0, 0)
    blocks, later = call(
        reduce_kernel, [((KVH, LB, HD), bf16), ((OWN * HD, HD), bf16)], count=1, flops=10**8
    )(got_back)
    spread = lax.all_to_all(blocks, "head", 0, 0, axis_index_groups=SAME_CORE)
    lin_dq, lin_dk, lin_dv, soft_out, soft_dq = call(
        inner_kernel, [FLAT] * 5, [WIDE], count=8, flops=4 * 10**9
    )(heads, att_grad, state, later, decay, own_out, own_dq, traded)
    spread = after(spread, lin_dk)
    spread_other = lax.ppermute(spread, "head", OTHER_CORE)
    soft_dk, soft_dv = call(
        spread_kernel,
        [((LB * KVH, HD), bf16), ((LB * KVH, HD), bf16)],
        [((LB * KVH, HD), f32)],
        count=2,
        flops=10**8,
    )(spread, spread_other)
    deep = lambda x: x.reshape(LB, OWN, HD)
    return (
        deep(lin_out),
        deep(lin_dq),
        deep(lin_dk),
        deep(lin_dv),
        deep(soft_out),
        deep(soft_dq),
        soft_dk.reshape(LB, KVH, HD),
        soft_dv.reshape(LB, KVH, HD),
    )


def solution(mesh):
    long, short = P("ctx", "head", None), P("ctx", None, None)
    return jax.shard_map(
        per_device,
        mesh=mesh,
        in_specs=(long, long, long, P("head", "ctx"), P("head", None), long, long, short, short, long, P()),
        out_specs=(long, long, long, long, long, long, short, short),
        check_vma=False,
    )
```

```python
import functools
import math

import jax
import jax.numpy as jnp
from jax import lax
from jax.experimental import pallas as pl
from jax.experimental.pallas import tpu as pltpu
from jax.sharding import PartitionSpec as P

HEAD_TOTAL = 64
HD = 128
KVH = 8
LB = 256
BLK = 128
CTX = 16
HEADS = 16
OWN = 4
ROWS = LB * OWN
HALF = LB // 2
SLICE = OWN * HD // CTX
EPSILON = 1e-05
FAR_BELOW = -1e30
SCALE_LIN = 1.0 / HD
SCALE_SOFT = 1.0 / math.sqrt(HD)
LOG2E = 1.4426950408889634
KEYS = 512
PIECES = KEYS // HALF
PER_SOURCE = CTX // PIECES
GROUPS = 2 * PER_SOURCE
SPAN = PIECES * LB

f32 = jnp.float32
bf16 = jnp.bfloat16
PRECISE = lax.Precision.HIGHEST


def dot(a, b, dims, precision=None):
    return lax.dot_general(a, b, (dims, ((), ())), precision=precision, preferred_element_type=f32)


NN = ((1,), (0,))
NT = ((1,), (1,))
TN = ((0,), (0,))


def split_heads(source, scratch):
    scratch[...] = source[...].astype(f32)
    return [scratch[pl.ds(h, LB, stride=OWN), :] for h in range(OWN)]


def join_heads(parts, scratch, target):
    for h in range(OWN):
        scratch[pl.ds(h, LB, stride=OWN), :] = parts[h]
    target[...] = scratch[...].astype(bf16)


def run_sums(log_decay):
    row = lax.broadcasted_iota(jnp.int32, (LB, LB), 0)
    col = lax.broadcasted_iota(jnp.int32, (LB, LB), 1)
    upto = (row <= col).astype(f32)
    as_rows = dot(log_decay, upto, NN, PRECISE)
    as_cols = dot((row >= col).astype(f32), log_decay, NT, PRECISE)
    return as_rows, as_cols, row, col


def local_kernel(
    k_hbm, v_hbm, decay_hbm, sk_hbm, sv_hbm, sq_hbm, sg_hbm, pay_hbm, trade_hbm,
    scratch, raw, halves, decay_ref, kv_ref, own_ref, trade_ref, sems, out_sems,
):
    side = lax.axis_index("head") % 2
    kv = lax.axis_index("head") // 2
    half = pl.ds(pl.multiple_of(side * (HALF * KVH), HALF * KVH), HALF * KVH)
    copies = [
        pltpu.make_async_copy(sk_hbm.at[half], halves.at[0], sems.at[0]),
        pltpu.make_async_copy(sv_hbm.at[half], halves.at[1], sems.at[1]),
        pltpu.make_async_copy(k_hbm, raw.at[0], sems.at[2]),
        pltpu.make_async_copy(v_hbm, raw.at[1], sems.at[3]),
        pltpu.make_async_copy(decay_hbm, decay_ref, sems.at[4]),
    ] + [
        pltpu.make_async_copy(
            x.at[pl.ds(ROWS // 2, ROWS // 2)], trade_ref.at[pl.ds(n * (ROWS // 2), ROWS // 2)], sems.at[5 + n]
        )
        for n, x in enumerate((sq_hbm, sg_hbm))
    ]
    for copy in copies:
        copy.start()
    for n in range(2):
        copies[n].wait()
        scratch[...] = halves[n].astype(f32)
        kv_ref[n * HALF : (n + 1) * HALF, :] = scratch[pl.ds(kv, HALF, stride=KVH), :].astype(bf16)
    sent = [
        pltpu.make_async_copy(kv_ref, pay_hbm.at[j, pl.ds(0, LB)], out_sems.at[j]) for j in range(CTX)
    ]
    for copy in sent:
        copy.start()
    for copy in copies[5:]:
        copy.wait()
    traded = pltpu.make_async_copy(trade_ref, trade_hbm, out_sems.at[CTX + 1])
    traded.start()
    copies[4].wait()
    as_rows, as_cols, row, col = run_sums(decay_ref[...])
    copies[2].wait()
    keys_wide = split_heads(raw.at[0], scratch)
    copies[3].wait()
    values = [x.astype(bf16) for x in split_heads(raw.at[1], scratch)]
    for h in range(OWN):
        run_col = as_cols[:, h : h + 1]
        total = as_rows[h : h + 1, LB - 1 : LB]
        tailed = (keys_wide[h] * jnp.exp(total - run_col)).astype(bf16)
        own = dot(tailed, values[h], TN).astype(bf16)
        high = total.astype(bf16).astype(f32)
        marks = jnp.concatenate(
            [jnp.broadcast_to(high, (8, HD)), jnp.broadcast_to(total - high, (8, HD))], axis=0
        ).astype(bf16)
        for i in range(OWN):
            j = h * OWN + i
            own_ref[j, 0:SLICE, :] = own[i * SLICE : (i + 1) * SLICE]
            own_ref[j, SLICE:, :] = marks
    states = pltpu.make_async_copy(own_ref, pay_hbm.at[:, pl.ds(LB, SLICE + 16)], out_sems.at[CTX])
    states.start()
    for copy in sent + [traded, states]:
        copy.wait()


def within_kernel(q_ref, k_ref, v_ref, decay_ref, within_ref, heads_ref, scratch):
    as_rows, as_cols, row, col = run_sums(decay_ref[...])
    for n, ref in enumerate((q_ref, k_ref, v_ref)):
        for h, part in enumerate(split_heads(ref, scratch)):
            heads_ref[n, h] = part.astype(bf16)
    for h in range(OWN):
        decays = jnp.exp(jnp.where(row >= col, as_cols[:, h : h + 1] - as_rows[h : h + 1, :], FAR_BELOW))
        weights = (dot(heads_ref[0, h], heads_ref[1, h], NT) * decays * SCALE_LIN).astype(bf16)
        within_ref[h] = dot(weights, heads_ref[2, h], NN)


def prefix_kernel(got_ref, out_ref):
    state = jnp.zeros((SLICE, HD), f32)
    for j in range(CTX):
        out_ref[j] = state.astype(bf16)
        marks = got_ref[j, LB + SLICE :, :].astype(f32)
        fade = jnp.exp(marks[0:1, :] + marks[8:9, :])
        state = fade * state + got_ref[j, LB : LB + SLICE, :].astype(f32)


def attend_kernel(within_ref, heads_ref, state_ref, decay_ref, grad_ref, gain_ref, att_ref, up_ref, sums_ref, scratch):
    _, as_cols, _, _ = run_sums(decay_ref[...])
    grads = split_heads(grad_ref, scratch)
    squares = jnp.zeros((LB, HD), f32)
    crossed = jnp.zeros((LB, HD), f32)
    for h in range(OWN):
        state = state_ref[h * HD : (h + 1) * HD, :]
        fade = SCALE_LIN * jnp.exp(as_cols[:, h : h + 1])
        attended = within_ref[h] + fade * dot(heads_ref[0, h], state, NN)
        upstream = grads[h] * gain_ref[h : h + 1, :]
        att_ref[h] = attended
        up_ref[h] = upstream
        squares = squares + attended * attended
        crossed = crossed + upstream * attended
    ones = jnp.ones((8, HD), f32)
    square_row = dot(ones, squares, NT, PRECISE)
    cross_row = dot(ones, crossed, NT, PRECISE)
    both = [x[0:1, n * HALF : (n + 1) * HALF] for x in (square_row, cross_row) for n in range(2)]
    for j in range(HEADS):
        for n in range(4):
            sums_ref[j, n : n + 1, :] = both[n]


def grad_kernel(att_ref, up_ref, got_ref, heads_ref, decay_ref, gain_ref, out_ref, ag_ref, back_ref, scratch):
    _, as_cols, row, col = run_sums(decay_ref[...])
    total = got_ref[0]
    for j in range(1, HEADS):
        total = total + got_ref[j]
    wide = jnp.concatenate(
        [jnp.concatenate([total[n : n + 1], total[n + 1 : n + 2]], axis=1) for n in (0, 2)]
        + [jnp.zeros((6, LB), f32)],
        axis=0,
    )
    cols = dot((row == col).astype(f32), wide, NT, PRECISE)
    inverse = lax.rsqrt(cols[:, 0:1] / (HEAD_TOTAL * HD) + EPSILON)
    pull = inverse * inverse * inverse * (cols[:, 1:2] / (HEAD_TOTAL * HD))
    outs = []
    for h in range(OWN):
        attended = att_ref[h]
        outs.append(attended * inverse * gain_ref[h : h + 1, :])
        att_grad = (inverse * up_ref[h] - attended * pull).astype(bf16)
        ag_ref[h] = att_grad
        faded = (heads_ref[0, h].astype(f32) * jnp.exp(as_cols[:, h : h + 1])).astype(bf16)
        back = dot(faded, att_grad, TN).astype(bf16)
        back_ref[h * HD : (h + 1) * HD, :] = back
    join_heads(outs, scratch, out_ref)


def inner_kernel(
    heads_ref, ag_ref, state_ref, later_ref, decay_ref, out_ref, sdq_ref, traded_ref,
    dq_ref, dk_ref, dv_ref, soft_out_ref, soft_dq_ref, scratch,
):
    for n, (own, target) in enumerate(((out_ref, soft_out_ref), (sdq_ref, soft_dq_ref))):
        target[0 : ROWS // 2] = own[...]
        target[ROWS // 2 :] = traded_ref[n * (ROWS // 2) : (n + 1) * (ROWS // 2)]
    as_rows, as_cols, row, col = run_sums(decay_ref[...])
    query_grads, key_grads, value_grads = [], [], []
    for h in range(OWN):
        run_row, run_col = as_rows[h : h + 1, :], as_cols[:, h : h + 1]
        query, key, value, grad = heads_ref[0, h], heads_ref[1, h], heads_ref[2, h], ag_ref[h]
        decays = SCALE_LIN * jnp.exp(jnp.where(row >= col, run_col - run_row, FAR_BELOW))
        turned = SCALE_LIN * jnp.exp(jnp.where(col >= row, run_row - run_col, FAR_BELOW))
        grad_weights = (dot(grad, value, NT) * decays).astype(bf16)
        grad_turned = (dot(value, grad, NT) * turned).astype(bf16)
        weights_turned = (dot(key, query, NT) * turned).astype(bf16)
        state = state_ref[h * HD : (h + 1) * HD, :]
        later = later_ref[h * HD : (h + 1) * HD, :]
        fade = SCALE_LIN * jnp.exp(run_col)
        tail = SCALE_LIN * jnp.exp(run_row[:, LB - 1 : LB] - run_col)
        query_grads.append(dot(grad_weights, key, NN) + fade * dot(grad, state, NT))
        key_grads.append(dot(grad_turned, query, NN) + tail * dot(value, later, NT))
        value_grads.append(dot(weights_turned, grad, NN) + tail * dot(key, later, NN))
    join_heads(query_grads, scratch, dq_ref)
    join_heads(key_grads, scratch, dk_ref)
    join_heads(value_grads, scratch, dv_ref)


def keys_of(ref, g, part):
    return ref[pl.ds(g * PIECES, PIECES), part * HALF : (part + 1) * HALF, :].reshape(KEYS, HD)


def soft_kernel(
    reach_ref, q_ref, do_ref, trade_ref, mine_ref, other_ref, out_ref, dq_ref, back_ref, dmine_ref, dother_ref,
    rows_ref, s_ref, p_ref, top_ref, mass_ref, sum_ref, turned_ref, grad_ref, row_ref,
):
    here = lax.axis_index("ctx")
    side = lax.axis_index("head") % 2
    blocks = (2 * here, 2 * CTX - 1 - 2 * here)
    bases = [block * BLK for block in blocks]
    reaches = [reach_ref[block] * BLK for block in blocks]
    lowest = [jnp.maximum(base + 1, reach) // SPAN for base, reach in zip(bases, reaches)]
    used = [(jnp.maximum(base + BLK, reach) + SPAN - 1) // SPAN for base, reach in zip(bases, reaches)]
    common, most = jnp.minimum(used[0], used[1]), jnp.maximum(used[0], used[1])
    larger = (used[1] > used[0]).astype(jnp.int32)
    whole = pl.ds(0, ROWS)
    part = pl.ds(pl.multiple_of(larger * (ROWS // 2), ROWS // 2), ROWS // 2)
    full_both = jnp.minimum(jnp.minimum(lowest[0], lowest[1]), common)
    full_part = jnp.clip(jnp.where(larger == 1, lowest[1], lowest[0]), common, most)

    rows_ref[0 : ROWS // 2] = q_ref[0 : ROWS // 2]
    rows_ref[ROWS // 2 :] = trade_ref[0 : ROWS // 2]
    lane = lax.broadcasted_iota(jnp.int32, (8, ROWS), 1)
    second = lane >= ROWS // 2
    place = jnp.where(second, lane - ROWS // 2, lane) // OWN
    row_ref[...] = jnp.maximum(
        jnp.where(second, bases[1], bases[0]) + place + 1, jnp.where(second, reaches[1], reaches[0])
    ).astype(f32)
    top_ref[...] = jnp.full((8, ROWS), FAR_BELOW, f32)
    mass_ref[...] = jnp.zeros((8, ROWS), f32)
    sum_ref[...] = jnp.zeros((HD, ROWS), f32)

    def over_keys(step):
        def run(low, high, cols, width, masked):
            @pl.loop(low, high)
            def _(g):
                step(g, g, mine_ref, dmine_ref, side, cols, width, masked)
                step(g, PER_SOURCE + g, other_ref, dother_ref, 1 - side, cols, width, masked)

        return run

    def find_max(g, at, ref, _, half, cols, width, masked):
        scores = dot(keys_of(ref, g, 0), rows_ref[cols, :], NT)
        if masked:
            index = lax.broadcasted_iota(jnp.int32, (KEYS, 1), 0)
            where = g * SPAN + half * HALF + (index // HALF) * LB + index % HALF
            scores = jnp.where(where.astype(f32) < row_ref[0:1, cols], scores, FAR_BELOW)
        s_ref[at, :, cols] = scores
        top_ref[:, cols] = jnp.maximum(top_ref[:, cols], jnp.max(scores.reshape(KEYS // 8, 8, width), axis=0))

    run = over_keys(find_max)
    run(0, full_both, whole, ROWS, False)
    run(full_both, common, whole, ROWS, True)
    run(common, full_part, part, ROWS // 2, False)
    run(full_part, most, part, ROWS // 2, True)
    factor = SCALE_SOFT * LOG2E
    row_ref[...] = jnp.broadcast_to(jnp.max(top_ref[...], axis=0, keepdims=True) * factor, (8, ROWS))

    def weigh(g, at, ref, _, half, cols, width, masked):
        probs = jnp.exp2(s_ref[at, :, cols] * factor - row_ref[0:1, cols])
        mass_ref[:, cols] = mass_ref[:, cols] + jnp.sum(probs.reshape(KEYS // 8, 8, width), axis=0)
        probs = probs.astype(bf16)
        p_ref[at, :, cols] = probs
        sum_ref[:, cols] = sum_ref[:, cols] + dot(keys_of(ref, g, 1), probs, TN)

    run = over_keys(weigh)
    run(0, common, whole, ROWS, False)
    run(common, most, part, ROWS // 2, False)

    inverse = 1.0 / jnp.sum(mass_ref[...], axis=0, keepdims=True)
    out = (sum_ref[...] * inverse).astype(bf16)
    out_rows = out.T
    out_ref[...] = out_rows[0 : ROWS // 2]
    back_ref[0 : ROWS // 2] = out_rows[ROWS // 2 :]
    grads = jnp.concatenate(
        [do_ref[0 : ROWS // 2].astype(f32).T, trade_ref[ROWS // 2 :].astype(f32).T], axis=1
    )
    adjust = inverse * SCALE_SOFT
    row_ref[...] = jnp.broadcast_to(
        jnp.sum(grads * out.astype(f32), axis=0, keepdims=True) * adjust, (8, ROWS)
    )
    turned = (grads * adjust).astype(bf16)
    turned_ref[...] = turned
    grad_ref[...] = turned.T
    sum_ref[...] = jnp.zeros((HD, ROWS), f32)

    def pull(g, at, ref, target, half, cols, width, masked):
        probs = p_ref[at, :, cols]
        moved = dot(keys_of(ref, g, 1), turned_ref[:, cols], NN)
        pulls = (probs.astype(f32) * (moved - row_ref[0:1, cols])).astype(bf16)
        dk = dot(pulls, rows_ref[cols, :], NN)
        dv = dot(probs, grad_ref[cols, :], NN) * (1.0 / SCALE_SOFT)
        target[pl.ds(g * PIECES, PIECES), 0:HALF, :] = dk.astype(bf16).reshape(PIECES, HALF, HD)
        target[pl.ds(g * PIECES, PIECES), HALF:LB, :] = dv.astype(bf16).reshape(PIECES, HALF, HD)
        sum_ref[:, cols] = sum_ref[:, cols] + dot(keys_of(ref, g, 0), pulls, TN)

    run = over_keys(pull)
    run(0, common, whole, ROWS, False)
    run(common, most, part, ROWS // 2, False)
    dq_rows = sum_ref[...].astype(bf16).T
    dq_ref[...] = dq_rows[0 : ROWS // 2]
    back_ref[ROWS // 2 :] = dq_rows[ROWS // 2 :]

    @pl.loop(most, PER_SOURCE)
    def _(g):
        zero = jnp.zeros((PIECES, LB, HD), bf16)
        dmine_ref[pl.ds(g * PIECES, PIECES)] = zero
        dother_ref[pl.ds(g * PIECES, PIECES)] = zero


def merge_kernel(mine_ref, got_ref, back_ref, pay_ref):
    for j in range(CTX):
        pay_ref[j, 0:LB, :] = (mine_ref[j].astype(f32) + got_ref[j].astype(f32)).astype(bf16)
        pay_ref[j, LB:, :] = back_ref[j]


def reduce_kernel(got_ref, first_ref, block_ref, out_ref):
    block = got_ref[0, 0:LB, :].astype(f32)
    for j in range(1, CTX):
        block = block + got_ref[j, 0:LB, :].astype(f32)
    block_ref[...] = block.astype(bf16)
    state = jnp.zeros((SLICE, HD), f32)
    for j in reversed(range(CTX)):
        out_ref[j] = state.astype(bf16)
        marks = first_ref[j, LB + SLICE :, :].astype(f32)
        fade = jnp.exp(marks[0:1, :] + marks[8:9, :])
        state = fade * state + got_ref[j, LB:, :].astype(f32)


def pair_kernel(own_ref, below_ref, above_ref, up_ref, down_ref):
    up_ref[0:LB] = own_ref[...]
    up_ref[LB:] = below_ref[...]
    down_ref[0:LB] = own_ref[...]
    down_ref[LB:] = above_ref[...]


def gather_kernel(own_ref, below_ref, above_ref, far_ref, up_ref, down_ref, out_ref):
    z = lax.axis_index("head") // 2
    for shift, ref, at in (
        (0, own_ref, 0), (-2, below_ref, 0), (2, above_ref, 0), (4, far_ref, 0),
        (-1, up_ref, 0), (-3, up_ref, 1), (1, down_ref, 0), (3, down_ref, 1),
    ):
        out_ref[(z + shift + KVH) % KVH] = ref[at * LB : (at + 1) * LB, :]


def spread_kernel(mine_ref, other_ref, dk_ref, dv_ref, scratch):
    side = lax.axis_index("head") % 2
    for part, target in ((0, dk_ref), (1, dv_ref)):
        for z in range(KVH):
            rows = slice(part * HALF, (part + 1) * HALF)
            scratch[pl.ds(side * (HALF * KVH) + z, HALF, stride=KVH), :] = mine_ref[z, rows, :].astype(f32)
            scratch[pl.ds((1 - side) * (HALF * KVH) + z, HALF, stride=KVH), :] = other_ref[z, rows, :].astype(f32)
        target[...] = scratch[...].astype(bf16)


def call(kernel, outs, scratch=(), smem=(), hbm=(), hbm_out=(), count=0, flops=0, limit=8):
    spaces = [
        pl.BlockSpec(memory_space=pltpu.SMEM if n in smem else pl.ANY if n in hbm else pltpu.VMEM)
        for n in range(count)
    ]
    return pl.pallas_call(
        kernel,
        out_shape=[jax.ShapeDtypeStruct(shape, kind) for shape, kind in outs],
        in_specs=spaces,
        out_specs=[
            pl.BlockSpec(memory_space=pl.ANY if n in hbm_out else pltpu.VMEM) for n in range(len(outs))
        ],
        scratch_shapes=[x if not isinstance(x, tuple) else pltpu.VMEM(*x) for x in scratch],
        compiler_params=pltpu.CompilerParams(vmem_limit_bytes=limit * 1024 * 1024),
        cost_estimate=pl.CostEstimate(flops=flops, bytes_accessed=1 << 20, transcendentals=0),
    )


def after(value, *earlier):
    return lax.optimization_barrier((value,) + earlier)[0]


WIDE = ((ROWS, HD), f32)
FLAT = ((ROWS, HD), bf16)
BY_HEAD = ((OWN, LB, HD), f32)
HALF_FLAT = ((ROWS // 2, HD), bf16)
KEY_PARTS = ((CTX, LB, HD), bf16)
MIRROR = [(i, CTX - 1 - i) for i in range(CTX)]
OTHER_CORE = [(i, i ^ 1) for i in range(HEADS)]
ALONG = {k: [(i, (i + 2 * k) % HEADS) for i in range(HEADS)] for k in (-2, -1, 1, 2, 4)}


def per_device(lin_q, lin_k, lin_v, decay, lin_gain, lin_grad, soft_q, soft_k, soft_v, soft_grad, reach):
    flat = lambda x: x.reshape(-1, HD)
    lin_q, lin_k, lin_v, lin_grad, soft_q, soft_grad, soft_k, soft_v = map(
        flat, (lin_q, lin_k, lin_v, lin_grad, soft_q, soft_grad, soft_k, soft_v)
    )
    pay, trade = call(
        local_kernel,
        [((CTX, LB + SLICE + 16, HD), bf16), FLAT],
        [
            WIDE,
            ((2, ROWS, HD), bf16),
            ((2, HALF * KVH, HD), bf16),
            ((OWN, LB), f32),
            ((LB, HD), bf16),
            ((CTX, SLICE + 16, HD), bf16),
            FLAT,
            pltpu.SemaphoreType.DMA((7,)),
            pltpu.SemaphoreType.DMA((CTX + 2,)),
        ],
        hbm=(0, 1, 2, 3, 4, 5, 6),
        hbm_out=(0, 1),
        count=7,
        flops=10**9,
        limit=60,
    )(lin_k, lin_v, decay, soft_k, soft_v, soft_q, soft_grad)
    within, heads = call(
        within_kernel, [BY_HEAD, ((3, OWN, LB, HD), bf16)], [WIDE], count=4, flops=10**9, limit=60
    )(lin_q, lin_k, lin_v, after(decay, pay))
    trade = lax.ppermute(trade, "ctx", MIRROR)
    mine = lax.all_to_all(pay, "ctx", 0, 0)
    (prefixes,) = call(prefix_kernel, [((CTX, SLICE, HD), bf16)], count=1, flops=10**8)(
        after(mine, within)
    )
    state = lax.all_to_all(prefixes, "ctx", 0, 0).reshape(OWN * HD, HD)
    attended, upstream, sums = call(
        attend_kernel,
        [BY_HEAD, BY_HEAD, ((HEADS, 4, HALF), f32)],
        [WIDE],
        count=6,
        flops=10**9,
    )(within, heads, state, decay, lin_grad, lin_gain)
    other = lax.ppermute(after(mine, sums, trade), "head", OTHER_CORE)
    total = lax.all_to_all(after(sums, trade), "head", 0, 0)
    own_out, own_dq, traded, dmine, dother = call(
        soft_kernel,
        [HALF_FLAT, HALF_FLAT, FLAT, KEY_PARTS, KEY_PARTS],
        [
            FLAT,
            ((GROUPS, KEYS, ROWS), f32),
            ((GROUPS, KEYS, ROWS), bf16),
            ((8, ROWS), f32),
            ((8, ROWS), f32),
            ((HD, ROWS), f32),
            ((HD, ROWS), bf16),
            FLAT,
            ((8, ROWS), f32),
        ],
        smem=(0,),
        count=6,
        flops=10**10,
        limit=36,
    )(reach, after(soft_q, total), soft_grad, trade, mine, other)
    dgot = lax.ppermute(dother, "head", OTHER_CORE)
    lin_out, att_grad, back = call(
        grad_kernel,
        [FLAT, ((OWN, LB, HD), bf16), ((OWN * HD, HD), bf16)],
        [WIDE],
        count=6,
        flops=2 * 10**9,
    )(attended, upstream, total, heads, decay, after(lin_gain, own_out))
    (pay_back,) = call(merge_kernel, [((CTX, LB + SLICE, HD), bf16)], count=3, flops=10**8)(
        dmine, dgot, back.reshape(CTX, SLICE, HD)
    )
    got_back = lax.all_to_all(pay_back, "ctx", 0, 0)
    block, suffixes = call(
        reduce_kernel, [((LB, HD), bf16), ((CTX, SLICE, HD), bf16)], count=2, flops=10**8
    )(got_back, mine)
    along = lambda x, k: lax.ppermute(x, "head", ALONG[k])
    below, above, far = along(block, 2), along(block, -2), along(block, 4)
    traded = lax.ppermute(after(traded, block), "ctx", MIRROR)
    later = lax.all_to_all(suffixes, "ctx", 0, 0).reshape(OWN * HD, HD)
    up, down = call(pair_kernel, [((2 * LB, HD), bf16)] * 2, count=3, flops=10**8)(block, below, after(above, later))
    up, down = along(up, 1), along(down, -1)
    lin_dq, lin_dk, lin_dv, soft_out, soft_dq = call(
        inner_kernel, [FLAT] * 5, [WIDE], count=8, flops=4 * 10**9
    )(heads, att_grad, state, later, decay, own_out, own_dq, traded)
    (spread,) = call(gather_kernel, [((KVH, LB, HD), bf16)], count=6, flops=10**8)(
        after(block, lin_dk), below, above, far, up, down
    )
    spread_other = lax.ppermute(spread, "head", OTHER_CORE)
    soft_dk, soft_dv = call(
        spread_kernel,
        [((LB * KVH, HD), bf16), ((LB * KVH, HD), bf16)],
        [((LB * KVH, HD), f32)],
        count=2,
        flops=10**8,
    )(spread, spread_other)
    deep = lambda x: x.reshape(LB, OWN, HD)
    return (
        deep(lin_out),
        deep(lin_dq),
        deep(lin_dk),
        deep(lin_dv),
        deep(soft_out),
        deep(soft_dq),
        soft_dk.reshape(LB, KVH, HD),
        soft_dv.reshape(LB, KVH, HD),
    )


def solution(mesh):
    long, short = P("ctx", "head", None), P("ctx", None, None)
    return jax.shard_map(
        per_device,
        mesh=mesh,
        in_specs=(long, long, long, P("head", "ctx"), P("head", None), long, long, short, short, long, P()),
        out_specs=(long, long, long, long, long, long, short, short),
        check_vma=False,
    )
```

```python
import functools
import math

import jax
import jax.numpy as jnp
from jax import lax
from jax.experimental import pallas as pl
from jax.experimental.pallas import tpu as pltpu
from jax.sharding import PartitionSpec as P

HEAD_TOTAL = 64
HD = 128
KVH = 8
LB = 256
BLK = 128
CTX = 16
HEADS = 16
OWN = 4
ROWS = LB * OWN
HALF = LB // 2
SLICE = OWN * HD // CTX
EPSILON = 1e-05
FAR_BELOW = -1e30
SCALE_LIN = 1.0 / HD
SCALE_SOFT = 1.0 / math.sqrt(HD)
LOG2E = 1.4426950408889634
KEYS = 512
PIECES = KEYS // HALF
PER_SOURCE = CTX // PIECES
GROUPS = 2 * PER_SOURCE
SPAN = PIECES * LB

f32 = jnp.float32
bf16 = jnp.bfloat16
PRECISE = lax.Precision.HIGHEST


def dot(a, b, dims, precision=None):
    return lax.dot_general(a, b, (dims, ((), ())), precision=precision, preferred_element_type=f32)


NN = ((1,), (0,))
NT = ((1,), (1,))
TN = ((0,), (0,))


def split_heads(source, scratch):
    scratch[...] = source[...].astype(f32)
    return [scratch[pl.ds(h, LB, stride=OWN), :] for h in range(OWN)]


def join_heads(parts, scratch, target):
    for h in range(OWN):
        scratch[pl.ds(h, LB, stride=OWN), :] = parts[h]
    target[...] = scratch[...].astype(bf16)


def run_sums(log_decay):
    row = lax.broadcasted_iota(jnp.int32, (LB, LB), 0)
    col = lax.broadcasted_iota(jnp.int32, (LB, LB), 1)
    upto = (row <= col).astype(f32)
    as_rows = dot(log_decay, upto, NN, PRECISE)
    as_cols = dot((row >= col).astype(f32), log_decay, NT, PRECISE)
    return as_rows, as_cols, row, col


def local_kernel(
    k_hbm, v_hbm, decay_hbm, sk_hbm, sv_hbm, sq_hbm, sg_hbm, pay_hbm, trade_hbm,
    scratch, raw, halves, decay_ref, kv_ref, own_ref, trade_ref, sems, out_sems,
):
    side = lax.axis_index("head") % 2
    kv = lax.axis_index("head") // 2
    half = pl.ds(pl.multiple_of(side * (HALF * KVH), HALF * KVH), HALF * KVH)
    copies = [
        pltpu.make_async_copy(sk_hbm.at[half], halves.at[0], sems.at[0]),
        pltpu.make_async_copy(sv_hbm.at[half], halves.at[1], sems.at[1]),
        pltpu.make_async_copy(k_hbm, raw.at[0], sems.at[2]),
        pltpu.make_async_copy(v_hbm, raw.at[1], sems.at[3]),
        pltpu.make_async_copy(decay_hbm, decay_ref, sems.at[4]),
    ] + [
        pltpu.make_async_copy(
            x.at[pl.ds(ROWS // 2, ROWS // 2)], trade_ref.at[pl.ds(n * (ROWS // 2), ROWS // 2)], sems.at[5 + n]
        )
        for n, x in enumerate((sq_hbm, sg_hbm))
    ]
    for copy in copies:
        copy.start()
    for n in range(2):
        copies[n].wait()
        scratch[...] = halves[n].astype(f32)
        kv_ref[n * HALF : (n + 1) * HALF, :] = scratch[pl.ds(kv, HALF, stride=KVH), :].astype(bf16)
    sent = [
        pltpu.make_async_copy(kv_ref, pay_hbm.at[j, pl.ds(0, LB)], out_sems.at[j]) for j in range(CTX)
    ]
    for copy in sent:
        copy.start()
    for copy in copies[5:]:
        copy.wait()
    traded = pltpu.make_async_copy(trade_ref, trade_hbm, out_sems.at[CTX + 1])
    traded.start()
    copies[4].wait()
    as_rows, as_cols, row, col = run_sums(decay_ref[...])
    copies[2].wait()
    keys_wide = split_heads(raw.at[0], scratch)
    copies[3].wait()
    values = [x.astype(bf16) for x in split_heads(raw.at[1], scratch)]
    for h in range(OWN):
        run_col = as_cols[:, h : h + 1]
        total = as_rows[h : h + 1, LB - 1 : LB]
        tailed = (keys_wide[h] * jnp.exp(total - run_col)).astype(bf16)
        own = dot(tailed, values[h], TN).astype(bf16)
        high = total.astype(bf16).astype(f32)
        marks = jnp.concatenate(
            [jnp.broadcast_to(high, (8, HD)), jnp.broadcast_to(total - high, (8, HD))], axis=0
        ).astype(bf16)
        for i in range(OWN):
            j = h * OWN + i
            own_ref[j, 0:SLICE, :] = own[i * SLICE : (i + 1) * SLICE]
            own_ref[j, SLICE:, :] = marks
    states = pltpu.make_async_copy(own_ref, pay_hbm.at[:, pl.ds(LB, SLICE + 16)], out_sems.at[CTX])
    states.start()
    for copy in sent + [traded, states]:
        copy.wait()


def within_kernel(q_ref, k_ref, v_ref, decay_ref, within_ref, heads_ref, scratch):
    as_rows, as_cols, row, col = run_sums(decay_ref[...])
    for n, ref in enumerate((q_ref, k_ref, v_ref)):
        for h, part in enumerate(split_heads(ref, scratch)):
            heads_ref[n, h] = part.astype(bf16)
    for h in range(OWN):
        decays = jnp.exp(jnp.where(row >= col, as_cols[:, h : h + 1] - as_rows[h : h + 1, :], FAR_BELOW))
        weights = (dot(heads_ref[0, h], heads_ref[1, h], NT) * decays * SCALE_LIN).astype(bf16)
        within_ref[h] = dot(weights, heads_ref[2, h], NN)


def prefix_kernel(got_ref, out_ref):
    state = jnp.zeros((SLICE, HD), f32)
    for j in range(CTX):
        out_ref[j] = state.astype(bf16)
        marks = got_ref[j, LB + SLICE :, :].astype(f32)
        fade = jnp.exp(marks[0:1, :] + marks[8:9, :])
        state = fade * state + got_ref[j, LB : LB + SLICE, :].astype(f32)


def attend_kernel(within_ref, heads_ref, state_ref, decay_ref, grad_ref, gain_ref, att_ref, up_ref, sums_ref, scratch):
    _, as_cols, _, _ = run_sums(decay_ref[...])
    grads = split_heads(grad_ref, scratch)
    squares = jnp.zeros((LB, HD), f32)
    crossed = jnp.zeros((LB, HD), f32)
    for h in range(OWN):
        state = state_ref[h * HD : (h + 1) * HD, :]
        fade = SCALE_LIN * jnp.exp(as_cols[:, h : h + 1])
        attended = within_ref[h] + fade * dot(heads_ref[0, h], state, NN)
        upstream = grads[h] * gain_ref[h : h + 1, :]
        att_ref[h] = attended
        up_ref[h] = upstream
        squares = squares + attended * attended
        crossed = crossed + upstream * attended
    ones = jnp.ones((8, HD), f32)
    square_row = dot(ones, squares, NT, PRECISE)
    cross_row = dot(ones, crossed, NT, PRECISE)
    both = [x[0:1, n * HALF : (n + 1) * HALF] for x in (square_row, cross_row) for n in range(2)]
    for j in range(HEADS):
        for n in range(4):
            sums_ref[j, n : n + 1, :] = both[n]


def grad_kernel(att_ref, up_ref, got_ref, heads_ref, decay_ref, gain_ref, out_ref, ag_ref, back_ref, scratch):
    _, as_cols, row, col = run_sums(decay_ref[...])
    total = got_ref[0]
    for j in range(1, HEADS):
        total = total + got_ref[j]
    wide = jnp.concatenate(
        [jnp.concatenate([total[n : n + 1], total[n + 1 : n + 2]], axis=1) for n in (0, 2)]
        + [jnp.zeros((6, LB), f32)],
        axis=0,
    )
    cols = dot((row == col).astype(f32), wide, NT, PRECISE)
    inverse = lax.rsqrt(cols[:, 0:1] / (HEAD_TOTAL * HD) + EPSILON)
    pull = inverse * inverse * inverse * (cols[:, 1:2] / (HEAD_TOTAL * HD))
    outs = []
    for h in range(OWN):
        attended = att_ref[h]
        outs.append(attended * inverse * gain_ref[h : h + 1, :])
        att_grad = (inverse * up_ref[h] - attended * pull).astype(bf16)
        ag_ref[h] = att_grad
        faded = (heads_ref[0, h].astype(f32) * jnp.exp(as_cols[:, h : h + 1])).astype(bf16)
        back = dot(faded, att_grad, TN).astype(bf16)
        back_ref[h * HD : (h + 1) * HD, :] = back
    join_heads(outs, scratch, out_ref)


def inner_kernel(
    heads_ref, ag_ref, state_ref, later_ref, decay_ref, dq_ref, dk_ref, dv_ref, scratch
):
    as_rows, as_cols, row, col = run_sums(decay_ref[...])
    query_grads, key_grads, value_grads = [], [], []
    for h in range(OWN):
        run_row, run_col = as_rows[h : h + 1, :], as_cols[:, h : h + 1]
        query, key, value, grad = heads_ref[0, h], heads_ref[1, h], heads_ref[2, h], ag_ref[h]
        decays = SCALE_LIN * jnp.exp(jnp.where(row >= col, run_col - run_row, FAR_BELOW))
        turned = SCALE_LIN * jnp.exp(jnp.where(col >= row, run_row - run_col, FAR_BELOW))
        grad_weights = (dot(grad, value, NT) * decays).astype(bf16)
        grad_turned = (dot(value, grad, NT) * turned).astype(bf16)
        weights_turned = (dot(key, query, NT) * turned).astype(bf16)
        state = state_ref[h * HD : (h + 1) * HD, :]
        later = later_ref[h * HD : (h + 1) * HD, :]
        fade = SCALE_LIN * jnp.exp(run_col)
        tail = SCALE_LIN * jnp.exp(run_row[:, LB - 1 : LB] - run_col)
        query_grads.append(dot(grad_weights, key, NN) + fade * dot(grad, state, NT))
        key_grads.append(dot(grad_turned, query, NN) + tail * dot(value, later, NT))
        value_grads.append(dot(weights_turned, grad, NN) + tail * dot(key, later, NN))
    join_heads(query_grads, scratch, dq_ref)
    join_heads(key_grads, scratch, dk_ref)
    join_heads(value_grads, scratch, dv_ref)


def keys_of(ref, g, part):
    return ref[pl.ds(g * PIECES, PIECES), part * HALF : (part + 1) * HALF, :].reshape(KEYS, HD)


def soft_kernel(
    reach_ref, q_ref, do_ref, trade_ref, mine_ref, other_ref, out_ref, dq_ref, back_ref, dmine_ref, dother_ref,
    rows_ref, s_ref, p_ref, top_ref, mass_ref, sum_ref, turned_ref, grad_ref, row_ref,
):
    here = lax.axis_index("ctx")
    side = lax.axis_index("head") % 2
    blocks = (2 * here, 2 * CTX - 1 - 2 * here)
    bases = [block * BLK for block in blocks]
    reaches = [reach_ref[block] * BLK for block in blocks]
    lowest = [jnp.maximum(base + 1, reach) // SPAN for base, reach in zip(bases, reaches)]
    used = [(jnp.maximum(base + BLK, reach) + SPAN - 1) // SPAN for base, reach in zip(bases, reaches)]
    common, most = jnp.minimum(used[0], used[1]), jnp.maximum(used[0], used[1])
    larger = (used[1] > used[0]).astype(jnp.int32)
    whole = pl.ds(0, ROWS)
    part = pl.ds(pl.multiple_of(larger * (ROWS // 2), ROWS // 2), ROWS // 2)
    full_both = jnp.minimum(jnp.minimum(lowest[0], lowest[1]), common)
    full_part = jnp.clip(jnp.where(larger == 1, lowest[1], lowest[0]), common, most)

    rows_ref[0 : ROWS // 2] = q_ref[0 : ROWS // 2]
    rows_ref[ROWS // 2 :] = trade_ref[0 : ROWS // 2]
    lane = lax.broadcasted_iota(jnp.int32, (8, ROWS), 1)
    second = lane >= ROWS // 2
    place = jnp.where(second, lane - ROWS // 2, lane) // OWN
    row_ref[...] = jnp.maximum(
        jnp.where(second, bases[1], bases[0]) + place + 1, jnp.where(second, reaches[1], reaches[0])
    ).astype(f32)
    top_ref[...] = jnp.full((8, ROWS), FAR_BELOW, f32)
    mass_ref[...] = jnp.zeros((8, ROWS), f32)
    sum_ref[...] = jnp.zeros((HD, ROWS), f32)

    def over_keys(step):
        def run(low, high, cols, width, masked):
            @pl.loop(low, high)
            def _(g):
                step(g, g, mine_ref, dmine_ref, side, cols, width, masked)
                step(g, PER_SOURCE + g, other_ref, dother_ref, 1 - side, cols, width, masked)

        return run

    def find_max(g, at, ref, _, half, cols, width, masked):
        scores = dot(keys_of(ref, g, 0), rows_ref[cols, :], NT)
        if masked:
            index = lax.broadcasted_iota(jnp.int32, (KEYS, 1), 0)
            where = g * SPAN + half * HALF + (index // HALF) * LB + index % HALF
            scores = jnp.where(where.astype(f32) < row_ref[0:1, cols], scores, FAR_BELOW)
        s_ref[at, :, cols] = scores
        top_ref[:, cols] = jnp.maximum(top_ref[:, cols], jnp.max(scores.reshape(KEYS // 8, 8, width), axis=0))

    run = over_keys(find_max)
    run(0, full_both, whole, ROWS, False)
    run(full_both, common, whole, ROWS, True)
    run(common, full_part, part, ROWS // 2, False)
    run(full_part, most, part, ROWS // 2, True)
    factor = SCALE_SOFT * LOG2E
    row_ref[...] = jnp.broadcast_to(jnp.max(top_ref[...], axis=0, keepdims=True) * factor, (8, ROWS))

    def weigh(g, at, ref, _, half, cols, width, masked):
        probs = jnp.exp2(s_ref[at, :, cols] * factor - row_ref[0:1, cols])
        mass_ref[:, cols] = mass_ref[:, cols] + jnp.sum(probs.reshape(KEYS // 8, 8, width), axis=0)
        probs = probs.astype(bf16)
        p_ref[at, :, cols] = probs
        sum_ref[:, cols] = sum_ref[:, cols] + dot(keys_of(ref, g, 1), probs, TN)

    run = over_keys(weigh)
    run(0, common, whole, ROWS, False)
    run(common, most, part, ROWS // 2, False)

    inverse = 1.0 / jnp.sum(mass_ref[...], axis=0, keepdims=True)
    out = (sum_ref[...] * inverse).astype(bf16)
    out_rows = out.T
    out_ref[...] = out_rows[0 : ROWS // 2]
    back_ref[0 : ROWS // 2] = out_rows[ROWS // 2 :]
    grads = jnp.concatenate(
        [do_ref[0 : ROWS // 2].astype(f32).T, trade_ref[ROWS // 2 :].astype(f32).T], axis=1
    )
    adjust = inverse * SCALE_SOFT
    row_ref[...] = jnp.broadcast_to(
        jnp.sum(grads * out.astype(f32), axis=0, keepdims=True) * adjust, (8, ROWS)
    )
    turned = (grads * adjust).astype(bf16)
    turned_ref[...] = turned
    grad_ref[...] = turned.T
    sum_ref[...] = jnp.zeros((HD, ROWS), f32)

    def pull(g, at, ref, target, half, cols, width, masked):
        probs = p_ref[at, :, cols]
        moved = dot(keys_of(ref, g, 1), turned_ref[:, cols], NN)
        pulls = (probs.astype(f32) * (moved - row_ref[0:1, cols])).astype(bf16)
        dk = dot(pulls, rows_ref[cols, :], NN)
        dv = dot(probs, grad_ref[cols, :], NN) * (1.0 / SCALE_SOFT)
        target[pl.ds(g * PIECES, PIECES), 0:HALF, :] = dk.astype(bf16).reshape(PIECES, HALF, HD)
        target[pl.ds(g * PIECES, PIECES), HALF:LB, :] = dv.astype(bf16).reshape(PIECES, HALF, HD)
        sum_ref[:, cols] = sum_ref[:, cols] + dot(keys_of(ref, g, 0), pulls, TN)

    run = over_keys(pull)
    run(0, common, whole, ROWS, False)
    run(common, most, part, ROWS // 2, False)
    dq_rows = sum_ref[...].astype(bf16).T
    dq_ref[...] = dq_rows[0 : ROWS // 2]
    back_ref[ROWS // 2 :] = dq_rows[ROWS // 2 :]

    @pl.loop(most, PER_SOURCE)
    def _(g):
        zero = jnp.zeros((PIECES, LB, HD), bf16)
        dmine_ref[pl.ds(g * PIECES, PIECES)] = zero
        dother_ref[pl.ds(g * PIECES, PIECES)] = zero


def merge_kernel(mine_ref, got_ref, back_ref, pay_ref):
    for j in range(CTX):
        pay_ref[j, 0:LB, :] = (mine_ref[j].astype(f32) + got_ref[j].astype(f32)).astype(bf16)
        pay_ref[j, LB:, :] = back_ref[j]


def reduce_kernel(got_ref, first_ref, block_ref, out_ref):
    block = got_ref[0, 0:LB, :].astype(f32)
    for j in range(1, CTX):
        block = block + got_ref[j, 0:LB, :].astype(f32)
    block_ref[...] = block.astype(bf16)
    state = jnp.zeros((SLICE, HD), f32)
    for j in reversed(range(CTX)):
        out_ref[j] = state.astype(bf16)
        marks = first_ref[j, LB + SLICE :, :].astype(f32)
        fade = jnp.exp(marks[0:1, :] + marks[8:9, :])
        state = fade * state + got_ref[j, LB:, :].astype(f32)


def pair_kernel(own_ref, below_ref, above_ref, up_ref, down_ref):
    up_ref[0:LB] = own_ref[...]
    up_ref[LB:] = below_ref[...]
    down_ref[0:LB] = own_ref[...]
    down_ref[LB:] = above_ref[...]


def gather_kernel(own_ref, below_ref, above_ref, far_ref, up_ref, down_ref, out_ref):
    z = lax.axis_index("head") // 2
    for shift, ref, at in (
        (0, own_ref, 0), (-2, below_ref, 0), (2, above_ref, 0), (4, far_ref, 0),
        (-1, up_ref, 0), (-3, up_ref, 1), (1, down_ref, 0), (3, down_ref, 1),
    ):
        out_ref[(z + shift + KVH) % KVH] = ref[at * LB : (at + 1) * LB, :]


def fill_rows(source_ref, scratch):
    filled = []
    for part in range(2):
        for z in range(KVH):
            rows = source_ref[z, part * HALF : (part + 1) * HALF, :]
            scratch[pl.ds(z, HALF, stride=KVH), :] = rows.astype(f32)
        filled.append(scratch[...].astype(bf16))
    return filled


def near_kernel(mine_ref, rows_ref, scratch):
    for part, rows in enumerate(fill_rows(mine_ref, scratch)):
        rows_ref[part] = rows


def spread_kernel(
    near_ref, other_ref, out_ref, sdq_ref, traded_ref, dk_ref, dv_ref, soft_out_ref, soft_dq_ref, scratch
):
    side = lax.axis_index("head") % 2
    here = pl.ds(pl.multiple_of(side * (HALF * KVH), HALF * KVH), HALF * KVH)
    there = pl.ds(pl.multiple_of((1 - side) * (HALF * KVH), HALF * KVH), HALF * KVH)
    for n, (own, target) in enumerate(((out_ref, soft_out_ref), (sdq_ref, soft_dq_ref))):
        target[0 : ROWS // 2] = own[...]
        target[ROWS // 2 :] = traded_ref[n * (ROWS // 2) : (n + 1) * (ROWS // 2)]
    for part, rows in enumerate(fill_rows(other_ref, scratch)):
        target = (dk_ref, dv_ref)[part]
        target[here, :] = near_ref[part]
        target[there, :] = rows


def call(kernel, outs, scratch=(), smem=(), hbm=(), hbm_out=(), count=0, flops=0, limit=8):
    spaces = [
        pl.BlockSpec(memory_space=pltpu.SMEM if n in smem else pl.ANY if n in hbm else pltpu.VMEM)
        for n in range(count)
    ]
    return pl.pallas_call(
        kernel,
        out_shape=[jax.ShapeDtypeStruct(shape, kind) for shape, kind in outs],
        in_specs=spaces,
        out_specs=[
            pl.BlockSpec(memory_space=pl.ANY if n in hbm_out else pltpu.VMEM) for n in range(len(outs))
        ],
        scratch_shapes=[x if not isinstance(x, tuple) else pltpu.VMEM(*x) for x in scratch],
        compiler_params=pltpu.CompilerParams(vmem_limit_bytes=limit * 1024 * 1024),
        cost_estimate=pl.CostEstimate(flops=flops, bytes_accessed=1 << 20, transcendentals=0),
    )


def after(value, *earlier):
    return lax.optimization_barrier((value,) + earlier)[0]


WIDE = ((ROWS, HD), f32)
FLAT = ((ROWS, HD), bf16)
BY_HEAD = ((OWN, LB, HD), f32)
HALF_FLAT = ((ROWS // 2, HD), bf16)
KEY_PARTS = ((CTX, LB, HD), bf16)
MIRROR = [(i, CTX - 1 - i) for i in range(CTX)]
OTHER_CORE = [(i, i ^ 1) for i in range(HEADS)]
ALONG = {k: [(i, (i + 2 * k) % HEADS) for i in range(HEADS)] for k in (-2, -1, 1, 2, 4)}


def per_device(lin_q, lin_k, lin_v, decay, lin_gain, lin_grad, soft_q, soft_k, soft_v, soft_grad, reach):
    flat = lambda x: x.reshape(-1, HD)
    lin_q, lin_k, lin_v, lin_grad, soft_q, soft_grad, soft_k, soft_v = map(
        flat, (lin_q, lin_k, lin_v, lin_grad, soft_q, soft_grad, soft_k, soft_v)
    )
    pay, trade = call(
        local_kernel,
        [((CTX, LB + SLICE + 16, HD), bf16), FLAT],
        [
            WIDE,
            ((2, ROWS, HD), bf16),
            ((2, HALF * KVH, HD), bf16),
            ((OWN, LB), f32),
            ((LB, HD), bf16),
            ((CTX, SLICE + 16, HD), bf16),
            FLAT,
            pltpu.SemaphoreType.DMA((7,)),
            pltpu.SemaphoreType.DMA((CTX + 2,)),
        ],
        hbm=(0, 1, 2, 3, 4, 5, 6),
        hbm_out=(0, 1),
        count=7,
        flops=10**9,
        limit=60,
    )(lin_k, lin_v, decay, soft_k, soft_v, soft_q, soft_grad)
    within, heads = call(
        within_kernel, [BY_HEAD, ((3, OWN, LB, HD), bf16)], [WIDE], count=4, flops=10**9, limit=60
    )(lin_q, lin_k, lin_v, after(decay, pay))
    trade = lax.ppermute(trade, "ctx", MIRROR)
    mine = lax.all_to_all(pay, "ctx", 0, 0)
    (prefixes,) = call(prefix_kernel, [((CTX, SLICE, HD), bf16)], count=1, flops=10**8)(
        after(mine, within)
    )
    state = lax.all_to_all(prefixes, "ctx", 0, 0).reshape(OWN * HD, HD)
    attended, upstream, sums = call(
        attend_kernel,
        [BY_HEAD, BY_HEAD, ((HEADS, 4, HALF), f32)],
        [WIDE],
        count=6,
        flops=10**9,
    )(within, heads, state, decay, lin_grad, lin_gain)
    other = lax.ppermute(after(mine, sums, trade), "head", OTHER_CORE)
    total = lax.all_to_all(after(sums, trade), "head", 0, 0)
    own_out, own_dq, traded, dmine, dother = call(
        soft_kernel,
        [HALF_FLAT, HALF_FLAT, FLAT, KEY_PARTS, KEY_PARTS],
        [
            FLAT,
            ((GROUPS, KEYS, ROWS), f32),
            ((GROUPS, KEYS, ROWS), bf16),
            ((8, ROWS), f32),
            ((8, ROWS), f32),
            ((HD, ROWS), f32),
            ((HD, ROWS), bf16),
            FLAT,
            ((8, ROWS), f32),
        ],
        smem=(0,),
        count=6,
        flops=10**10,
        limit=36,
    )(reach, after(soft_q, total), soft_grad, trade, mine, other)
    dgot = lax.ppermute(dother, "head", OTHER_CORE)
    lin_out, att_grad, back = call(
        grad_kernel,
        [FLAT, ((OWN, LB, HD), bf16), ((OWN * HD, HD), bf16)],
        [WIDE],
        count=6,
        flops=2 * 10**9,
    )(attended, upstream, total, heads, decay, after(lin_gain, own_out))
    (pay_back,) = call(merge_kernel, [((CTX, LB + SLICE, HD), bf16)], count=3, flops=10**8)(
        dmine, dgot, back.reshape(CTX, SLICE, HD)
    )
    got_back = lax.all_to_all(pay_back, "ctx", 0, 0)
    block, suffixes = call(
        reduce_kernel, [((LB, HD), bf16), ((CTX, SLICE, HD), bf16)], count=2, flops=10**8
    )(got_back, mine)
    along = lambda x, k: lax.ppermute(x, "head", ALONG[k])
    below, above, far = along(block, 2), along(block, -2), along(block, 4)
    later = lax.all_to_all(suffixes, "ctx", 0, 0).reshape(OWN * HD, HD)
    up, down = call(pair_kernel, [((2 * LB, HD), bf16)] * 2, count=3, flops=10**8)(block, below, after(above, later))
    up, down = along(up, 1), along(down, -1)
    traded = lax.ppermute(after(traded, block), "ctx", MIRROR)
    lin_dq, lin_dk, lin_dv = call(inner_kernel, [FLAT] * 3, [WIDE], count=5, flops=4 * 10**9)(
        heads, att_grad, state, later, decay
    )
    (spread,) = call(gather_kernel, [((KVH, LB, HD), bf16)], count=6, flops=10**8)(
        after(block, lin_dk, traded), below, above, far, up, down
    )
    spread_other = lax.ppermute(spread, "head", OTHER_CORE)
    (near,) = call(
        near_kernel,
        [((2, HALF * KVH, HD), bf16)],
        [((HALF * KVH, HD), f32)],
        count=1,
        flops=10**8,
    )(spread)
    soft_dk, soft_dv, soft_out, soft_dq = call(
        spread_kernel,
        [((LB * KVH, HD), bf16), ((LB * KVH, HD), bf16), FLAT, FLAT],
        [((HALF * KVH, HD), f32)],
        count=5,
        flops=10**8,
    )(near, spread_other, own_out, own_dq, traded)
    deep = lambda x: x.reshape(LB, OWN, HD)
    return (
        deep(lin_out),
        deep(lin_dq),
        deep(lin_dk),
        deep(lin_dv),
        deep(soft_out),
        deep(soft_dq),
        soft_dk.reshape(LB, KVH, HD),
        soft_dv.reshape(LB, KVH, HD),
    )


def solution(mesh):
    long, short = P("ctx", "head", None), P("ctx", None, None)
    return jax.shard_map(
        per_device,
        mesh=mesh,
        in_specs=(long, long, long, P("head", "ctx"), P("head", None), long, long, short, short, long, P()),
        out_specs=(long, long, long, long, long, long, short, short),
        check_vma=False,
    )
```

```python
import functools
import math

import jax
import jax.numpy as jnp
from jax import lax
from jax.experimental import pallas as pl
from jax.experimental.pallas import tpu as pltpu
from jax.sharding import PartitionSpec as P

HEAD_TOTAL = 64
HD = 128
KVH = 8
LB = 256
BLK = 128
CTX = 16
HEADS = 16
OWN = 4
ROWS = LB * OWN
HALF = LB // 2
SLICE = OWN * HD // CTX
EPSILON = 1e-05
FAR_BELOW = -1e30
SCALE_LIN = 1.0 / HD
SCALE_SOFT = 1.0 / math.sqrt(HD)
LOG2E = 1.4426950408889634
KEYS = 512
PIECES = KEYS // HALF
PER_SOURCE = CTX // PIECES
GROUPS = 2 * PER_SOURCE
SPAN = PIECES * LB

f32 = jnp.float32
bf16 = jnp.bfloat16
PRECISE = lax.Precision.HIGHEST


def dot(a, b, dims, precision=None):
    return lax.dot_general(a, b, (dims, ((), ())), precision=precision, preferred_element_type=f32)


NN = ((1,), (0,))
NT = ((1,), (1,))
TN = ((0,), (0,))


def split_heads(source, scratch):
    scratch[...] = source[...].astype(f32)
    return [scratch[pl.ds(h, LB, stride=OWN), :] for h in range(OWN)]


def join_heads(parts, scratch, target):
    for h in range(OWN):
        scratch[pl.ds(h, LB, stride=OWN), :] = parts[h]
    target[...] = scratch[...].astype(bf16)


def to_columns(rows):
    return jnp.concatenate([rows, jnp.zeros((HD - rows.shape[0], LB), f32)], axis=0).T


def run_sums(log_decay):
    row = lax.broadcasted_iota(jnp.int32, (LB, LB), 0)
    col = lax.broadcasted_iota(jnp.int32, (LB, LB), 1)
    upto = (row <= col).astype(f32)
    as_rows = dot(log_decay, upto, NN, PRECISE)
    return as_rows, to_columns(as_rows), row, col


def local_kernel(
    k_hbm, v_hbm, decay_hbm, sk_hbm, sv_hbm, sq_hbm, sg_hbm, pay_hbm, trade_hbm,
    scratch, raw, halves, decay_ref, kv_ref, own_ref, trade_ref, sems, out_sems,
):
    side = lax.axis_index("head") % 2
    kv = lax.axis_index("head") // 2
    half = pl.ds(pl.multiple_of(side * (HALF * KVH), HALF * KVH), HALF * KVH)
    copies = [
        pltpu.make_async_copy(sk_hbm.at[half], halves.at[0], sems.at[0]),
        pltpu.make_async_copy(sv_hbm.at[half], halves.at[1], sems.at[1]),
        pltpu.make_async_copy(k_hbm, raw.at[0], sems.at[2]),
        pltpu.make_async_copy(v_hbm, raw.at[1], sems.at[3]),
        pltpu.make_async_copy(decay_hbm, decay_ref, sems.at[4]),
    ] + [
        pltpu.make_async_copy(
            x.at[pl.ds(ROWS // 2, ROWS // 2)], trade_ref.at[pl.ds(n * (ROWS // 2), ROWS // 2)], sems.at[5 + n]
        )
        for n, x in enumerate((sq_hbm, sg_hbm))
    ]
    for copy in copies:
        copy.start()
    for n in range(2):
        copies[n].wait()
        scratch[...] = halves[n].astype(f32)
        kv_ref[n * HALF : (n + 1) * HALF, :] = scratch[pl.ds(kv, HALF, stride=KVH), :].astype(bf16)
    sent = [
        pltpu.make_async_copy(kv_ref, pay_hbm.at[j, pl.ds(0, LB)], out_sems.at[j]) for j in range(CTX)
    ]
    for copy in sent:
        copy.start()
    for copy in copies[5:]:
        copy.wait()
    traded = pltpu.make_async_copy(trade_ref, trade_hbm, out_sems.at[CTX + 1])
    traded.start()
    copies[4].wait()
    as_rows, as_cols, row, col = run_sums(decay_ref[...])
    copies[2].wait()
    keys_wide = split_heads(raw.at[0], scratch)
    copies[3].wait()
    values = [x.astype(bf16) for x in split_heads(raw.at[1], scratch)]
    for h in range(OWN):
        run_col = as_cols[:, h : h + 1]
        total = as_rows[h : h + 1, LB - 1 : LB]
        tailed = (keys_wide[h] * jnp.exp(total - run_col)).astype(bf16)
        own = dot(tailed, values[h], TN).astype(bf16)
        high = total.astype(bf16).astype(f32)
        marks = jnp.concatenate(
            [jnp.broadcast_to(high, (8, HD)), jnp.broadcast_to(total - high, (8, HD))], axis=0
        ).astype(bf16)
        for i in range(OWN):
            j = h * OWN + i
            own_ref[j, 0:SLICE, :] = own[i * SLICE : (i + 1) * SLICE]
            own_ref[j, SLICE:, :] = marks
    states = pltpu.make_async_copy(own_ref, pay_hbm.at[:, pl.ds(LB, SLICE + 16)], out_sems.at[CTX])
    states.start()
    for copy in sent + [traded, states]:
        copy.wait()


def within_kernel(q_ref, k_ref, v_ref, decay_ref, within_ref, heads_ref, scratch):
    as_rows, as_cols, row, col = run_sums(decay_ref[...])
    for n, ref in enumerate((q_ref, k_ref, v_ref)):
        for h, part in enumerate(split_heads(ref, scratch)):
            heads_ref[n, h] = part.astype(bf16)
    for h in range(OWN):
        decays = jnp.exp(jnp.where(row >= col, as_cols[:, h : h + 1] - as_rows[h : h + 1, :], FAR_BELOW))
        weights = (dot(heads_ref[0, h], heads_ref[1, h], NT) * decays * SCALE_LIN).astype(bf16)
        within_ref[h] = dot(weights, heads_ref[2, h], NN)


def prefix_kernel(got_ref, out_ref):
    state = jnp.zeros((SLICE, HD), f32)
    for j in range(CTX):
        out_ref[j] = state.astype(bf16)
        marks = got_ref[j, LB + SLICE :, :].astype(f32)
        fade = jnp.exp(marks[0:1, :] + marks[8:9, :])
        state = fade * state + got_ref[j, LB : LB + SLICE, :].astype(f32)


def attend_kernel(within_ref, heads_ref, state_ref, decay_ref, grad_ref, gain_ref, att_ref, up_ref, sums_ref, scratch):
    _, as_cols, _, _ = run_sums(decay_ref[...])
    grads = split_heads(grad_ref, scratch)
    squares = jnp.zeros((LB, HD), f32)
    crossed = jnp.zeros((LB, HD), f32)
    for h in range(OWN):
        state = state_ref[h * HD : (h + 1) * HD, :]
        fade = SCALE_LIN * jnp.exp(as_cols[:, h : h + 1])
        attended = within_ref[h] + fade * dot(heads_ref[0, h], state, NN)
        upstream = grads[h] * gain_ref[h : h + 1, :]
        att_ref[h] = attended
        up_ref[h] = upstream
        squares = squares + attended * attended
        crossed = crossed + upstream * attended
    ones = jnp.ones((8, HD), f32)
    square_row = dot(ones, squares, NT, PRECISE)
    cross_row = dot(ones, crossed, NT, PRECISE)
    both = [x[0:1, n * HALF : (n + 1) * HALF] for x in (square_row, cross_row) for n in range(2)]
    for j in range(HEADS):
        for n in range(4):
            sums_ref[j, n : n + 1, :] = both[n]


def grad_kernel(att_ref, up_ref, got_ref, heads_ref, decay_ref, gain_ref, out_ref, ag_ref, back_ref, scratch):
    _, as_cols, row, col = run_sums(decay_ref[...])
    total = got_ref[0]
    for j in range(1, HEADS):
        total = total + got_ref[j]
    wide = jnp.concatenate(
        [jnp.concatenate([total[n : n + 1], total[n + 1 : n + 2]], axis=1) for n in (0, 2)], axis=0
    )
    cols = to_columns(wide)
    inverse = lax.rsqrt(cols[:, 0:1] / (HEAD_TOTAL * HD) + EPSILON)
    pull = inverse * inverse * inverse * (cols[:, 1:2] / (HEAD_TOTAL * HD))
    outs = []
    for h in range(OWN):
        attended = att_ref[h]
        outs.append(attended * inverse * gain_ref[h : h + 1, :])
        att_grad = (inverse * up_ref[h] - attended * pull).astype(bf16)
        ag_ref[h] = att_grad
        faded = (heads_ref[0, h].astype(f32) * jnp.exp(as_cols[:, h : h + 1])).astype(bf16)
        back = dot(faded, att_grad, TN).astype(bf16)
        back_ref[h * HD : (h + 1) * HD, :] = back
    join_heads(outs, scratch, out_ref)


def inner_kernel(
    heads_ref, ag_ref, state_ref, later_ref, decay_ref, dq_ref, dk_ref, dv_ref, scratch
):
    as_rows, as_cols, row, col = run_sums(decay_ref[...])
    query_grads, key_grads, value_grads = [], [], []
    for h in range(OWN):
        run_row, run_col = as_rows[h : h + 1, :], as_cols[:, h : h + 1]
        query, key, value, grad = heads_ref[0, h], heads_ref[1, h], heads_ref[2, h], ag_ref[h]
        decays = SCALE_LIN * jnp.exp(jnp.where(row >= col, run_col - run_row, FAR_BELOW))
        turned = SCALE_LIN * jnp.exp(jnp.where(col >= row, run_row - run_col, FAR_BELOW))
        grad_weights = (dot(grad, value, NT) * decays).astype(bf16)
        grad_turned = (dot(value, grad, NT) * turned).astype(bf16)
        weights_turned = (dot(key, query, NT) * turned).astype(bf16)
        state = state_ref[h * HD : (h + 1) * HD, :]
        later = later_ref[h * HD : (h + 1) * HD, :]
        fade = SCALE_LIN * jnp.exp(run_col)
        tail = SCALE_LIN * jnp.exp(run_row[:, LB - 1 : LB] - run_col)
        query_grads.append(dot(grad_weights, key, NN) + fade * dot(grad, state, NT))
        key_grads.append(dot(grad_turned, query, NN) + tail * dot(value, later, NT))
        value_grads.append(dot(weights_turned, grad, NN) + tail * dot(key, later, NN))
    join_heads(query_grads, scratch, dq_ref)
    join_heads(key_grads, scratch, dk_ref)
    join_heads(value_grads, scratch, dv_ref)


def keys_of(ref, g, part):
    return ref[pl.ds(g * PIECES, PIECES), part * HALF : (part + 1) * HALF, :].reshape(KEYS, HD)


def soft_kernel(
    reach_ref, q_ref, do_ref, trade_ref, mine_ref, other_ref, out_ref, dq_ref, back_ref, dmine_ref, dother_ref,
    rows_ref, s_ref, p_ref, top_ref, mass_ref, sum_ref, turned_ref, grad_ref, row_ref,
):
    here = lax.axis_index("ctx")
    side = lax.axis_index("head") % 2
    blocks = (2 * here, 2 * CTX - 1 - 2 * here)
    bases = [block * BLK for block in blocks]
    reaches = [reach_ref[block] * BLK for block in blocks]
    lowest = [jnp.maximum(base + 1, reach) // SPAN for base, reach in zip(bases, reaches)]
    used = [(jnp.maximum(base + BLK, reach) + SPAN - 1) // SPAN for base, reach in zip(bases, reaches)]
    common, most = jnp.minimum(used[0], used[1]), jnp.maximum(used[0], used[1])
    larger = (used[1] > used[0]).astype(jnp.int32)
    whole = pl.ds(0, ROWS)
    part = pl.ds(pl.multiple_of(larger * (ROWS // 2), ROWS // 2), ROWS // 2)
    full_both = jnp.minimum(jnp.minimum(lowest[0], lowest[1]), common)
    full_part = jnp.clip(jnp.where(larger == 1, lowest[1], lowest[0]), common, most)

    rows_ref[0 : ROWS // 2] = q_ref[0 : ROWS // 2]
    rows_ref[ROWS // 2 :] = trade_ref[0 : ROWS // 2]
    lane = lax.broadcasted_iota(jnp.int32, (8, ROWS), 1)
    second = lane >= ROWS // 2
    place = jnp.where(second, lane - ROWS // 2, lane) // OWN
    row_ref[...] = jnp.maximum(
        jnp.where(second, bases[1], bases[0]) + place + 1, jnp.where(second, reaches[1], reaches[0])
    ).astype(f32)
    top_ref[...] = jnp.full((8, ROWS), FAR_BELOW, f32)
    mass_ref[...] = jnp.zeros((8, ROWS), f32)
    sum_ref[...] = jnp.zeros((HD, ROWS), f32)

    def over_keys(step):
        def run(low, high, cols, width, masked):
            @pl.loop(low, high)
            def _(g):
                step(g, g, mine_ref, dmine_ref, side, cols, width, masked)
                step(g, PER_SOURCE + g, other_ref, dother_ref, 1 - side, cols, width, masked)

        return run

    def find_max(g, at, ref, _, half, cols, width, masked):
        scores = dot(keys_of(ref, g, 0), rows_ref[cols, :], NT)
        if masked:
            index = lax.broadcasted_iota(jnp.int32, (KEYS, 1), 0)
            where = g * SPAN + half * HALF + (index // HALF) * LB + index % HALF
            scores = jnp.where(where.astype(f32) < row_ref[0:1, cols], scores, FAR_BELOW)
        s_ref[at, :, cols] = scores
        top_ref[:, cols] = jnp.maximum(top_ref[:, cols], jnp.max(scores.reshape(KEYS // 8, 8, width), axis=0))

    run = over_keys(find_max)
    run(0, full_both, whole, ROWS, False)
    run(full_both, common, whole, ROWS, True)
    run(common, full_part, part, ROWS // 2, False)
    run(full_part, most, part, ROWS // 2, True)
    factor = SCALE_SOFT * LOG2E
    row_ref[...] = jnp.broadcast_to(jnp.max(top_ref[...], axis=0, keepdims=True) * factor, (8, ROWS))

    def weigh(g, at, ref, _, half, cols, width, masked):
        probs = jnp.exp2(s_ref[at, :, cols] * factor - row_ref[0:1, cols])
        mass_ref[:, cols] = mass_ref[:, cols] + jnp.sum(probs.reshape(KEYS // 8, 8, width), axis=0)
        probs = probs.astype(bf16)
        p_ref[at, :, cols] = probs
        sum_ref[:, cols] = sum_ref[:, cols] + dot(keys_of(ref, g, 1), probs, TN)

    run = over_keys(weigh)
    run(0, common, whole, ROWS, False)
    run(common, most, part, ROWS // 2, False)

    inverse = 1.0 / jnp.sum(mass_ref[...], axis=0, keepdims=True)
    out = (sum_ref[...] * inverse).astype(bf16)
    out_rows = out.T
    out_ref[...] = out_rows[0 : ROWS // 2]
    back_ref[0 : ROWS // 2] = out_rows[ROWS // 2 :]
    grads = jnp.concatenate(
        [do_ref[0 : ROWS // 2].astype(f32).T, trade_ref[ROWS // 2 :].astype(f32).T], axis=1
    )
    adjust = inverse * SCALE_SOFT
    row_ref[...] = jnp.broadcast_to(
        jnp.sum(grads * out.astype(f32), axis=0, keepdims=True) * adjust, (8, ROWS)
    )
    turned = (grads * adjust).astype(bf16)
    turned_ref[...] = turned
    grad_ref[...] = turned.T
    sum_ref[...] = jnp.zeros((HD, ROWS), f32)

    def pull(g, at, ref, target, half, cols, width, masked):
        probs = p_ref[at, :, cols]
        moved = dot(keys_of(ref, g, 1), turned_ref[:, cols], NN)
        pulls = (probs.astype(f32) * (moved - row_ref[0:1, cols])).astype(bf16)
        dk = dot(pulls, rows_ref[cols, :], NN)
        dv = dot(probs, grad_ref[cols, :], NN) * (1.0 / SCALE_SOFT)
        target[pl.ds(g * PIECES, PIECES), 0:HALF, :] = dk.astype(bf16).reshape(PIECES, HALF, HD)
        target[pl.ds(g * PIECES, PIECES), HALF:LB, :] = dv.astype(bf16).reshape(PIECES, HALF, HD)
        sum_ref[:, cols] = sum_ref[:, cols] + dot(keys_of(ref, g, 0), pulls, TN)

    run = over_keys(pull)
    run(0, common, whole, ROWS, False)
    run(common, most, part, ROWS // 2, False)
    dq_rows = sum_ref[...].astype(bf16).T
    dq_ref[...] = dq_rows[0 : ROWS // 2]
    back_ref[ROWS // 2 :] = dq_rows[ROWS // 2 :]

    @pl.loop(most, PER_SOURCE)
    def _(g):
        zero = jnp.zeros((PIECES, LB, HD), bf16)
        dmine_ref[pl.ds(g * PIECES, PIECES)] = zero
        dother_ref[pl.ds(g * PIECES, PIECES)] = zero


def merge_kernel(mine_ref, got_ref, back_ref, pay_ref):
    for j in range(CTX):
        pay_ref[j, 0:LB, :] = (mine_ref[j].astype(f32) + got_ref[j].astype(f32)).astype(bf16)
        pay_ref[j, LB:, :] = back_ref[j]


def reduce_kernel(got_ref, first_ref, block_ref, out_ref):
    block = got_ref[0, 0:LB, :].astype(f32)
    for j in range(1, CTX):
        block = block + got_ref[j, 0:LB, :].astype(f32)
    block_ref[...] = block.astype(bf16)
    state = jnp.zeros((SLICE, HD), f32)
    for j in reversed(range(CTX)):
        out_ref[j] = state.astype(bf16)
        marks = first_ref[j, LB + SLICE :, :].astype(f32)
        fade = jnp.exp(marks[0:1, :] + marks[8:9, :])
        state = fade * state + got_ref[j, LB:, :].astype(f32)


def pair_kernel(own_ref, below_ref, above_ref, up_ref, down_ref):
    up_ref[0:LB] = own_ref[...]
    up_ref[LB:] = below_ref[...]
    down_ref[0:LB] = own_ref[...]
    down_ref[LB:] = above_ref[...]


def gather_kernel(own_ref, below_ref, above_ref, far_ref, up_ref, down_ref, out_ref):
    z = lax.axis_index("head") // 2
    for shift, ref, at in (
        (0, own_ref, 0), (-2, below_ref, 0), (2, above_ref, 0), (4, far_ref, 0),
        (-1, up_ref, 0), (-3, up_ref, 1), (1, down_ref, 0), (3, down_ref, 1),
    ):
        out_ref[(z + shift + KVH) % KVH] = ref[at * LB : (at + 1) * LB, :]


def fill_rows(source_ref, scratch):
    filled = []
    for part in range(2):
        for z in range(KVH):
            rows = source_ref[z, part * HALF : (part + 1) * HALF, :]
            scratch[pl.ds(z, HALF, stride=KVH), :] = rows.astype(f32)
        filled.append(scratch[...].astype(bf16))
    return filled


def near_kernel(mine_ref, out_ref, sdq_ref, traded_ref, rows_ref, soft_out_ref, soft_dq_ref, scratch):
    for n, (own, target) in enumerate(((out_ref, soft_out_ref), (sdq_ref, soft_dq_ref))):
        target[0 : ROWS // 2] = own[...]
        target[ROWS // 2 :] = traded_ref[n * (ROWS // 2) : (n + 1) * (ROWS // 2)]
    for part, rows in enumerate(fill_rows(mine_ref, scratch)):
        rows_ref[part] = rows


def spread_kernel(near_ref, other_ref, dk_ref, dv_ref, scratch):
    side = lax.axis_index("head") % 2
    here = pl.ds(pl.multiple_of(side * (HALF * KVH), HALF * KVH), HALF * KVH)
    there = pl.ds(pl.multiple_of((1 - side) * (HALF * KVH), HALF * KVH), HALF * KVH)
    for part, rows in enumerate(fill_rows(other_ref, scratch)):
        target = (dk_ref, dv_ref)[part]
        target[here, :] = near_ref[part]
        target[there, :] = rows


def call(kernel, outs, scratch=(), smem=(), hbm=(), hbm_out=(), count=0, flops=0, limit=8):
    spaces = [
        pl.BlockSpec(memory_space=pltpu.SMEM if n in smem else pl.ANY if n in hbm else pltpu.VMEM)
        for n in range(count)
    ]
    return pl.pallas_call(
        kernel,
        out_shape=[jax.ShapeDtypeStruct(shape, kind) for shape, kind in outs],
        in_specs=spaces,
        out_specs=[
            pl.BlockSpec(memory_space=pl.ANY if n in hbm_out else pltpu.VMEM) for n in range(len(outs))
        ],
        scratch_shapes=[x if not isinstance(x, tuple) else pltpu.VMEM(*x) for x in scratch],
        compiler_params=pltpu.CompilerParams(vmem_limit_bytes=limit * 1024 * 1024),
        cost_estimate=pl.CostEstimate(flops=flops, bytes_accessed=1 << 20, transcendentals=0),
    )


def after(value, *earlier):
    return lax.optimization_barrier((value,) + earlier)[0]


WIDE = ((ROWS, HD), f32)
FLAT = ((ROWS, HD), bf16)
BY_HEAD = ((OWN, LB, HD), f32)
HALF_FLAT = ((ROWS // 2, HD), bf16)
KEY_PARTS = ((CTX, LB, HD), bf16)
MIRROR = [(i, CTX - 1 - i) for i in range(CTX)]
OTHER_CORE = [(i, i ^ 1) for i in range(HEADS)]
ALONG = {k: [(i, (i + 2 * k) % HEADS) for i in range(HEADS)] for k in (-2, -1, 1, 2, 4)}


def per_device(lin_q, lin_k, lin_v, decay, lin_gain, lin_grad, soft_q, soft_k, soft_v, soft_grad, reach):
    flat = lambda x: x.reshape(-1, HD)
    lin_q, lin_k, lin_v, lin_grad, soft_q, soft_grad, soft_k, soft_v = map(
        flat, (lin_q, lin_k, lin_v, lin_grad, soft_q, soft_grad, soft_k, soft_v)
    )
    pay, trade = call(
        local_kernel,
        [((CTX, LB + SLICE + 16, HD), bf16), FLAT],
        [
            WIDE,
            ((2, ROWS, HD), bf16),
            ((2, HALF * KVH, HD), bf16),
            ((OWN, LB), f32),
            ((LB, HD), bf16),
            ((CTX, SLICE + 16, HD), bf16),
            FLAT,
            pltpu.SemaphoreType.DMA((7,)),
            pltpu.SemaphoreType.DMA((CTX + 2,)),
        ],
        hbm=(0, 1, 2, 3, 4, 5, 6),
        hbm_out=(0, 1),
        count=7,
        flops=10**9,
        limit=60,
    )(lin_k, lin_v, decay, soft_k, soft_v, soft_q, soft_grad)
    within, heads = call(
        within_kernel, [BY_HEAD, ((3, OWN, LB, HD), bf16)], [WIDE], count=4, flops=10**9, limit=60
    )(lin_q, lin_k, lin_v, after(decay, pay))
    trade = lax.ppermute(trade, "ctx", MIRROR)
    mine = lax.all_to_all(pay, "ctx", 0, 0)
    (prefixes,) = call(prefix_kernel, [((CTX, SLICE, HD), bf16)], count=1, flops=10**8)(
        after(mine, within)
    )
    state = lax.all_to_all(prefixes, "ctx", 0, 0).reshape(OWN * HD, HD)
    attended, upstream, sums = call(
        attend_kernel,
        [BY_HEAD, BY_HEAD, ((HEADS, 4, HALF), f32)],
        [WIDE],
        count=6,
        flops=10**9,
    )(within, heads, state, decay, lin_grad, lin_gain)
    other = lax.ppermute(after(mine, sums, trade), "head", OTHER_CORE)
    total = lax.all_to_all(after(sums, trade), "head", 0, 0)
    own_out, own_dq, traded, dmine, dother = call(
        soft_kernel,
        [HALF_FLAT, HALF_FLAT, FLAT, KEY_PARTS, KEY_PARTS],
        [
            FLAT,
            ((GROUPS, KEYS, ROWS), f32),
            ((GROUPS, KEYS, ROWS), bf16),
            ((8, ROWS), f32),
            ((8, ROWS), f32),
            ((HD, ROWS), f32),
            ((HD, ROWS), bf16),
            FLAT,
            ((8, ROWS), f32),
        ],
        smem=(0,),
        count=6,
        flops=10**10,
        limit=36,
    )(reach, after(soft_q, total), soft_grad, trade, mine, other)
    dgot = lax.ppermute(dother, "head", OTHER_CORE)
    lin_out, att_grad, back = call(
        grad_kernel,
        [FLAT, ((OWN, LB, HD), bf16), ((OWN * HD, HD), bf16)],
        [WIDE],
        count=6,
        flops=2 * 10**9,
    )(attended, upstream, total, heads, decay, after(lin_gain, own_out))
    (pay_back,) = call(merge_kernel, [((CTX, LB + SLICE, HD), bf16)], count=3, flops=10**8)(
        dmine, dgot, back.reshape(CTX, SLICE, HD)
    )
    got_back = lax.all_to_all(pay_back, "ctx", 0, 0)
    block, suffixes = call(
        reduce_kernel, [((LB, HD), bf16), ((CTX, SLICE, HD), bf16)], count=2, flops=10**8
    )(got_back, mine)
    along = lambda x, k: lax.ppermute(x, "head", ALONG[k])
    below, above, far = along(block, 2), along(block, -2), along(block, 4)
    later = lax.all_to_all(suffixes, "ctx", 0, 0).reshape(OWN * HD, HD)
    up, down = call(pair_kernel, [((2 * LB, HD), bf16)] * 2, count=3, flops=10**8)(block, below, after(above, later))
    up, down = along(up, 1), along(down, -1)
    traded = lax.ppermute(after(traded, block), "ctx", MIRROR)
    lin_dq, lin_dk, lin_dv = call(inner_kernel, [FLAT] * 3, [WIDE], count=5, flops=4 * 10**9)(
        heads, att_grad, state, later, decay
    )
    (spread,) = call(gather_kernel, [((KVH, LB, HD), bf16)], count=6, flops=10**8)(
        after(block, lin_dk, traded), below, above, far, up, down
    )
    spread_other = lax.ppermute(spread, "head", OTHER_CORE)
    near, soft_out, soft_dq = call(
        near_kernel,
        [((2, HALF * KVH, HD), bf16), FLAT, FLAT],
        [((HALF * KVH, HD), f32)],
        count=4,
        flops=10**8,
    )(spread, own_out, own_dq, traded)
    soft_dk, soft_dv = call(
        spread_kernel,
        [((LB * KVH, HD), bf16), ((LB * KVH, HD), bf16)],
        [((HALF * KVH, HD), f32)],
        count=2,
        flops=10**8,
    )(near, spread_other)
    deep = lambda x: x.reshape(LB, OWN, HD)
    return (
        deep(lin_out),
        deep(lin_dq),
        deep(lin_dk),
        deep(lin_dv),
        deep(soft_out),
        deep(soft_dq),
        soft_dk.reshape(LB, KVH, HD),
        soft_dv.reshape(LB, KVH, HD),
    )


def solution(mesh):
    long, short = P("ctx", "head", None), P("ctx", None, None)
    return jax.shard_map(
        per_device,
        mesh=mesh,
        in_specs=(long, long, long, P("head", "ctx"), P("head", None), long, long, short, short, long, P()),
        out_specs=(long, long, long, long, long, long, short, short),
        check_vma=False,
    )
```

```python
import functools
import math

import jax
import jax.numpy as jnp
from jax import lax
from jax.experimental import pallas as pl
from jax.experimental.pallas import tpu as pltpu
from jax.sharding import PartitionSpec as P

HEAD_TOTAL = 64
HD = 128
KVH = 8
LB = 256
BLK = 128
CTX = 16
HEADS = 16
OWN = 4
ROWS = LB * OWN
HALF = LB // 2
SLICE = OWN * HD // CTX
EPSILON = 1e-05
FAR_BELOW = -1e30
SCALE_LIN = 1.0 / HD
SCALE_SOFT = 1.0 / math.sqrt(HD)
LOG2E = 1.4426950408889634
KEYS = 512
PIECES = KEYS // HALF
PER_SOURCE = CTX // PIECES
GROUPS = 2 * PER_SOURCE
SPAN = PIECES * LB

f32 = jnp.float32
bf16 = jnp.bfloat16
PRECISE = lax.Precision.HIGHEST


def dot(a, b, dims, precision=None):
    return lax.dot_general(a, b, (dims, ((), ())), precision=precision, preferred_element_type=f32)


NN = ((1,), (0,))
NT = ((1,), (1,))
TN = ((0,), (0,))


def split_heads(source, scratch):
    scratch[...] = source[...].astype(f32)
    return [scratch[pl.ds(h, LB, stride=OWN), :] for h in range(OWN)]


def join_heads(parts, scratch, target):
    for h in range(OWN):
        scratch[pl.ds(h, LB, stride=OWN), :] = parts[h]
    target[...] = scratch[...].astype(bf16)


def to_columns(rows):
    return jnp.concatenate([rows, jnp.zeros((HD - rows.shape[0], LB), f32)], axis=0).T


def run_sums(log_decay):
    row = lax.broadcasted_iota(jnp.int32, (LB, LB), 0)
    col = lax.broadcasted_iota(jnp.int32, (LB, LB), 1)
    upto = (row <= col).astype(f32)
    as_rows = dot(log_decay, upto, NN, PRECISE)
    return as_rows, to_columns(as_rows), row, col


def local_kernel(
    k_hbm, v_hbm, decay_hbm, sk_hbm, sv_hbm, sq_hbm, sg_hbm, pay_hbm, trade_hbm,
    scratch, raw, halves, decay_ref, kv_ref, own_ref, trade_ref, sems, out_sems,
):
    side = lax.axis_index("head") % 2
    kv = lax.axis_index("head") // 2
    half = pl.ds(pl.multiple_of(side * (HALF * KVH), HALF * KVH), HALF * KVH)
    copies = [
        pltpu.make_async_copy(sk_hbm.at[half], halves.at[0], sems.at[0]),
        pltpu.make_async_copy(sv_hbm.at[half], halves.at[1], sems.at[1]),
        pltpu.make_async_copy(k_hbm, raw.at[0], sems.at[2]),
        pltpu.make_async_copy(v_hbm, raw.at[1], sems.at[3]),
        pltpu.make_async_copy(decay_hbm, decay_ref, sems.at[4]),
    ] + [
        pltpu.make_async_copy(
            x.at[pl.ds(ROWS // 2, ROWS // 2)], trade_ref.at[pl.ds(n * (ROWS // 2), ROWS // 2)], sems.at[5 + n]
        )
        for n, x in enumerate((sq_hbm, sg_hbm))
    ]
    for copy in copies:
        copy.start()
    for n in range(2):
        copies[n].wait()
        scratch[...] = halves[n].astype(f32)
        kv_ref[n * HALF : (n + 1) * HALF, :] = scratch[pl.ds(kv, HALF, stride=KVH), :].astype(bf16)
    sent = [
        pltpu.make_async_copy(kv_ref, pay_hbm.at[j, pl.ds(0, LB)], out_sems.at[j]) for j in range(CTX)
    ]
    for copy in sent:
        copy.start()
    for copy in copies[5:]:
        copy.wait()
    traded = pltpu.make_async_copy(trade_ref, trade_hbm, out_sems.at[CTX + 1])
    traded.start()
    copies[4].wait()
    as_rows, as_cols, row, col = run_sums(decay_ref[...])
    copies[2].wait()
    keys_wide = split_heads(raw.at[0], scratch)
    copies[3].wait()
    values = [x.astype(bf16) for x in split_heads(raw.at[1], scratch)]
    for h in range(OWN):
        run_col = as_cols[:, h : h + 1]
        total = as_rows[h : h + 1, LB - 1 : LB]
        tailed = (keys_wide[h] * jnp.exp(total - run_col)).astype(bf16)
        own = dot(tailed, values[h], TN).astype(bf16)
        high = total.astype(bf16).astype(f32)
        marks = jnp.concatenate(
            [jnp.broadcast_to(high, (8, HD)), jnp.broadcast_to(total - high, (8, HD))], axis=0
        ).astype(bf16)
        for i in range(OWN):
            j = h * OWN + i
            own_ref[j, 0:SLICE, :] = own[i * SLICE : (i + 1) * SLICE]
            own_ref[j, SLICE:, :] = marks
    states = pltpu.make_async_copy(own_ref, pay_hbm.at[:, pl.ds(LB, SLICE + 16)], out_sems.at[CTX])
    states.start()
    for copy in sent + [traded, states]:
        copy.wait()


def within_kernel(q_ref, k_ref, v_ref, decay_ref, within_ref, heads_ref, scratch):
    as_rows, as_cols, row, col = run_sums(decay_ref[...])
    for n, ref in enumerate((q_ref, k_ref, v_ref)):
        for h, part in enumerate(split_heads(ref, scratch)):
            heads_ref[n, h] = part.astype(bf16)
    for h in range(OWN):
        decays = jnp.exp(jnp.where(row >= col, as_cols[:, h : h + 1] - as_rows[h : h + 1, :], FAR_BELOW))
        weights = (dot(heads_ref[0, h], heads_ref[1, h], NT) * decays * SCALE_LIN).astype(bf16)
        within_ref[h] = dot(weights, heads_ref[2, h], NN)


def prefix_kernel(got_ref, out_ref):
    state = jnp.zeros((SLICE, HD), f32)
    for j in range(CTX):
        out_ref[j] = state.astype(bf16)
        marks = got_ref[j, LB + SLICE :, :].astype(f32)
        fade = jnp.exp(marks[0:1, :] + marks[8:9, :])
        state = fade * state + got_ref[j, LB : LB + SLICE, :].astype(f32)


def attend_kernel(within_ref, heads_ref, state_ref, decay_ref, grad_ref, gain_ref, att_ref, up_ref, sums_ref, scratch):
    _, as_cols, _, _ = run_sums(decay_ref[...])
    grads = split_heads(grad_ref, scratch)
    squares = jnp.zeros((LB, HD), f32)
    crossed = jnp.zeros((LB, HD), f32)
    for h in range(OWN):
        state = state_ref[h * HD : (h + 1) * HD, :]
        fade = SCALE_LIN * jnp.exp(as_cols[:, h : h + 1])
        attended = within_ref[h] + fade * dot(heads_ref[0, h], state, NN)
        upstream = grads[h] * gain_ref[h : h + 1, :]
        att_ref[h] = attended
        up_ref[h] = upstream
        squares = squares + attended * attended
        crossed = crossed + upstream * attended
    ones = jnp.ones((8, HD), f32)
    square_row = dot(ones, squares, NT, PRECISE)
    cross_row = dot(ones, crossed, NT, PRECISE)
    both = [x[0:1, n * HALF : (n + 1) * HALF] for x in (square_row, cross_row) for n in range(2)]
    for j in range(HEADS):
        for n in range(4):
            sums_ref[j, n : n + 1, :] = both[n]


def grad_kernel(att_ref, up_ref, got_ref, heads_ref, decay_ref, gain_ref, out_ref, ag_ref, back_ref, scratch):
    _, as_cols, row, col = run_sums(decay_ref[...])
    total = got_ref[0]
    for j in range(1, HEADS):
        total = total + got_ref[j]
    wide = jnp.concatenate(
        [jnp.concatenate([total[n : n + 1], total[n + 1 : n + 2]], axis=1) for n in (0, 2)], axis=0
    )
    cols = to_columns(wide)
    inverse = lax.rsqrt(cols[:, 0:1] / (HEAD_TOTAL * HD) + EPSILON)
    pull = inverse * inverse * inverse * (cols[:, 1:2] / (HEAD_TOTAL * HD))
    outs = []
    for h in range(OWN):
        attended = att_ref[h]
        outs.append(attended * inverse * gain_ref[h : h + 1, :])
        att_grad = (inverse * up_ref[h] - attended * pull).astype(bf16)
        ag_ref[h] = att_grad
        faded = (heads_ref[0, h].astype(f32) * jnp.exp(as_cols[:, h : h + 1])).astype(bf16)
        back = dot(faded, att_grad, TN).astype(bf16)
        back_ref[h * HD : (h + 1) * HD, :] = back
    join_heads(outs, scratch, out_ref)


def inner_kernel(
    heads_ref, ag_ref, state_ref, later_ref, decay_ref, dq_ref, dk_ref, dv_ref, scratch
):
    as_rows, as_cols, row, col = run_sums(decay_ref[...])
    query_grads, key_grads, value_grads = [], [], []
    for h in range(OWN):
        run_row, run_col = as_rows[h : h + 1, :], as_cols[:, h : h + 1]
        query, key, value, grad = heads_ref[0, h], heads_ref[1, h], heads_ref[2, h], ag_ref[h]
        decays = SCALE_LIN * jnp.exp(jnp.where(row >= col, run_col - run_row, FAR_BELOW))
        turned = SCALE_LIN * jnp.exp(jnp.where(col >= row, run_row - run_col, FAR_BELOW))
        grad_weights = (dot(grad, value, NT) * decays).astype(bf16)
        grad_turned = (dot(value, grad, NT) * turned).astype(bf16)
        weights_turned = (dot(key, query, NT) * turned).astype(bf16)
        state = state_ref[h * HD : (h + 1) * HD, :]
        later = later_ref[h * HD : (h + 1) * HD, :]
        fade = SCALE_LIN * jnp.exp(run_col)
        tail = SCALE_LIN * jnp.exp(run_row[:, LB - 1 : LB] - run_col)
        query_grads.append(dot(grad_weights, key, NN) + fade * dot(grad, state, NT))
        key_grads.append(dot(grad_turned, query, NN) + tail * dot(value, later, NT))
        value_grads.append(dot(weights_turned, grad, NN) + tail * dot(key, later, NN))
    join_heads(query_grads, scratch, dq_ref)
    join_heads(key_grads, scratch, dk_ref)
    join_heads(value_grads, scratch, dv_ref)


def keys_of(ref, g, part):
    return ref[pl.ds(g * PIECES, PIECES), part * HALF : (part + 1) * HALF, :].reshape(KEYS, HD)


def soft_kernel(
    reach_ref, q_ref, do_ref, trade_ref, mine_ref, other_ref, out_ref, dq_ref, back_ref, dmine_ref, dother_ref,
    rows_ref, s_ref, p_ref, top_ref, mass_ref, sum_ref, turned_ref, grad_ref, row_ref,
):
    here = lax.axis_index("ctx")
    side = lax.axis_index("head") % 2
    blocks = (2 * here, 2 * CTX - 1 - 2 * here)
    bases = [block * BLK for block in blocks]
    reaches = [reach_ref[block] * BLK for block in blocks]
    lowest = [jnp.maximum(base + 1, reach) // SPAN for base, reach in zip(bases, reaches)]
    used = [(jnp.maximum(base + BLK, reach) + SPAN - 1) // SPAN for base, reach in zip(bases, reaches)]
    common, most = jnp.minimum(used[0], used[1]), jnp.maximum(used[0], used[1])
    larger = (used[1] > used[0]).astype(jnp.int32)
    whole = pl.ds(0, ROWS)
    part = pl.ds(pl.multiple_of(larger * (ROWS // 2), ROWS // 2), ROWS // 2)
    full_both = jnp.minimum(jnp.minimum(lowest[0], lowest[1]), common)
    full_part = jnp.clip(jnp.where(larger == 1, lowest[1], lowest[0]), common, most)

    rows_ref[0 : ROWS // 2] = q_ref[0 : ROWS // 2]
    rows_ref[ROWS // 2 :] = trade_ref[0 : ROWS // 2]
    lane = lax.broadcasted_iota(jnp.int32, (8, ROWS), 1)
    second = lane >= ROWS // 2
    place = jnp.where(second, lane - ROWS // 2, lane) // OWN
    row_ref[...] = jnp.maximum(
        jnp.where(second, bases[1], bases[0]) + place + 1, jnp.where(second, reaches[1], reaches[0])
    ).astype(f32)
    top_ref[...] = jnp.full((8, ROWS), FAR_BELOW, f32)
    mass_ref[...] = jnp.zeros((8, ROWS), f32)
    sum_ref[...] = jnp.zeros((HD, ROWS), f32)

    def over_keys(step):
        def run(low, high, cols, width, masked):
            @pl.loop(low, high)
            def _(g):
                step(g, g, mine_ref, dmine_ref, side, cols, width, masked)
                step(g, PER_SOURCE + g, other_ref, dother_ref, 1 - side, cols, width, masked)

        return run

    def find_max(g, at, ref, _, half, cols, width, masked):
        scores = dot(keys_of(ref, g, 0), rows_ref[cols, :], NT)
        if masked:
            index = lax.broadcasted_iota(jnp.int32, (KEYS, 1), 0)
            where = g * SPAN + half * HALF + (index // HALF) * LB + index % HALF
            scores = jnp.where(where.astype(f32) < row_ref[0:1, cols], scores, FAR_BELOW)
        s_ref[at, :, cols] = scores
        top_ref[:, cols] = jnp.maximum(top_ref[:, cols], jnp.max(scores.reshape(KEYS // 8, 8, width), axis=0))

    run = over_keys(find_max)
    run(0, full_both, whole, ROWS, False)
    run(full_both, common, whole, ROWS, True)
    run(common, full_part, part, ROWS // 2, False)
    run(full_part, most, part, ROWS // 2, True)
    factor = SCALE_SOFT * LOG2E
    row_ref[...] = jnp.broadcast_to(jnp.max(top_ref[...], axis=0, keepdims=True) * factor, (8, ROWS))

    def weigh(g, at, ref, _, half, cols, width, masked):
        probs = jnp.exp2(s_ref[at, :, cols] * factor - row_ref[0:1, cols])
        mass_ref[:, cols] = mass_ref[:, cols] + jnp.sum(probs.reshape(KEYS // 8, 8, width), axis=0)
        probs = probs.astype(bf16)
        p_ref[at, :, cols] = probs
        sum_ref[:, cols] = sum_ref[:, cols] + dot(keys_of(ref, g, 1), probs, TN)

    run = over_keys(weigh)
    run(0, common, whole, ROWS, False)
    run(common, most, part, ROWS // 2, False)

    inverse = 1.0 / jnp.sum(mass_ref[...], axis=0, keepdims=True)
    out = (sum_ref[...] * inverse).astype(bf16)
    out_rows = out.T
    out_ref[...] = out_rows[0 : ROWS // 2]
    back_ref[0 : ROWS // 2] = out_rows[ROWS // 2 :]
    grads = jnp.concatenate(
        [do_ref[0 : ROWS // 2].astype(f32).T, trade_ref[ROWS // 2 :].astype(f32).T], axis=1
    )
    adjust = inverse * SCALE_SOFT
    row_ref[...] = jnp.broadcast_to(
        jnp.sum(grads * out.astype(f32), axis=0, keepdims=True) * adjust, (8, ROWS)
    )
    turned = (grads * adjust).astype(bf16)
    turned_ref[...] = turned
    grad_ref[...] = turned.T
    sum_ref[...] = jnp.zeros((HD, ROWS), f32)

    def pull(g, at, ref, target, half, cols, width, masked):
        probs = p_ref[at, :, cols]
        moved = dot(keys_of(ref, g, 1), turned_ref[:, cols], NN)
        pulls = (probs.astype(f32) * (moved - row_ref[0:1, cols])).astype(bf16)
        dk = dot(pulls, rows_ref[cols, :], NN)
        dv = dot(probs, grad_ref[cols, :], NN) * (1.0 / SCALE_SOFT)
        target[pl.ds(g * PIECES, PIECES), 0:HALF, :] = dk.astype(bf16).reshape(PIECES, HALF, HD)
        target[pl.ds(g * PIECES, PIECES), HALF:LB, :] = dv.astype(bf16).reshape(PIECES, HALF, HD)
        sum_ref[:, cols] = sum_ref[:, cols] + dot(keys_of(ref, g, 0), pulls, TN)

    run = over_keys(pull)
    run(0, common, whole, ROWS, False)
    run(common, most, part, ROWS // 2, False)
    dq_rows = sum_ref[...].astype(bf16).T
    dq_ref[...] = dq_rows[0 : ROWS // 2]
    back_ref[ROWS // 2 :] = dq_rows[ROWS // 2 :]

    @pl.loop(most, PER_SOURCE)
    def _(g):
        zero = jnp.zeros((PIECES, LB, HD), bf16)
        dmine_ref[pl.ds(g * PIECES, PIECES)] = zero
        dother_ref[pl.ds(g * PIECES, PIECES)] = zero


def merge_kernel(mine_ref, got_ref, back_ref, pay_ref):
    for j in range(CTX):
        pay_ref[j, 0:LB, :] = (mine_ref[j].astype(f32) + got_ref[j].astype(f32)).astype(bf16)
        pay_ref[j, LB:, :] = back_ref[j]


def reduce_kernel(got_ref, first_ref, block_ref, out_ref):
    block = got_ref[0, 0:LB, :].astype(f32)
    for j in range(1, CTX):
        block = block + got_ref[j, 0:LB, :].astype(f32)
    block_ref[...] = block.astype(bf16)
    state = jnp.zeros((SLICE, HD), f32)
    for j in reversed(range(CTX)):
        out_ref[j] = state.astype(bf16)
        marks = first_ref[j, LB + SLICE :, :].astype(f32)
        fade = jnp.exp(marks[0:1, :] + marks[8:9, :])
        state = fade * state + got_ref[j, LB:, :].astype(f32)


def pair_kernel(own_ref, below_ref, above_ref, up_ref, down_ref):
    up_ref[0:LB] = own_ref[...]
    up_ref[LB:] = below_ref[...]
    down_ref[0:LB] = own_ref[...]
    down_ref[LB:] = above_ref[...]


def gather_kernel(own_ref, below_ref, above_ref, far_ref, up_ref, down_ref, out_ref):
    z = lax.axis_index("head") // 2
    for shift, ref, at in (
        (0, own_ref, 0), (-2, below_ref, 0), (2, above_ref, 0), (4, far_ref, 0),
        (-1, up_ref, 0), (-3, up_ref, 1), (1, down_ref, 0), (3, down_ref, 1),
    ):
        out_ref[(z + shift + KVH) % KVH] = ref[at * LB : (at + 1) * LB, :]


def fill_rows(source_ref, scratch):
    filled = []
    for part in range(2):
        for z in range(KVH):
            rows = source_ref[z, part * HALF : (part + 1) * HALF, :]
            scratch[pl.ds(z, HALF, stride=KVH), :] = rows.astype(f32)
        filled.append(scratch[...].astype(bf16))
    return filled


def near_kernel(mine_ref, out_ref, sdq_ref, traded_ref, rows_ref, soft_out_ref, soft_dq_ref, scratch):
    for n, (own, target) in enumerate(((out_ref, soft_out_ref), (sdq_ref, soft_dq_ref))):
        target[0 : ROWS // 2] = own[...]
        target[ROWS // 2 :] = traded_ref[n * (ROWS // 2) : (n + 1) * (ROWS // 2)]
    for part, rows in enumerate(fill_rows(mine_ref, scratch)):
        rows_ref[part] = rows


def spread_kernel(near_ref, other_ref, dk_ref, dv_ref, scratch):
    side = lax.axis_index("head") % 2
    here = pl.ds(pl.multiple_of(side * (HALF * KVH), HALF * KVH), HALF * KVH)
    there = pl.ds(pl.multiple_of((1 - side) * (HALF * KVH), HALF * KVH), HALF * KVH)
    for part, rows in enumerate(fill_rows(other_ref, scratch)):
        target = (dk_ref, dv_ref)[part]
        target[here, :] = near_ref[part]
        target[there, :] = rows


def call(kernel, outs, scratch=(), smem=(), hbm=(), hbm_out=(), count=0, flops=0, limit=8):
    spaces = [
        pl.BlockSpec(memory_space=pltpu.SMEM if n in smem else pl.ANY if n in hbm else pltpu.VMEM)
        for n in range(count)
    ]
    return pl.pallas_call(
        kernel,
        out_shape=[jax.ShapeDtypeStruct(shape, kind) for shape, kind in outs],
        in_specs=spaces,
        out_specs=[
            pl.BlockSpec(memory_space=pl.ANY if n in hbm_out else pltpu.VMEM) for n in range(len(outs))
        ],
        scratch_shapes=[x if not isinstance(x, tuple) else pltpu.VMEM(*x) for x in scratch],
        compiler_params=pltpu.CompilerParams(vmem_limit_bytes=limit * 1024 * 1024),
        cost_estimate=pl.CostEstimate(flops=flops, bytes_accessed=1 << 20, transcendentals=0),
    )


def after(value, *earlier):
    return lax.optimization_barrier((value,) + earlier)[0]


WIDE = ((ROWS, HD), f32)
FLAT = ((ROWS, HD), bf16)
BY_HEAD = ((OWN, LB, HD), f32)
HALF_FLAT = ((ROWS // 2, HD), bf16)
KEY_PARTS = ((CTX, LB, HD), bf16)
MIRROR = [(i, CTX - 1 - i) for i in range(CTX)]
OTHER_CORE = [(i, i ^ 1) for i in range(HEADS)]
ALONG = {k: [(i, (i + 2 * k) % HEADS) for i in range(HEADS)] for k in (-2, -1, 1, 2, 4)}


def per_device(lin_q, lin_k, lin_v, decay, lin_gain, lin_grad, soft_q, soft_k, soft_v, soft_grad, reach):
    flat = lambda x: x.reshape(-1, HD)
    lin_q, lin_k, lin_v, lin_grad, soft_q, soft_grad, soft_k, soft_v = map(
        flat, (lin_q, lin_k, lin_v, lin_grad, soft_q, soft_grad, soft_k, soft_v)
    )
    pay, trade = call(
        local_kernel,
        [((CTX, LB + SLICE + 16, HD), bf16), FLAT],
        [
            WIDE,
            ((2, ROWS, HD), bf16),
            ((2, HALF * KVH, HD), bf16),
            ((OWN, LB), f32),
            ((LB, HD), bf16),
            ((CTX, SLICE + 16, HD), bf16),
            FLAT,
            pltpu.SemaphoreType.DMA((7,)),
            pltpu.SemaphoreType.DMA((CTX + 2,)),
        ],
        hbm=(0, 1, 2, 3, 4, 5, 6),
        hbm_out=(0, 1),
        count=7,
        flops=10**9,
        limit=60,
    )(lin_k, lin_v, decay, soft_k, soft_v, soft_q, soft_grad)
    within, heads = call(
        within_kernel, [BY_HEAD, ((3, OWN, LB, HD), bf16)], [WIDE], count=4, flops=10**9, limit=60
    )(lin_q, lin_k, lin_v, after(decay, pay))
    trade = lax.ppermute(trade, "ctx", MIRROR)
    mine = lax.all_to_all(pay, "ctx", 0, 0)
    (prefixes,) = call(prefix_kernel, [((CTX, SLICE, HD), bf16)], count=1, flops=10**8)(
        after(mine, within)
    )
    state = lax.all_to_all(prefixes, "ctx", 0, 0).reshape(OWN * HD, HD)
    attended, upstream, sums = call(
        attend_kernel,
        [BY_HEAD, BY_HEAD, ((HEADS, 4, HALF), f32)],
        [WIDE],
        count=6,
        flops=10**9,
    )(within, heads, state, decay, lin_grad, lin_gain)
    other = lax.ppermute(after(mine, sums, trade), "head", OTHER_CORE)
    total = lax.all_to_all(after(sums, trade), "head", 0, 0)
    own_out, own_dq, traded, dmine, dother = call(
        soft_kernel,
        [HALF_FLAT, HALF_FLAT, FLAT, KEY_PARTS, KEY_PARTS],
        [
            FLAT,
            ((GROUPS, KEYS, ROWS), f32),
            ((GROUPS, KEYS, ROWS), bf16),
            ((8, ROWS), f32),
            ((8, ROWS), f32),
            ((HD, ROWS), f32),
            ((HD, ROWS), bf16),
            FLAT,
            ((8, ROWS), f32),
        ],
        smem=(0,),
        count=6,
        flops=10**10,
        limit=36,
    )(reach, after(soft_q, total), soft_grad, trade, mine, other)
    dgot = lax.ppermute(dother, "head", OTHER_CORE)
    lin_out, att_grad, back = call(
        grad_kernel,
        [FLAT, ((OWN, LB, HD), bf16), ((OWN * HD, HD), bf16)],
        [WIDE],
        count=6,
        flops=2 * 10**9,
    )(attended, upstream, total, heads, decay, after(lin_gain, own_out))
    (pay_back,) = call(merge_kernel, [((CTX, LB + SLICE, HD), bf16)], count=3, flops=10**8)(
        dmine, dgot, back.reshape(CTX, SLICE, HD)
    )
    got_back = lax.all_to_all(pay_back, "ctx", 0, 0)
    block, suffixes = call(
        reduce_kernel, [((LB, HD), bf16), ((CTX, SLICE, HD), bf16)], count=2, flops=10**8
    )(got_back, mine)
    along = lambda x, k: lax.ppermute(x, "head", ALONG[k])
    below, above, far = along(block, 2), along(block, -2), along(block, 4)
    later = lax.all_to_all(suffixes, "ctx", 0, 0).reshape(OWN * HD, HD)
    up, down = call(pair_kernel, [((2 * LB, HD), bf16)] * 2, count=3, flops=10**8)(block, below, above)
    up, down = along(up, 1), along(down, -1)
    traded = lax.ppermute(after(traded, block), "ctx", MIRROR)
    lin_dq, lin_dk, lin_dv = call(inner_kernel, [FLAT] * 3, [WIDE], count=5, flops=4 * 10**9)(
        heads, att_grad, state, later, decay
    )
    (spread,) = call(gather_kernel, [((KVH, LB, HD), bf16)], count=6, flops=10**8)(
        after(block, lin_dk, traded), below, above, far, up, down
    )
    spread_other = lax.ppermute(spread, "head", OTHER_CORE)
    near, soft_out, soft_dq = call(
        near_kernel,
        [((2, HALF * KVH, HD), bf16), FLAT, FLAT],
        [((HALF * KVH, HD), f32)],
        count=4,
        flops=10**8,
    )(spread, own_out, own_dq, traded)
    soft_dk, soft_dv = call(
        spread_kernel,
        [((LB * KVH, HD), bf16), ((LB * KVH, HD), bf16)],
        [((HALF * KVH, HD), f32)],
        count=2,
        flops=10**8,
    )(near, spread_other)
    deep = lambda x: x.reshape(LB, OWN, HD)
    return (
        deep(lin_out),
        deep(lin_dq),
        deep(lin_dk),
        deep(lin_dv),
        deep(soft_out),
        deep(soft_dq),
        soft_dk.reshape(LB, KVH, HD),
        soft_dv.reshape(LB, KVH, HD),
    )


def solution(mesh):
    long, short = P("ctx", "head", None), P("ctx", None, None)
    return jax.shard_map(
        per_device,
        mesh=mesh,
        in_specs=(long, long, long, P("head", "ctx"), P("head", None), long, long, short, short, long, P()),
        out_specs=(long, long, long, long, long, long, short, short),
        check_vma=False,
    )
```
